32 devices in a mesh: wide: 8 (over z, x), narrow: 4 (over y, core).
Axes of the slice: x: 2, y: 2, z: 4, core: 2. Of those that a mesh axis runs over, the one named last changes fastest.
Arguments:
- views: bfloat16 [128, 7, 7, 2048], P('wide', None, None, 'narrow'), may hold values from -6 to 6
- crops: bfloat16 [256, 3, 3, 2048], P('wide', None, None, 'narrow'), may hold values from -6 to 6
- image_count: int32 [8], P('wide'), may hold values from 2 to 8, as said below
- w_reduce: bfloat16 [2048, 512], P(None, 'narrow'), may hold values from -0.125 to 0.125
- w_spatial: bfloat16 [3, 3, 512, 512], P(None, None, 'narrow'), may hold values from -0.09375 to 0.09375
- w_expand: bfloat16 [512, 2048], P('narrow'), may hold values from -0.25 to 0.25
- gain_one: float32 [512], P('narrow'), may hold values from 0.5 to 1.5
- shift_one: float32 [512], P('narrow'), may hold values from -3 to 3
- gain_two: float32 [512], P('narrow'), may hold values from 0.5 to 1.5
- shift_two: float32 [512], P('narrow'), may hold values from -3 to 3
- gain_three: float32 [2048], P('narrow'), may hold values from 0.5 to 1.5
- shift_three: float32 [2048], P('narrow'), may hold values from -3 to 3
- view_cotangent: bfloat16 [128, 7, 7, 2048], P('wide', None, None, 'narrow'), may hold values from -6 to 6
- crop_cotangent: bfloat16 [256, 3, 3, 2048], P('wide', None, None, 'narrow'), may hold values from -6 to 6
Outputs:
- view_result: bfloat16 [128, 7, 7, 2048], P('wide', None, None, 'narrow')
- crop_result: bfloat16 [256, 3, 3, 2048], P('wide', None, None, 'narrow')
- view_gradient: bfloat16 [128, 7, 7, 2048], P('wide', None, None, 'narrow')
- crop_gradient: bfloat16 [256, 3, 3, 2048], P('wide', None, None, 'narrow')
- reduce_gradient: float32 [2048, 512], P(None, 'narrow')
- spatial_gradient: float32 [3, 3, 512, 512], P(None, None, 'narrow')
- expand_gradient: float32 [512, 2048], P('narrow')
- gain_one_grad: float32 [512], P('narrow')
- shift_one_grad: float32 [512], P('narrow')
- gain_two_grad: float32 [512], P('narrow')
- shift_two_grad: float32 [512], P('narrow')
- gain_three_grad: float32 [2048], P('narrow')
- shift_three_grad: float32 [2048], P('narrow')
The draws below stay inside these ranges and needn't reach their ends.
Inputs may be any that keep to these rules, and one draw needn't show every extreme that they name: image_count[d] real images among the 8 slots of wide index d, the later slots being padding; in every draw some index has all 8.
All inputs are finite; a program needn't handle non-finite values.
Results may differ from the reference program's by a relative error of at most 0.013.
Values may be sent and summed in bfloat16 or wider, within the bound.
A program may use at most 128 MiB of HBM per device.

```python
import jax
import jax.numpy as jnp
from jax import lax

C = 2048
M = 512
IMG_DEV = 8
VIEW_SIDE = 7
CROP_SIDE = 3
VIEWS = 128
CROPS = 256
N_WIDE = 8


def draw_image_count(key, part):
    key = jax.random.fold_in(key, 11)
    first_key, second_key = jax.random.split(key)
    counts = jax.random.randint(first_key, (N_WIDE,), max(1, IMG_DEV // 3), IMG_DEV + 1)
    filled = jax.random.randint(second_key, (), 0, N_WIDE)
    return jnp.where(jnp.arange(N_WIDE) == filled, IMG_DEV, counts).astype(jnp.int32)


def level_of(stream_key, shape, cuts, least, top_value):
    factor_of, own = 1.0, jax.random.fold_in(stream_key, 6)
    for axis_at, blocks in cuts:
        heights = jnp.exp(jax.random.uniform(jax.random.fold_in(own, axis_at), (blocks,), jnp.float32, least / len(cuts), top_value / len(cuts)))
        factor_of = factor_of * jnp.repeat(heights, shape[axis_at] // blocks).reshape([-1 if axis == axis_at else 1 for axis in range(len(shape))])
    return factor_of


def scatter_about(rng, dims, width, bound, shards=(), kind=jnp.bfloat16):
    drawn = width * jax.random.normal(rng, dims, jnp.float32)
    if shards:
        drawn = drawn * level_of(rng, dims, shards, -0.22, 0.18)
    return jnp.clip(drawn, -bound, bound).astype(kind)


def setup_inputs(seed: int = 0) -> dict:
    keys = jax.random.split(jax.random.key(seed), 15)
    views = scatter_about(keys[0], (VIEWS, VIEW_SIDE, VIEW_SIDE, C), 1.0, 6.0, ((0, 8), (3, 4)))
    crops = scatter_about(keys[1], (CROPS, CROP_SIDE, CROP_SIDE, C), 1.0, 6.0, ((0, 8), (3, 4)))
    image_count = draw_image_count(jax.random.fold_in(keys[14], 71), 0)
    w_reduce = scatter_about(keys[3], (C, M), C ** -0.5, 0.125, ((1, 4),))
    w_spatial = scatter_about(keys[4], (3, 3, M, M), (9 * M) ** -0.5, 0.09375, ((2, 4),))
    w_expand = scatter_about(keys[5], (M, C), M ** -0.5, 0.25, ((0, 4),))
    gain_one = jnp.clip(0.5 + 1.0 * jax.random.uniform(keys[6], (M,), jnp.float32) ** level_of(keys[6], (M,), ((0, 4),), -0.2, 0.2), 0.5, 1.5)
    shift_one = scatter_about(keys[7], (M,), 0.5, 3.0, ((0, 4),), jnp.float32)
    gain_two = jnp.clip(0.5 + 1.0 * jax.random.uniform(keys[8], (M,), jnp.float32) ** level_of(keys[8], (M,), ((0, 4),), -0.2, 0.2), 0.5, 1.5)
    shift_two = scatter_about(keys[9], (M,), 0.5, 3.0, ((0, 4),), jnp.float32)
    gain_three = jnp.clip(0.5 + 1.0 * jax.random.uniform(keys[10], (C,), jnp.float32) ** level_of(keys[10], (C,), ((0, 4),), -0.2, 0.2), 0.5, 1.5)
    shift_three = scatter_about(keys[11], (C,), 0.5, 3.0, ((0, 4),), jnp.float32)
    view_cotangent = scatter_about(keys[12], (VIEWS, VIEW_SIDE, VIEW_SIDE, C), 1.0, 6.0, ((0, 8), (3, 4)))
    crop_cotangent = scatter_about(keys[13], (CROPS, CROP_SIDE, CROP_SIDE, C), 1.0, 6.0, ((0, 8), (3, 4)))
    return {"views": views, "crops": crops, "image_count": image_count, "w_reduce": w_reduce, "w_spatial": w_spatial, "w_expand": w_expand, "gain_one": gain_one, "shift_one": shift_one, "gain_two": gain_two, "shift_two": shift_two, "gain_three": gain_three, "shift_three": shift_three, "view_cotangent": view_cotangent, "crop_cotangent": crop_cotangent}


@jax.custom_vjp
def low(v):
    return lax.optimization_barrier(v.astype(jnp.bfloat16)).astype(jnp.float32)

@jax.custom_vjp
def low_back(v):
    return v

def low_keep(v):
    return (low(v), None)

def low_pass(kept, grad):
    return (grad,)

def back_keep(v):
    return (v, None)

def back_low(kept, grad):
    return (low(grad),)
low.defvjp(low_keep, low_pass)
low_back.defvjp(back_keep, back_low)
epsilon = 1e-05

def row_mask(image_count, per_image, number):
    image = jnp.arange(number, dtype=jnp.int32) // per_image
    owner = image // IMG_DEV
    within = image % IMG_DEV
    return (within < image_count[owner]).astype(jnp.float32)[:, None, None, None]

def pointwise(values, weight):
    return jnp.einsum('nhwc,cd->nhwd', values, weight, precision=lax.Precision.HIGHEST)

def spatial(values, weight):
    return lax.conv_general_dilated(values, weight, (1, 1), 'SAME', dimension_numbers=('NHWC', 'HWIO', 'NHWC'), precision=lax.Precision.HIGHEST)

def batch_norm(groups, row_masks, pixel_count, gain, shift):
    center = (lax.optimization_barrier(jnp.sum(groups[0] * row_masks[0], axis=(0, 1, 2))) + lax.optimization_barrier(jnp.sum(groups[1] * row_masks[1], axis=(0, 1, 2)))) / pixel_count
    spread = (lax.optimization_barrier(jnp.sum(jnp.square(groups[0] - center) * row_masks[0], axis=(0, 1, 2))) + lax.optimization_barrier(jnp.sum(jnp.square(groups[1] - center) * row_masks[1], axis=(0, 1, 2)))) / pixel_count
    scaling = gain * lax.rsqrt(spread + epsilon)
    return tuple(((values - center) * scaling + shift for values in groups))

def forward(views, crops, w_reduce, w_spatial, w_expand, gain_one, shift_one, gain_two, shift_two, gain_three, shift_three, row_masks, pixel_count):
    inputs = (views, crops)
    reduced = tuple((low_back(pointwise(values, w_reduce)) for values in inputs))
    hidden_one = tuple((low(jax.nn.silu(values)) for values in batch_norm(reduced, row_masks, pixel_count, gain_one, shift_one)))
    mixed = tuple((low_back(spatial(values, w_spatial)) for values in hidden_one))
    hidden_two = tuple((low(jax.nn.silu(values)) for values in batch_norm(mixed, row_masks, pixel_count, gain_two, shift_two)))
    expanded = tuple((low_back(pointwise(values, w_expand)) for values in hidden_two))
    normed = batch_norm(expanded, row_masks, pixel_count, gain_three, shift_three)
    return tuple((masked * jax.nn.silu(values + source) for values, source, masked in zip(normed, inputs, row_masks)))

def reference(views, crops, image_count, w_reduce, w_spatial, w_expand, gain_one, shift_one, gain_two, shift_two, gain_three, shift_three, view_cotangent, crop_cotangent):
    row_masks = (row_mask(image_count, 2, views.shape[0]), row_mask(image_count, 4, crops.shape[0]))
    pixel_count = jnp.sum(image_count).astype(jnp.float32) * (2 * VIEW_SIDE * VIEW_SIDE + 4 * CROP_SIDE * CROP_SIDE)
    params = (views.astype(jnp.float32), crops.astype(jnp.float32), w_reduce.astype(jnp.float32), w_spatial.astype(jnp.float32), w_expand.astype(jnp.float32), gain_one, shift_one, gain_two, shift_two, gain_three, shift_three)
    results, pullback = jax.vjp(lambda *items: forward(*items, row_masks, pixel_count), *params)
    grads = pullback((view_cotangent.astype(jnp.float32), crop_cotangent.astype(jnp.float32)))
    return (results[0].astype(jnp.bfloat16), results[1].astype(jnp.bfloat16), grads[0].astype(jnp.bfloat16), grads[1].astype(jnp.bfloat16), grads[2], grads[3], grads[4], grads[5], grads[6], grads[7], grads[8], grads[9], grads[10])
```

```python
import functools

import jax
import jax.numpy as jnp
from jax import lax
from jax.experimental import pallas as pl
from jax.experimental.pallas import tpu as pltpu
from jax.sharding import PartitionSpec as P

MESH = pl.DeviceIdType.MESH
EPS = 1e-05
NARROW = 4
CHUNKS = 4
ROW_TILE = 16
VIEWS_EACH = 2
CROPS_EACH = 4
TAPS = [(i, j) for i in range(3) for j in range(3)]
XOR = (0, 2, 1, 3)
POS = (0, 2, 1, 3)
F32 = jnp.float32
BF16 = jnp.bfloat16


def dot(a, b):
    return jnp.dot(a, b, preferred_element_type=F32)


def dot_right(a, b):
    return lax.dot_general(a, b, (((1,), (1,)), ((), ())), preferred_element_type=F32)


def dot_left(a, b):
    return lax.dot_general(a, b, (((0,), (0,)), ((), ())), preferred_element_type=F32)


def logistic(v):
    return 0.5 + 0.5 * jnp.tanh(0.5 * v)


def flip(index, bit):
    return index + bit - 2 * bit * ((index // bit) % 2)


def wider(tile, lanes):
    return jnp.concatenate([tile] * (lanes // 128), axis=1) if lanes > 128 else tile


def fold(v):
    return jnp.sum(v.reshape(v.shape[0] // 8, 8, v.shape[1]), axis=0)


def total(v):
    return jnp.sum(v, axis=0, keepdims=True)


def flat(v):
    return jnp.concatenate([v[k : k + 1] for k in range(v.shape[0])], axis=1)


class Links:
    def __init__(self, send_sems, recv_sems):
        self.send_sems, self.recv_sems, self.used, self.sent = send_sems, recv_sems, 0, []

    def send(self, source, target, peer):
        copy = pltpu.make_async_remote_copy(
            source,
            target,
            self.send_sems.at[self.used],
            self.recv_sems.at[self.used],
            device_id=peer,
            device_id_type=MESH,
        )
        self.used += 1
        copy.start()
        self.sent.append(copy)
        return copy


def kernel(wide, dims, *refs):
    views_side, views_block, crops_side, crops_block, rows, padded = dims
    (
        count_ref, views, crops, view_cot, crop_cot, w_reduce, w_spatial, w_expand,
        gain1, shift1, gain2, shift2, gain3, shift3,
        view_out, crop_out, view_grad, crop_grad, reduce_out, spatial_out, expand_out, small, large,
        x, cot, wr, ws, we, mask, stat, keep, near_out, near_in, far_out, far_in,
        red, mix, back, view_pad, crop_pad, taps, ht, ex, b3, ge, gm, tp, gr, res, dx,
        acc_e, acc_s, acc_r, out_e, out_s, out_r, stage_e, stage_r,
        e_send, e_recv, s_send, s_recv, r_send, r_recv,
        send_sems, recv_sems, stat_send, stat_recv, local_sems,
    ) = refs
    w = lax.axis_index("wide")
    q = lax.axis_index("narrow")
    near, far = (w, flip(q, 1)), (w, flip(q, 2))
    inner = w_reduce.shape[1]
    own = x.shape[1]
    chunk = padded // CHUNKS
    half = 2 * inner
    nview = views.shape[0]
    links = Links(send_sems, recv_sems)
    slot = [0]

    def local(source, target):
        copy = pltpu.make_async_copy(source, target, local_sems.at[slot[0]])
        slot[0] += 1
        copy.start()
        return copy

    def part(r):
        return pl.ds(r * chunk, chunk)

    def lanes(p, width=inner):
        return pl.ds(p * width, width)

    def dyn_lanes(p, width=inner):
        return pl.ds(pl.multiple_of(p * width, width), width)

    def narrow_peer(p):
        i = q
        if XOR[p] & 1:
            i = flip(i, 1)
        if XOR[p] & 2:
            i = flip(i, 2)
        return i

    def loop(body, init, step):
        return lax.fori_loop(
            0, padded // step, lambda i, c: body(pl.ds(pl.multiple_of(i * step, step), step), c), init
        )

    own_reduce = local(
        w_reduce.at[pl.ds(pl.multiple_of(q * own, own), own), :], wr.at[:, lanes(0)]
    )
    load_x = [local(views, x.at[pl.ds(0, nview)]), local(crops, x.at[pl.ds(nview, rows - nview)])]
    load_spatial = [
        local(w_spatial.at[:, dyn_lanes(narrow_peer(p))], ws.at[:, lanes(p)]) for p in range(NARROW)
    ]
    own_expand = local(w_expand.at[:, dyn_lanes(q, own)], we.at[lanes(0), :])
    load_cot = [
        local(view_cot, cot.at[pl.ds(0, nview)]), local(crop_cot, cot.at[pl.ds(nview, rows - nview)])
    ]
    barrier = pltpu.get_barrier_semaphore()
    for p in range(1, NARROW):
        pl.semaphore_signal(barrier, inc=1, device_id=(w, narrow_peer(p)), device_id_type=MESH)

    def greet(k, c):
        pl.semaphore_signal(barrier, inc=1, device_id=(lax.rem(w + k, wide), q), device_id_type=MESH)
        return c

    lax.fori_loop(1, wide, greet, 0)
    pl.semaphore_wait(barrier, NARROW - 1 + wide - 1)

    sent_reduce = {
        p: links.send(
            w_reduce.at[pl.ds(pl.multiple_of(narrow_peer(p) * own, own), own), :],
            wr.at[:, lanes(p)],
            (w, narrow_peer(p)),
        )
        for p in (3, 1, 2)
    }
    sent_expand = {
        p: links.send(
            w_expand.at[:, dyn_lanes(narrow_peer(p), own)], we.at[lanes(p), :], (w, narrow_peer(p))
        )
        for p in (3, 1, 2)
    }

    real = count_ref[0]
    row = lax.broadcasted_iota(jnp.int32, (chunk, 128), 0)
    for r in range(CHUNKS):
        at = row + r * chunk
        image = jnp.where(
            at < nview,
            (at % views_block) // VIEWS_EACH,
            ((at - nview) % crops_block) // CROPS_EACH,
        )
        alive = jnp.where((image < real) & (at < rows), 1.0, 0.0)
        mask[part(r)] = alive.astype(F32)
    tail = pl.ds(rows, padded - rows)
    x[tail] = jnp.zeros((padded - rows, own), BF16)
    cot[tail] = jnp.zeros((padded - rows, own), BF16)
    taps[tail] = jnp.zeros((padded - rows, len(TAPS) * inner), BF16)
    view_pad[...] = jnp.zeros(view_pad.shape, BF16)
    crop_pad[...] = jnp.zeros(crop_pad.shape, BF16)
    my_count = real.astype(F32) * float(
        VIEWS_EACH * views_side**2 + CROPS_EACH * crops_side**2
    )

    def exchange(k, tile):
        stat[k, w] = tile

        def put(step, c):
            pltpu.make_async_remote_copy(
                stat.at[k, w],
                stat.at[k, w],
                stat_send.at[k],
                stat_recv.at[k],
                device_id=(lax.rem(w + step, wide), q),
                device_id_type=MESH,
            ).start()
            return c

        lax.fori_loop(1, wide, put, 0, unroll=wide <= 16)

    def exchanged(k):
        several = stat.at[k, pl.ds(0, wide - 1)]
        pltpu.make_async_copy(several, several, stat_recv.at[k]).wait()

    def exchange_end(k):
        several = stat.at[k, pl.ds(0, wide - 1)]
        pltpu.make_async_copy(several, several, stat_send.at[k]).wait()

    def moments(ref, step):
        size = ref.shape[1]
        zero = jnp.zeros((8, size), F32)
        sums = total(loop(lambda at, c: c + fold(ref[at] * wider(mask[at], size)), zero, step))
        center = sums / my_count
        squares = total(
            loop(
                lambda at, c: c + fold(jnp.square(ref[at] - center) * wider(mask[at], size)), zero, step
            )
        )
        return sums, squares

    def rows_of(k, lo, n):
        return stat[k, :, pl.ds(lo, n), :]

    def combine(sums, squares, counts, pixels):
        center = jnp.sum(sums, axis=0) / pixels
        spread = (
            jnp.sum(squares + counts * jnp.square(sums / counts - center[None]), axis=0) / pixels
        )
        return center, lax.rsqrt(spread + EPS)

    def reduce_scatter(k, give, hold, target, meanwhile=lambda: None):
        first, second = [], []
        for r in range(CHUNKS):
            near_out[k, part(r)] = give(r).astype(BF16)
            first.append(links.send(near_out.at[k, part(r)], near_in.at[k, part(r)], near))
        for r in range(CHUNKS):
            keep[part(r)] = hold(r)
            first[r].wait_recv()
            far_out[k, part(r)] = (
                keep[part(r), lanes(1)] + near_in[k, part(r), lanes(1)].astype(F32)
            ).astype(BF16)
            second.append(links.send(far_out.at[k, part(r)], far_in.at[k, part(r)], far))
            target[part(r)] = keep[part(r), lanes(0)] + near_in[k, part(r), lanes(0)].astype(F32)
        meanwhile()
        for r in range(CHUNKS):
            second[r].wait_recv()
            target[part(r)] = target[part(r)] + far_in[k, part(r)].astype(F32)

    def gather(ref, use, meanwhile=lambda: None):
        straight, across, onward = [], [], []
        for r in range(CHUNKS):
            across.append(links.send(ref.at[part(r), lanes(0)], ref.at[part(r), lanes(1)], far))
            straight.append(links.send(ref.at[part(r), lanes(0)], ref.at[part(r), lanes(2)], near))
        meanwhile()
        for r in range(CHUNKS):
            across[r].wait_recv()
            onward.append(links.send(ref.at[part(r), lanes(1)], ref.at[part(r), lanes(3)], near))
        for r in range(CHUNKS):
            straight[r].wait_recv()
            onward[r].wait_recv()
            use(r)

    def all_reduce(acc, out, sends, recvs, spread_out):
        low, size, halved, used = 0, acc.shape[1], [], 0
        bit = 1
        while bit < wide:
            mine = (w // bit) % 2
            peer = (flip(w, bit), q)
            if (size // 2) % ROW_TILE == 0:
                size //= 2
                held = low + mine * size
                given = low + (1 - mine) * size
                halved.append(bit)
            else:
                held = given = low
            held = pl.multiple_of(held, ROW_TILE)
            given = pl.multiple_of(given, ROW_TILE)
            box = pl.ds(used, size)
            used += size
            copy_rows(acc, given, sends, used - size, size)
            copy = links.send(sends.at[:, box], recvs.at[:, box], peer)
            yield
            copy.wait_recv()
            add_rows(acc, held, recvs, used - size, size)
            low = held
            bit *= 2
        yield from spread_out(low, size)
        for bit in reversed(halved):
            mine = (w // bit) % 2
            box = pl.ds(low, size)
            copy = links.send(out.at[:, box], out.at[:, box], (flip(w, bit), q))
            yield
            copy.wait_recv()
            low = pl.multiple_of(low - mine * size, ROW_TILE)
            size *= 2

    def copy_rows(source, low, target, at, size):
        def body(i, c):
            target[:, pl.ds(pl.multiple_of(at + i * 16, 16), 16)] = source[
                :, pl.ds(pl.multiple_of(low + i * 16, 16), 16)
            ].astype(target.dtype)
            return c

        lax.fori_loop(0, size // 16, body, 0)

    def add_rows(target, low, source, at, size):
        def body(i, c):
            box = pl.ds(pl.multiple_of(low + i * 16, 16), 16)
            target[:, box] = target[:, box] + source[
                :, pl.ds(pl.multiple_of(at + i * 16, 16), 16)
            ].astype(F32)
            return c

        lax.fori_loop(0, size // 16, body, 0)

    own_reduce.wait()
    for p in (2, 3, 1):
        sent_reduce[p].wait_recv()
    for copy in load_x:
        copy.wait()
    reduce_scatter(
        0,
        lambda r: dot(x[part(r)], wr[:, pl.ds(half, half)]),
        lambda r: dot(x[part(r)], wr[:, pl.ds(0, half)]),
        red,
    )
    sums, squares = moments(red, 64)
    exchange(
        0,
        jnp.concatenate(
            [sums, squares, jnp.full((1, inner), my_count, F32), jnp.zeros((5, inner), F32)], axis=0
        ),
    )
    exchanged(0)
    counts = rows_of(0, 2, 1)
    pixels = jnp.sum(counts, axis=0)
    center1, inverse1 = combine(rows_of(0, 0, 1), rows_of(0, 1, 1), counts, pixels)

    def normed(v, center, inverse, gain, shift):
        standard = (v - center) * inverse
        return standard, gain * standard + shift

    g1, s1, g2, s2 = gain1[...], shift1[...], gain2[...], shift2[...]
    g3, s3 = gain3[...], shift3[...]
    grids = (
        (views_side, views_block, 0, view_pad),
        (crops_side, crops_block, nview, crop_pad),
    )
    for side, block, base, pad in grids:
        line = side * block
        for h in range(side):
            _, v = normed(red[pl.ds(base + h * line, line)], center1, inverse1, g1, s1)
            pad[pl.ds(((h + 1) * (side + 2) + 1) * block, line)] = (v * logistic(v)).astype(BF16)
    for side, block, base, pad in grids:
        line = side * block
        for t, (i, j) in enumerate(TAPS):
            for h in range(side):
                taps[pl.ds(base + h * line, line), lanes(t)] = pad[
                    pl.ds(((h + i) * (side + 2) + j) * block, line)
                ]
    for copy in load_spatial:
        copy.wait()

    reduce_scatter(
        1,
        lambda r: dot(taps[part(r)], ws[:, pl.ds(half, half)]),
        lambda r: dot(taps[part(r)], ws[:, pl.ds(0, half)]),
        mix,
    )
    sums, squares = moments(mix, 64)
    exchange(1, jnp.concatenate([sums, squares, jnp.zeros((6, inner), F32)], axis=0))
    exchanged(1)
    center2, inverse2 = combine(rows_of(1, 0, 1), rows_of(1, 1, 1), counts, pixels)

    def second(at, c):
        _, v = normed(mix[at], center2, inverse2, g2, s2)
        ht[at, lanes(0)] = (v * logistic(v)).astype(BF16)
        return c

    loop(second, 0, 64)

    def ready():
        own_expand.wait()
        for p in (2, 3, 1):
            sent_expand[p].wait_recv()

    def expand(r):
        ex[part(r)] = dot(ht[part(r)], we[...])

    gather(ht, expand, ready)
    sums, squares = moments(ex, 32)
    tile = jnp.concatenate(
        [sums[:, 128 * k : 128 * k + 128] for k in range(own // 128)]
        + [squares[:, 128 * k : 128 * k + 128] for k in range(own // 128)],
        axis=0,
    )
    exchange(2, tile)
    for copy in load_cot:
        copy.wait()
    exchanged(2)
    groups = own // 128
    center3, inverse3 = combine(
        rows_of(2, 0, groups), rows_of(2, groups, groups), counts, pixels
    )
    center3, inverse3 = flat(center3), flat(inverse3)

    def third(at, c):
        standard, v = normed(ex[at], center3, inverse3, g3, s3)
        v = v + x[at].astype(F32)
        s = logistic(v)
        alive = wider(mask[at], own)
        res[at] = (alive * (v * s)).astype(BF16)
        g = cot[at].astype(F32) * alive * (s * (1.0 + v * (1.0 - s)))
        b3[at] = g
        return c[0] + fold(g), c[1] + fold(g * standard)

    zero = jnp.zeros((8, own), F32)
    shift_sum, gain_sum = loop(third, (zero, zero), 16)
    shift_sum, gain_sum = total(shift_sum), total(gain_sum)
    tile = jnp.concatenate(
        [gain_sum[:, 128 * k : 128 * k + 128] for k in range(groups)]
        + [shift_sum[:, 128 * k : 128 * k + 128] for k in range(groups)],
        axis=0,
    )
    exchange(3, tile)
    results = [
        local(res.at[pl.ds(0, nview)], view_out), local(res.at[pl.ds(nview, rows - nview)], crop_out)
    ]
    exchanged(3)
    both = jnp.sum(stat[3], axis=0)
    large[...] = both

    def back_terms(gain_grad, shift_grad, center, inverse, gain, n):
        scale = gain * inverse
        slope = scale * inverse * (gain_grad / n)
        return scale, scale * (shift_grad / n) - slope * center, slope

    scale3, base3, slope3 = back_terms(
        flat(both[:groups]), flat(both[groups:]), center3, inverse3, g3, wider(pixels, own)
    )

    def third_back(at, c):
        ge[at] = (
            scale3 * b3[at] - wider(mask[at], own) * (base3 + slope3 * ex[at])
        ).astype(BF16)
        return c

    loop(third_back, 0, 16)

    def spread_expand(low, size):
        at = pl.ds(low, size)
        got = []
        for p in range(1, NARROW):
            stage_e[p] = acc_e[p, at].astype(BF16)
            got.append(
                links.send(
                    stage_e.at[p], out_e.at[0, at, dyn_lanes(q, own)], (w, narrow_peer(p))
                )
            )
        out_e[0, at, dyn_lanes(q, own)] = acc_e[0, at].astype(BF16)
        yield
        for copy in got:
            copy.wait_recv()

    def spread_spatial(low, size):
        out_s[0, pl.ds(low, size)] = acc_s[0, pl.ds(low, size)].astype(BF16)
        yield from ()

    def spread_reduce(low, size):
        at = pl.ds(low, size)
        got = []
        for p in range(1, NARROW):
            stage_r[p] = acc_r[0, at, lanes(p)].astype(BF16)
            got.append(links.send(stage_r.at[p], out_r.at[q, at], (w, narrow_peer(p))))
        out_r[q, at] = acc_r[0, at, lanes(0)].astype(BF16)
        yield
        for copy in got:
            copy.wait_recv()

    tasks = {}

    def start(name, task):
        tasks[name] = task
        next(task)

    def advance(name):
        if next(tasks[name], "end") == "end":
            del tasks[name]

    def expand_gradient():
        for p in range(NARROW):
            acc_e[p] = dot_left(ht[:, lanes(p)], ge[...])
        start("e", all_reduce(acc_e, out_e, e_send, e_recv, spread_expand))

    reduce_scatter(
        2,
        lambda r: dot_right(ge[part(r)], we[pl.ds(half, half), :]),
        lambda r: dot_right(ge[part(r)], we[pl.ds(0, half), :]),
        back,
        expand_gradient,
    )

    def slope_of(v):
        s = logistic(v)
        return s * (1.0 + v * (1.0 - s))

    def second_back(at, c):
        standard, v = normed(mix[at], center2, inverse2, g2, s2)
        g = back[at] * slope_of(v)
        back[at] = g
        return c[0] + fold(g), c[1] + fold(g * standard)

    zero = jnp.zeros((8, inner), F32)
    shift_sum, gain_sum = loop(second_back, (zero, zero), 64)
    exchange(
        4, jnp.concatenate([total(gain_sum), total(shift_sum), jnp.zeros((6, inner), F32)], axis=0)
    )
    advance("e")
    exchanged(4)
    both = jnp.sum(stat[4], axis=0)
    small[pl.ds(8, 8)] = both
    scale2, base2, slope2 = back_terms(both[0:1], both[1:2], center2, inverse2, g2, pixels)

    def second_grad(at, c):
        gm[at, lanes(0)] = (scale2 * back[at] - mask[at] * (base2 + slope2 * mix[at])).astype(BF16)
        return c

    loop(second_grad, 0, 64)

    def spatial_back(r):
        tp[part(r)] = dot_right(gm[part(r)], ws[...])

    gather(gm, spatial_back, lambda: advance("e"))
    shift_sum = gain_sum = zero
    for side, block, base, pad in grids:
        line = side * block
        for h in range(side):
            g = None
            for t, (i, j) in enumerate(TAPS):
                source = h - (i - 1)
                if not 0 <= source < side:
                    continue
                begin = base + source * line
                if j == 1:
                    term = tp[pl.ds(begin, line), lanes(t)]
                elif j == 0:
                    term = jnp.concatenate(
                        [tp[pl.ds(begin + block, line - block), lanes(t)], jnp.zeros((block, inner), F32)]
                    )
                else:
                    term = jnp.concatenate(
                        [jnp.zeros((block, inner), F32), tp[pl.ds(begin, line - block), lanes(t)]]
                    )
                g = term if g is None else g + term
            at = pl.ds(base + h * line, line)
            standard, v = normed(red[at], center1, inverse1, g1, s1)
            g = g * slope_of(v)
            back[at] = g
            shift_sum = shift_sum + fold(g)
            gain_sum = gain_sum + fold(g * standard)
    back[tail] = jnp.zeros((padded - rows, inner), F32)
    exchange(
        5, jnp.concatenate([total(gain_sum), total(shift_sum), jnp.zeros((6, inner), F32)], axis=0)
    )
    for t in range(0, len(TAPS), 3):
        acc_s[0, pl.ds(t * inner, 3 * inner)] = dot_left(taps[:, pl.ds(t * inner, 3 * inner)], gm[...])
    advance("e")
    start("s", all_reduce(acc_s, out_s, s_send, s_recv, spread_spatial))
    exchanged(5)
    both = jnp.sum(stat[5], axis=0)
    small[pl.ds(0, 8)] = both
    scale1, base1, slope1 = back_terms(both[0:1], both[1:2], center1, inverse1, g1, pixels)

    def first_grad(at, c):
        gr[at, lanes(0)] = (scale1 * back[at] - mask[at] * (base1 + slope1 * red[at])).astype(BF16)
        return c

    loop(first_grad, 0, 64)

    def meanwhile():
        for name in list(tasks):
            advance(name)

    gather(gr, lambda r: None, meanwhile)
    acc_r[0] = dot_left(x[...], gr[...])
    start("r", all_reduce(acc_r, out_r, r_send, r_recv, spread_reduce))
    for r in range(CHUNKS):
        dx[part(r)] = (dot_right(gr[part(r)], wr[...]) + b3[part(r)]).astype(BF16)
    results += [
        local(dx.at[pl.ds(0, nview)], view_grad), local(dx.at[pl.ds(nview, rows - nview)], crop_grad)
    ]
    while tasks:
        for name in list(tasks):
            advance(name)
    results += [local(out_e.at[0], expand_out), local(out_r, reduce_out)]
    results += [
        local(out_s.at[0, :, lanes(p)], spatial_out.at[:, dyn_lanes(narrow_peer(p))])
        for p in range(NARROW)
    ]
    for copy in links.sent:
        copy.wait_send()
    for k in range(6):
        exchange_end(k)
    for copy in results:
        copy.wait()


def steps_of(size, wide):
    used, bit = 0, 1
    while bit < wide:
        if (size // 2) % ROW_TILE == 0:
            size //= 2
        used += size
        bit *= 2
    return used, size


def rows_first(a):
    return a.transpose(1, 2, 0, 3).reshape(-1, a.shape[3])


def images_first(a, like):
    n, h, w, c = like.shape
    return a.reshape(h, w, n, c).transpose(2, 0, 1, 3)


def per_device(wide, *args):
    (
        views, crops, image_count, w_reduce, w_spatial, w_expand,
        gain_one, shift_one, gain_two, shift_two, gain_three, shift_three, view_cot, crop_cot,
    ) = args
    own = views.shape[3]
    inner = w_reduce.shape[1]
    full = NARROW * inner
    nview = views.shape[0] * views.shape[1] * views.shape[2]
    ncrop = crops.shape[0] * crops.shape[1] * crops.shape[2]
    rows = nview + ncrop
    quantum = CHUNKS * ROW_TILE
    padded = -(-rows // quantum) * quantum
    dims = (views.shape[1], views.shape[0], crops.shape[1], crops.shape[0], rows, padded)
    ntaps = len(TAPS) * inner
    e_rows, e_left = steps_of(inner, wide)
    s_rows, _ = steps_of(ntaps, wide)
    r_rows, r_left = steps_of(own, wide)
    vm = pltpu.VMEM
    hbm = pl.BlockSpec(memory_space=pl.ANY)
    vmem = pl.BlockSpec(memory_space=pltpu.VMEM)
    smem = pl.BlockSpec(memory_space=pltpu.SMEM)
    outs = pl.pallas_call(
        functools.partial(kernel, wide, dims),
        name="block",
        out_shape=(
            jax.ShapeDtypeStruct((nview, own), BF16),
            jax.ShapeDtypeStruct((ncrop, own), BF16),
            jax.ShapeDtypeStruct((nview, own), BF16),
            jax.ShapeDtypeStruct((ncrop, own), BF16),
            jax.ShapeDtypeStruct((NARROW, own, inner), BF16),
            jax.ShapeDtypeStruct((ntaps, full), BF16),
            jax.ShapeDtypeStruct((inner, NARROW * own), BF16),
            jax.ShapeDtypeStruct((16, inner), F32),
            jax.ShapeDtypeStruct((8, 128), F32),
        ),
        in_specs=[smem] + [hbm] * 7 + [vmem] * 6,
        out_specs=[hbm] * 7 + [vmem] * 2,
        scratch_shapes=[
            vm((padded, own), BF16),
            vm((padded, own), BF16),
            vm((own, full), BF16),
            vm((ntaps, full), BF16),
            vm((full, own), BF16),
            vm((padded, 128), F32),
            vm((6, wide, 8, 128), F32),
            vm((padded, 2 * inner), F32),
            vm((3, padded, 2 * inner), BF16),
            vm((3, padded, 2 * inner), BF16),
            vm((3, padded, inner), BF16),
            vm((3, padded, inner), BF16),
            vm((padded, inner), F32),
            vm((padded, inner), F32),
            vm((padded, inner), F32),
            vm(((dims[0] + 2) ** 2 * dims[1], inner), BF16),
            vm(((dims[2] + 2) ** 2 * dims[3], inner), BF16),
            vm((padded, ntaps), BF16),
            vm((padded, full), BF16),
            vm((padded, own), F32),
            vm((padded, own), F32),
            vm((padded, own), BF16),
            vm((padded, full), BF16),
            vm((padded, ntaps), F32),
            vm((padded, full), BF16),
            vm((padded, own), BF16),
            vm((padded, own), BF16),
            vm((NARROW, inner, own), F32),
            vm((1, ntaps, full), F32),
            vm((1, own, full), F32),
            vm((1, inner, NARROW * own), BF16),
            vm((1, ntaps, full), BF16),
            vm((NARROW, own, inner), BF16),
            vm((NARROW, e_left, own), BF16),
            vm((NARROW, r_left, inner), BF16),
            vm((NARROW, e_rows, own), BF16),
            vm((NARROW, e_rows, own), BF16),
            vm((1, s_rows, full), BF16),
            vm((1, s_rows, full), BF16),
            vm((1, r_rows, full), BF16),
            vm((1, r_rows, full), BF16),
            pltpu.SemaphoreType.DMA((128,)),
            pltpu.SemaphoreType.DMA((128,)),
            pltpu.SemaphoreType.DMA((6,)),
            pltpu.SemaphoreType.DMA((6,)),
            pltpu.SemaphoreType.DMA((24,)),
        ],
        compiler_params=pltpu.CompilerParams(
            collective_id=0, has_side_effects=True, vmem_limit_bytes=62 * 2**20
        ),
    )(
        image_count,
        rows_first(views),
        rows_first(crops),
        rows_first(view_cot),
        rows_first(crop_cot),
        w_reduce,
        w_spatial.reshape(ntaps, full),
        w_expand,
        *(a.reshape(1, -1) for a in (gain_one, shift_one, gain_two, shift_two, gain_three, shift_three)),
    )
    view_out, crop_out, view_grad, crop_grad, reduce_g, spatial_g, expand_g, small, large = outs
    return (
        images_first(view_out, views),
        images_first(crop_out, crops),
        images_first(view_grad, views),
        images_first(crop_grad, crops),
        reduce_g.astype(F32).reshape(NARROW * own, inner),
        spatial_g.astype(F32).reshape(w_spatial.shape),
        expand_g.astype(F32),
        small[0],
        small[1],
        small[8],
        small[9],
        large[:4].reshape(-1),
        large[4:].reshape(-1),
    )


def solution(mesh):
    wide = mesh.shape["wide"]
    image = P("wide", None, None, "narrow")
    vector = P("narrow")
    return jax.shard_map(
        functools.partial(per_device, wide),
        mesh=mesh,
        in_specs=(
            image, image, P("wide"), P(None, "narrow"), P(None, None, "narrow", None), P("narrow", None),
            vector, vector, vector, vector, vector, vector, image, image,
        ),
        out_specs=(
            image, image, image, image, P(None, "narrow"), P(None, None, "narrow", None),
            P("narrow", None), vector, vector, vector, vector, vector, vector,
        ),
        check_vma=False,
    )
```

```python
import functools

import jax
import jax.numpy as jnp
from jax import lax
from jax.experimental import pallas as pl
from jax.experimental.pallas import tpu as pltpu
from jax.sharding import PartitionSpec as P

MESH = pl.DeviceIdType.MESH
EPS = 1e-05
ORDER = (
    ("s1", "s0", "e", "s3", "s2", "r0", "r1", "s1"),
    ("s0", "s3", "s2", "r0", "s1", "r1", "s3", "e", "s0", "r0", "s2", "r1", "s1", "s3"),
)
NARROW = 4
CHUNKS = 4
ROW_TILE = 16
GROUP = 8
VIEWS_EACH = 2
CROPS_EACH = 4
TAPS = [(i, j) for i in range(3) for j in range(3)]
XOR = (0, 2, 1, 3)
POS = (0, 2, 1, 3)
F32 = jnp.float32
BF16 = jnp.bfloat16


def dot(a, b):
    return jnp.dot(a, b, preferred_element_type=F32)


def dot_right(a, b):
    return lax.dot_general(a, b, (((1,), (1,)), ((), ())), preferred_element_type=F32)


def dot_left(a, b):
    return lax.dot_general(a, b, (((0,), (0,)), ((), ())), preferred_element_type=F32)


def logistic(v):
    return 0.5 + 0.5 * jnp.tanh(0.5 * v)


def flip(index, bit):
    return index + bit - 2 * bit * ((index // bit) % 2)


def wider(tile, lanes):
    return jnp.concatenate([tile] * (lanes // 128), axis=1) if lanes > 128 else tile


def fold(v):
    return jnp.sum(v.reshape(v.shape[0] // 8, 8, v.shape[1]), axis=0)


def total(v):
    return jnp.sum(v, axis=0, keepdims=True)


def flat(v):
    return jnp.concatenate([v[k : k + 1] for k in range(v.shape[0])], axis=1)


class Done:
    def wait_recv(self):
        pass


class Links:
    def __init__(self, send_sems, recv_sems):
        self.send_sems, self.recv_sems, self.used, self.sent = send_sems, recv_sems, 0, []

    def send(self, source, target, peer, background=""):
        copy = pltpu.make_async_remote_copy(
            source,
            target,
            self.send_sems.at[self.used],
            self.recv_sems.at[self.used],
            device_id=peer,
            device_id_type=MESH,
        )
        self.used += 1
        copy.start()
        self.sent.append(copy)
        return copy


class Group:
    def __init__(self, links, copies, total, kind):
        self.live = True
        send_sem, recv_sem = links.send_sems.at[links.used], links.recv_sems.at[links.used]
        links.used += 1
        for source, target, peer in copies:
            copy = pltpu.make_async_remote_copy(
                source, target, send_sem, recv_sem, device_id=peer, device_id_type=MESH
            )
            copy.start()
        self.arrival = pltpu.make_async_copy(total, total, recv_sem)
        self.departure = pltpu.make_async_copy(total, total, send_sem)
        links.sent.append(self)

    def wait_recv(self):
        if self.live:
            self.arrival.wait()

    def wait_send(self):
        self.departure.wait()


def kernel(wide, dims, *refs):
    views_side, views_block, crops_side, crops_block, rows, padded = dims
    (
        image_count, views, crops, view_cot, crop_cot, w_reduce, w_spatial, w_expand,
        gain1, shift1, gain2, shift2, gain3, shift3,
        view_out, crop_out, view_grad, crop_grad, reduce_out, spatial_out, expand_out, small_out, large_out,
        count_ref, inner_vectors, outer_vectors, small, large,
        x, xs, cot, wr, ws, we, mask, stat, stat_all, keep, near_out, near_in, far_out, far_in,
        red, mix, back, view_pad, crop_pad, taps, mall, ht, b3, ge, gall, gm, tp, gr, res, dx,
        out_e, out_s, out_r, stage_e, part_e, first_e, second_e, third_e,
        part_s, first_s, second_s, third_s, part_r, first_r, second_r, third_r,
        send_sems, recv_sems, stat_send, stat_recv, local_sems,
    ) = refs
    w = lax.axis_index("wide")
    q = lax.axis_index("narrow")
    near, far = (w, flip(q, 1)), (w, flip(q, 2))
    inner = w_reduce.shape[1]
    own = x.shape[1]
    full = NARROW * inner
    chunk = padded // CHUNKS
    half = 2 * inner
    nview = views.shape[0]
    group = min(wide, GROUP)
    ex = tp.at[:, pl.ds(0, own)]
    links = Links(send_sems, recv_sems)
    slot = [0]

    def local(source, target):
        copy = pltpu.make_async_copy(source, target, local_sems.at[slot[0]])
        slot[0] += 1
        copy.start()
        return copy

    def part(r):
        return pl.ds(r * chunk, chunk)

    def lanes(p, width=inner):
        return pl.ds(p * width, width)

    def dyn_lanes(p, width=inner):
        return pl.ds(pl.multiple_of(p * width, width), width)

    def narrow_peer(p):
        i = q
        if XOR[p] & 1:
            i = flip(i, 1)
        if XOR[p] & 2:
            i = flip(i, 2)
        return i

    def loop(body, init):
        return lax.fori_loop(
            0, CHUNKS, lambda i, c: body(pl.ds(pl.multiple_of(i * chunk, chunk), chunk), c), init
        )

    def own_rows(p):
        return pl.ds(pl.multiple_of(narrow_peer(p) * own, own), own)

    load_count = local(image_count, count_ref)
    load_vectors = [local(ref, inner_vectors.at[k]) for k, ref in enumerate((gain1, shift1, gain2, shift2))]
    load_vectors += [local(ref, outer_vectors.at[k]) for k, ref in enumerate((gain3, shift3))]
    load_reduce = [local(w_reduce.at[own_rows(2 * k), :], wr.at[k, :, lanes(0)]) for k in range(2)]
    load_x = [local(views, x.at[pl.ds(0, nview)]), local(crops, x.at[pl.ds(nview, rows - nview)])]
    load_spatial = [
        local(w_spatial.at[:, dyn_lanes(narrow_peer(p))], ws.at[:, lanes(p)]) for p in range(NARROW)
    ]
    own_expand = local(w_expand.at[:, dyn_lanes(q, own)], we.at[lanes(0), :])
    load_cot = [
        local(view_cot, cot.at[pl.ds(0, nview)]), local(crop_cot, cot.at[pl.ds(nview, rows - nview)])
    ]
    barrier = pltpu.get_barrier_semaphore()

    def greet(k, c):
        pl.semaphore_signal(
            barrier,
            inc=1,
            device_id=(lax.rem(w + k % wide, wide), lax.rem(q + k // wide, NARROW)),
            device_id_type=MESH,
        )
        return c

    everyone = NARROW * wide - 1
    lax.fori_loop(1, everyone + 1, greet, 0, unroll=wide <= 16)

    load_count.wait()
    real = count_ref[0]
    row = lax.broadcasted_iota(jnp.int32, (chunk, 128), 0)
    for r in range(CHUNKS):
        at = row + r * chunk
        image = jnp.where(
            at < nview,
            (at % views_block) // VIEWS_EACH,
            ((at - nview) % crops_block) // CROPS_EACH,
        )
        alive = jnp.where((image < real) & (at < rows), 1.0, 0.0)
        mask[part(r)] = alive.astype(F32)
    tail = pl.ds(rows, padded - rows)
    x[tail] = jnp.zeros((padded - rows, own), BF16)
    xs[1, tail] = jnp.zeros((padded - rows, own), BF16)
    cot[tail] = jnp.zeros((padded - rows, own), BF16)
    taps[tail] = jnp.zeros((padded - rows, len(TAPS) * inner), BF16)
    view_pad[...] = jnp.zeros(view_pad.shape, BF16)
    crop_pad[...] = jnp.zeros(crop_pad.shape, BF16)
    my_count = real.astype(F32) * float(
        VIEWS_EACH * views_side**2 + CROPS_EACH * crops_side**2
    )

    pl.semaphore_wait(barrier, everyone)

    far_reduce = [
        links.send(w_reduce.at[own_rows(1 + 2 * k), :], wr.at[k, :, lanes(1)], far) for k in range(2)
    ]
    near_x = [
        links.send(views, xs.at[1, pl.ds(0, nview)], near),
        links.send(crops, xs.at[1, pl.ds(nview, rows - nview)], near),
    ]
    near_reduce = [links.send(w_reduce.at[own_rows(2), :], wr.at[0, :, lanes(2)], near)]

    def exchange(k, tile, everywhere=False):
        board, me, n = (stat_all, q * wide + w, everyone) if everywhere else (stat, w, wide - 1)
        sem = k + 4 if everywhere else k
        board[k, me] = tile

        def put(step, c):
            pltpu.make_async_remote_copy(
                board.at[k, me],
                board.at[k, me],
                stat_send.at[sem],
                stat_recv.at[sem],
                device_id=(lax.rem(w + step % wide, wide), lax.rem(q + step // wide, NARROW)),
                device_id_type=MESH,
            ).start()
            return c

        lax.fori_loop(1, n + 1, put, 0, unroll=wide <= 16)
        several = board.at[k, pl.ds(0, n)]
        pending.append(pltpu.make_async_copy(several, several, stat_send.at[sem]))
        return pltpu.make_async_copy(several, several, stat_recv.at[sem])

    pending = []

    def moments(ref, after_center=lambda center: None):
        size = ref.shape[1]
        zero = jnp.zeros((8, size), F32)
        sums = total(loop(lambda at, c: c + fold(ref[at, :] * wider(mask[at, :], size)), zero))
        center = sums / my_count
        after_center(center)
        squares = total(
            loop(
                lambda at, c: c + fold(jnp.square(ref[at, :] - center) * wider(mask[at, :], size)),
                zero,
            )
        )
        return sums, squares

    def rows_of(k, lo, n):
        return stat[k, :, pl.ds(lo, n), :]

    def combine(sums, squares, counts, pixels):
        center = jnp.sum(sums, axis=0) / pixels
        spread = (
            jnp.sum(squares + counts * jnp.square(sums / counts - center[None]), axis=0) / pixels
        )
        return center, lax.rsqrt(spread + EPS)

    def reduce_scatter(k, give, hold, target, before_hold=lambda: None, meanwhile=lambda: None):
        first, second = [], []
        for copy in in_use.pop(k, ()):
            copy.wait_send()
            links.sent = [other for other in links.sent if other is not copy]
        for r in range(CHUNKS):
            near_out[k, part(r)] = give(r).astype(BF16)
            first.append(links.send(near_out.at[k, part(r)], near_in.at[k, part(r)], near))
        before_hold()
        for r in range(CHUNKS):
            keep[part(r)] = hold(r)
            first[r].wait_recv()
            far_out[k, part(r)] = (
                keep[part(r), lanes(1)] + near_in[k, part(r), lanes(1)].astype(F32)
            ).astype(BF16)
            second.append(links.send(far_out.at[k, part(r)], far_in.at[k, part(r)], far))
            target[part(r)] = keep[part(r), lanes(0)] + near_in[k, part(r), lanes(0)].astype(F32)
        meanwhile()
        for r in range(CHUNKS):
            second[r].wait_recv()
            target[part(r)] = target[part(r)] + far_in[k, part(r)].astype(F32)
        in_use[k] = first + second

    in_use = {}

    def gather_start(ref):
        across = [
            links.send(ref.at[part(r), lanes(0)], ref.at[part(r), lanes(1)], far) for r in range(CHUNKS)
        ]
        straight = links.send(ref.at[:, lanes(0)], ref.at[:, lanes(2)], near)
        return across, straight, []

    def gather_pass(ref, copies, some):
        across, straight, onward = copies
        for r in some:
            across[r].wait_recv()
            onward.append(links.send(ref.at[part(r), lanes(1)], ref.at[part(r), lanes(3)], near))

    def gather_end(ref, copies, use=lambda r: None):
        across, straight, onward = copies
        for r in range(CHUNKS + 1):
            if len(onward) < CHUNKS:
                gather_pass(ref, copies, [len(onward)])
            if r == 1:
                straight.wait_recv()
            if r > 0:
                onward[r - 1].wait_recv()
                use(r - 1)

    pieces, low = [], 0
    for r in range(2 * CHUNKS):
        size = chunk // 2 // ROW_TILE * ROW_TILE
        size = size if r % 2 else chunk - size
        pieces.append(pl.ds(low, size))
        low += size
    across_x, onward_x = [], []

    def share_x(count):
        for _ in range(count):
            at = pieces[len(across_x)]
            across_x.append(links.send(x.at[at], xs.at[0, at], far, "x"))

    def share_end():
        while len(onward_x) < len(across_x):
            at = pieces[len(onward_x)]
            across_x[len(onward_x)].wait_recv()
            onward_x.append(links.send(xs.at[0, at], xs.at[2, at], near, "x"))

    pair = lax.rem(w, 2)
    place = lax.rem(w, group) // 2
    quads = group // 2
    mine = pair * quads + place
    partner = (flip(w, 1), q)

    def quad_peer(k):
        return lax.rem(place + k, quads)

    def reduced(kind, parts, first, second, third, finish):
        copy = links.send(parts.at[pl.ds((1 - pair) * quads, quads)], first, partner, kind)
        yield
        copy.wait_recv()
        for k in range(quads):
            second[k] = (parts[pair * quads + k].astype(F32) + first[k].astype(F32)).astype(BF16)
        copy = Group(
            links,
            [
                (second.at[quad_peer(k)], third.at[place], (w + 2 * (quad_peer(k) - place), q))
                for k in range(1, quads)
            ],
            third.at[pl.ds(0, quads - 1)],
            kind,
        )
        third[place] = second[place]
        yield
        copy.wait_recv()
        value = jnp.sum(third[...].astype(F32), axis=0)
        bit = group
        while bit < wide:
            first[0] = value.astype(BF16)
            copy = links.send(first.at[0], first.at[1], (flip(w, bit), q))
            copy.wait_recv()
            copy.wait_send()
            value = first[0].astype(F32) + first[1].astype(F32)
            bit *= 2
        yield from finish(value)

    def spread(kind, out):
        copy = Group(
            links,
            [
                (out.at[mine], out.at[mine], (w + 2 * (quad_peer(k) - place), q))
                for k in range(1, quads)
            ],
            out.at[pl.ds(0, quads - 1)],
            kind,
        )
        yield
        copy.wait_recv()
        half_blocks = pl.ds(pair * quads, quads)
        copy = links.send(out.at[half_blocks], out.at[half_blocks], partner, kind)
        yield
        copy.wait_recv()

    tasks = {}

    def begin(name, task):
        tasks[name] = task
        next(task)

    def advance(*names):
        for name in names:
            if name in tasks and next(tasks[name], "end") == "end":
                del tasks[name]

    for copy in load_reduce + load_x:
        copy.wait()
    for copy in near_x:
        copy.wait_recv()

    def reduce_part(r, p):
        return dot(x[part(r)], wr[0, :, lanes(p)]) + dot(xs[1, part(r)], wr[1, :, lanes(p)])

    for r in range(CHUNKS):
        red[part(r)] = reduce_part(r, 0)
    for copy in far_reduce:
        copy.wait_recv()
    came = []
    for r in range(CHUNKS):
        far_out[0, part(r)] = reduce_part(r, 1).astype(BF16)
        came.append(links.send(far_out.at[0, part(r)], far_in.at[0, part(r)], far))
    near_reduce.append(links.send(wr.at[1, :, lanes(1)], wr.at[0, :, lanes(3)], near))
    for r in range(CHUNKS):
        came[r].wait_recv()
        red[part(r)] = red[part(r)] + far_in[0, part(r)].astype(F32)
    in_use[0] = came
    sent_expand = {
        p: links.send(
            w_expand.at[:, dyn_lanes(narrow_peer(p), own)], we.at[lanes(p), :], (w, narrow_peer(p))
        )
        for p in (3, 1, 2)
    }
    share_x(2)
    sums, squares = moments(red)
    arrived = exchange(
        0,
        jnp.concatenate(
            [sums, squares, jnp.full((1, inner), my_count, F32), jnp.zeros((5, inner), F32)], axis=0
        ),
    )
    for copy in load_spatial:
        copy.wait()
    arrived.wait()
    counts = rows_of(0, 2, 1)
    pixels = jnp.sum(counts, axis=0)
    center1, inverse1 = combine(rows_of(0, 0, 1), rows_of(0, 1, 1), counts, pixels)

    def normed(v, center, inverse, gain, shift):
        standard = (v - center) * inverse
        return standard, gain * standard + shift

    for copy in load_vectors:
        copy.wait()
    g1, s1, g2, s2 = (inner_vectors[k] for k in range(4))
    g3, s3 = (outer_vectors[k] for k in range(2))
    grids = (
        (views_side, views_block, 0, view_pad),
        (crops_side, crops_block, nview, crop_pad),
    )
    for side, block, lead, pad in grids:
        line = side * block
        for h in range(side):
            _, v = normed(red[pl.ds(lead + h * line, line)], center1, inverse1, g1, s1)
            pad[pl.ds(((h + 1) * (side + 2) + 1) * block, line)] = (v * logistic(v)).astype(BF16)
    for side, block, lead, pad in grids:
        line = side * block
        for t, (i, j) in enumerate(TAPS):
            for h in range(side):
                taps[pl.ds(lead + h * line, line), lanes(t)] = pad[
                    pl.ds(((h + i) * (side + 2) + j) * block, line)
                ]

    reduce_scatter(
        1,
        lambda r: dot(taps[part(r)], ws[:, pl.ds(half, half)]),
        lambda r: dot(taps[part(r)], ws[:, pl.ds(0, half)]),
        mix,
    )

    copies = []

    def centered(center):
        def body(at, c):
            mall[at, lanes(0)] = (mix[at] - center).astype(BF16)
            return c

        loop(body, 0)
        copies.append(gather_start(mall))

    sums, squares = moments(mix, centered)
    arrived = exchange(
        0, jnp.concatenate([sums, squares, g2, s2, jnp.zeros((4, inner), F32)], axis=0), True
    )
    own_expand.wait()
    for p in (2, 3, 1):
        sent_expand[p].wait_recv()
    gather_pass(mall, copies[0], range(2))
    arrived.wait()

    def board_rows(k, p, lo, n):
        return stat_all[k, pl.ds(narrow_peer(p) * wide, wide), pl.ds(lo, n), :]

    def board_row(k, p, lo):
        return stat_all[k, narrow_peer(p) * wide + w, pl.ds(lo, 1), :]

    blocks = [
        combine(board_rows(0, p, 0, 1), board_rows(0, p, 1, 1), counts, pixels) for p in range(NARROW)
    ]
    center2, inverse2 = blocks[0]
    inverse_all = jnp.concatenate([b[1] for b in blocks], axis=1)
    offset_all = jnp.concatenate(
        [board_row(0, p, 0) / my_count - blocks[p][0] for p in range(NARROW)], axis=1
    )
    gain_all = jnp.concatenate([board_row(0, p, 2) for p in range(NARROW)], axis=1)
    shift_all = jnp.concatenate([board_row(0, p, 3) for p in range(NARROW)], axis=1)
    scale_all = gain_all * inverse_all
    constant_all = scale_all * offset_all + shift_all

    def expand(r):
        v = mall[part(r), :].astype(F32) * scale_all + constant_all
        ht[part(r), :] = (v * logistic(v)).astype(BF16)
        ex[part(r), :] = dot(ht[part(r)], we[...])

    gather_end(mall, copies[0], expand)
    share_end()
    share_x(4)
    sums, squares = moments(ex)
    groups = own // 128

    def tiles(*values):
        return jnp.concatenate(
            [v[:, 128 * k : 128 * k + 128] for v in values for k in range(groups)], axis=0
        )

    arrived = exchange(1, tiles(sums, squares))
    for copy in load_cot:
        copy.wait()
    arrived.wait()
    center3, inverse3 = combine(
        rows_of(1, 0, groups), rows_of(1, groups, groups), counts, pixels
    )
    center3, inverse3 = flat(center3), flat(inverse3)

    def third(at, c):
        standard, v = normed(ex[at, :], center3, inverse3, g3, s3)
        v = v + x[at].astype(F32)
        s = logistic(v)
        alive = wider(mask[at], own)
        res[at] = (alive * (v * s)).astype(BF16)
        g = cot[at].astype(F32) * alive * (s * (1.0 + v * (1.0 - s)))
        b3[at] = g
        return c[0] + fold(g), c[1] + fold(g * standard)

    zero = jnp.zeros((8, own), F32)
    shift_sum, gain_sum = loop(third, (zero, zero))
    arrived = exchange(2, tiles(total(gain_sum), total(shift_sum)))
    results = [
        local(res.at[pl.ds(0, nview)], view_out), local(res.at[pl.ds(nview, rows - nview)], crop_out)
    ]
    arrived.wait()
    both = jnp.sum(stat[2], axis=0)
    large[...] = both
    results.append(local(large, large_out))

    def back_terms(gain_grad, shift_grad, offset, inverse, gain, n):
        scale = gain * inverse
        slope = scale * inverse * (gain_grad / n)
        return scale, scale * (shift_grad / n) + slope * offset, slope

    scale3, base3, slope3 = back_terms(
        flat(both[:groups]), flat(both[groups:]), -center3, inverse3, g3, wider(pixels, own)
    )

    def third_back(at, c):
        ge[at] = (
            scale3 * b3[at] - wider(mask[at], own) * (base3 + slope3 * ex[at, :])
        ).astype(BF16)
        return c

    loop(third_back, 0)

    size_e = inner // group

    def finish_e(value):
        stage_e[...] = value.astype(BF16)
        got = [
            links.send(
                stage_e.at[p], out_e.at[mine, :, dyn_lanes(q, own)], (w, narrow_peer(p)), "e"
            )
            for p in range(1, NARROW)
        ]
        out_e[mine, :, dyn_lanes(q, own)] = stage_e[0]
        yield
        for copy in got:
            copy.wait_recv()
        yield from spread("e", out_e)

    def expand_gradient():
        value = dot_left(ht[...], ge[...]).astype(BF16)
        for p in range(NARROW):
            part_e[:, p] = value[inner * p : inner * (p + 1)].reshape(group, size_e, own)
        begin("e", reduced("e", part_e, first_e, second_e, third_e, finish_e))
        share_end()

    reduce_scatter(
        0,
        lambda r: dot_right(ge[part(r)], we[pl.ds(half, half), :]),
        lambda r: dot_right(ge[part(r)], we[pl.ds(0, half), :]),
        back,
        meanwhile=expand_gradient,
    )

    def slope_of(v):
        s = logistic(v)
        return s * (1.0 + v * (1.0 - s))

    def second_back(at, c):
        standard, v = normed(mix[at], center2, inverse2, g2, s2)
        g = back[at] * slope_of(v)
        gall[at, lanes(0)] = g.astype(BF16)
        return c[0] + fold(g), c[1] + fold(g * standard)

    zero = jnp.zeros((8, inner), F32)
    shift_sum, gain_sum = loop(second_back, (zero, zero))
    copies = gather_start(gall)
    arrived = exchange(
        1,
        jnp.concatenate([total(gain_sum), total(shift_sum), jnp.zeros((6, inner), F32)], axis=0),
        True,
    )
    advance("e")
    gather_pass(gall, copies, range(2))
    arrived.wait()
    sums = [jnp.sum(board_rows(1, p, 0, 2), axis=0) for p in range(NARROW)]
    small[pl.ds(8, 8)] = jnp.concatenate([sums[0], jnp.zeros((6, inner), F32)], axis=0)
    scale2, base2, slope2 = back_terms(
        jnp.concatenate([v[0:1] for v in sums], axis=1),
        jnp.concatenate([v[1:2] for v in sums], axis=1),
        offset_all,
        inverse_all,
        gain_all,
        wider(pixels, full),
    )

    def columns(v, p, n=1):
        return v[:, inner * p : inner * (p + n)]

    def grad_mixed(at, some):
        for p in some:
            gm[at, lanes(p)] = (
                columns(scale2, p) * gall[at, lanes(p)].astype(F32)
                - mask[at] * (columns(base2, p) + columns(slope2, p) * mall[at, lanes(p)].astype(F32))
            ).astype(BF16)
        return 0

    def spatial_gradient(*some):
        value = dot_left(taps[...], jnp.concatenate([gm[:, lanes(p)] for p in some], axis=1))
        for k, p in enumerate(some):
            part_s[p] = columns(value, k).astype(BF16).reshape(part_s.shape[1:])

            def finish(value, p=p):
                out_s[p, mine] = value.astype(BF16)
                yield from spread("s", out_s.at[p])

            begin(
                "s%d" % p,
                reduced("s", part_s.at[p], first_s.at[p], second_s.at[p], third_s.at[p], finish),
            )

    copies[1].wait_recv()
    loop(lambda at, c: grad_mixed(at, (0, 2)), 0)
    spatial_gradient(0, 2)
    advance("e")

    def spatial_back(r):
        grad_mixed(part(r), (1, 3))
        tp[part(r)] = dot_right(gm[part(r)], ws[...])

    gather_end(gall, (copies[0], Done(), copies[2]), spatial_back)
    share_x(2)
    shift_sum = gain_sum = zero
    for side, block, lead, pad in grids:
        line = side * block
        for h in range(side):
            g = None
            for t, (i, j) in enumerate(TAPS):
                source = h - (i - 1)
                if not 0 <= source < side:
                    continue
                first = lead + source * line
                if j == 1:
                    term = tp[pl.ds(first, line), lanes(t)]
                elif j == 0:
                    term = jnp.concatenate(
                        [tp[pl.ds(first + block, line - block), lanes(t)], jnp.zeros((block, inner), F32)]
                    )
                else:
                    term = jnp.concatenate(
                        [jnp.zeros((block, inner), F32), tp[pl.ds(first, line - block), lanes(t)]]
                    )
                g = term if g is None else g + term
            at = pl.ds(lead + h * line, line)
            standard, v = normed(red[at], center1, inverse1, g1, s1)
            g = g * slope_of(v)
            back[at] = g
            shift_sum = shift_sum + fold(g)
            gain_sum = gain_sum + fold(g * standard)
    back[tail] = jnp.zeros((padded - rows, inner), F32)
    arrived = exchange(
        3, jnp.concatenate([total(gain_sum), total(shift_sum), jnp.zeros((6, inner), F32)], axis=0)
    )

    spatial_gradient(1, 3)
    advance("e", "s0", "s2")
    share_end()
    arrived.wait()
    both = jnp.sum(stat[3], axis=0)
    small[pl.ds(0, 8)] = both
    results.append(local(small, small_out))
    scale1, base1, slope1 = back_terms(both[0:1], both[1:2], -center1, inverse1, g1, pixels)

    def first_grad(at, c):
        gr[at, lanes(0)] = (scale1 * back[at] - mask[at] * (base1 + slope1 * red[at])).astype(BF16)
        return c

    loop(first_grad, 0)
    copies = gather_start(gr)

    for copy in onward_x:
        copy.wait_recv()
    per = own // 4
    for p in range(NARROW):
        source = x[...] if p == 0 else xs[p - 1]
        value = dot_left(gr[:, lanes(0)], source).astype(BF16)
        for k in range(4):
            part_r[k % 2, narrow_peer(p) * 2 + k // 2] = value[:, per * k : per * k + per]
    for k in range(2):

        def finish(value, k=k):
            out_r[k, mine] = value.T.astype(BF16)
            yield from spread("r", out_r.at[k])

        begin(
            "r%d" % k,
            reduced("r", part_r.at[k], first_r.at[k], second_r.at[k], third_r.at[k], finish),
        )
    advance(*ORDER[0])

    def input_gradient(r):
        dx[part(r)] = (dot_right(gr[part(r)], wr[0]) + b3[part(r)]).astype(BF16)

    for copy in near_reduce:
        copy.wait_recv()
    gather_end(gr, copies, input_gradient)
    results += [
        local(dx.at[pl.ds(0, nview)], view_grad), local(dx.at[pl.ds(nview, rows - nview)], crop_grad)
    ]
    advance(*ORDER[1])
    results.append(local(out_e, expand_out))
    while tasks:
        advance(*list(tasks))
    results += [
        local(out_s.at[p], spatial_out.at[:, :, dyn_lanes(narrow_peer(p))]) for p in range(NARROW)
    ]
    results.append(local(out_r, reduce_out))
    for copy in links.sent:
        copy.wait_send()
    for copy in pending:
        copy.wait()
    for copy in results:
        copy.wait()


def rows_first(a):
    return a.transpose(1, 2, 0, 3).reshape(-1, a.shape[3])


def images_first(a, like):
    n, h, w, c = like.shape
    return a.reshape(h, w, n, c).transpose(2, 0, 1, 3)


def per_device(wide, *args):
    (
        views, crops, image_count, w_reduce, w_spatial, w_expand,
        gain_one, shift_one, gain_two, shift_two, gain_three, shift_three, view_cot, crop_cot,
    ) = args
    own = views.shape[3]
    inner = w_reduce.shape[1]
    full = NARROW * inner
    nview = views.shape[0] * views.shape[1] * views.shape[2]
    ncrop = crops.shape[0] * crops.shape[1] * crops.shape[2]
    rows = nview + ncrop
    quantum = CHUNKS * ROW_TILE
    padded = -(-rows // quantum) * quantum
    dims = (views.shape[1], views.shape[0], crops.shape[1], crops.shape[0], rows, padded)
    ntaps = len(TAPS) * inner
    group = min(wide, GROUP)
    vm = pltpu.VMEM
    hbm = pl.BlockSpec(memory_space=pl.ANY)
    outs = pl.pallas_call(
        functools.partial(kernel, wide, dims),
        name="block",
        out_shape=(
            jax.ShapeDtypeStruct((nview, own), BF16),
            jax.ShapeDtypeStruct((ncrop, own), BF16),
            jax.ShapeDtypeStruct((nview, own), BF16),
            jax.ShapeDtypeStruct((ncrop, own), BF16),
            jax.ShapeDtypeStruct((2, group, own // 4, inner), BF16),
            jax.ShapeDtypeStruct((group, ntaps // group, full), BF16),
            jax.ShapeDtypeStruct((group, inner // group, NARROW * own), BF16),
            jax.ShapeDtypeStruct((16, inner), F32),
            jax.ShapeDtypeStruct((8, 128), F32),
        ),
        in_specs=[hbm] * 14,
        out_specs=[hbm] * 9,
        scratch_shapes=[
            pltpu.SMEM((1,), jnp.int32),
            vm((4, 1, inner), F32),
            vm((2, 1, own), F32),
            vm((16, inner), F32),
            vm((8, 128), F32),
            vm((padded, own), BF16),
            vm((NARROW - 1, padded, own), BF16),
            vm((padded, own), BF16),
            vm((2, own, full), BF16),
            vm((ntaps, full), BF16),
            vm((full, own), BF16),
            vm((padded, 128), F32),
            vm((4, wide, 8, 128), F32),
            vm((2, NARROW * wide, 8, 128), F32),
            vm((padded, 2 * inner), F32),
            vm((2, padded, 2 * inner), BF16),
            vm((2, padded, 2 * inner), BF16),
            vm((2, padded, inner), BF16),
            vm((2, padded, inner), BF16),
            vm((padded, inner), F32),
            vm((padded, inner), F32),
            vm((padded, inner), F32),
            vm(((dims[0] + 2) ** 2 * dims[1], inner), BF16),
            vm(((dims[2] + 2) ** 2 * dims[3], inner), BF16),
            vm((padded, ntaps), BF16),
            vm((padded, full), BF16),
            vm((padded, full), BF16),
            vm((padded, own), F32),
            vm((padded, own), BF16),
            vm((padded, full), BF16),
            vm((padded, full), BF16),
            vm((padded, ntaps), F32),
            vm((padded, full), BF16),
            vm((padded, own), BF16),
            vm((padded, own), BF16),
            vm((group, inner // group, NARROW * own), BF16),
            vm((NARROW, group, ntaps // group, inner), BF16),
            vm((2, group, own // 4, inner), BF16),
            vm((NARROW, inner // group, own), BF16),
            vm((group, NARROW, inner // group, own), BF16),
            *[vm((group // 2, NARROW, inner // group, own), BF16)] * 3,
            vm((NARROW, group, ntaps // group, inner), BF16),
            *[vm((NARROW, group // 2, ntaps // group, inner), BF16)] * 3,
            vm((2, group, inner, own // 4), BF16),
            *[vm((2, group // 2, inner, own // 4), BF16)] * 3,
            pltpu.SemaphoreType.DMA((112,)),
            pltpu.SemaphoreType.DMA((112,)),
            pltpu.SemaphoreType.DMA((6,)),
            pltpu.SemaphoreType.DMA((6,)),
            pltpu.SemaphoreType.DMA((34,)),
        ],
        compiler_params=pltpu.CompilerParams(
            collective_id=0, has_side_effects=True, vmem_limit_bytes=62 * 2**20
        ),
    )(
        image_count,
        rows_first(views),
        rows_first(crops),
        rows_first(view_cot),
        rows_first(crop_cot),
        w_reduce,
        w_spatial.reshape(ntaps, full),
        w_expand,
        *(a.reshape(1, -1) for a in (gain_one, shift_one, gain_two, shift_two, gain_three, shift_three)),
    )
    view_out, crop_out, view_grad, crop_grad, reduce_g, spatial_g, expand_g, small, large = outs
    return (
        images_first(view_out, views),
        images_first(crop_out, crops),
        images_first(view_grad, views),
        images_first(crop_grad, crops),
        reduce_g.astype(F32).transpose(1, 0, 2, 3).reshape(NARROW * own, inner),
        spatial_g.astype(F32).reshape(w_spatial.shape),
        expand_g.astype(F32).reshape(w_expand.shape),
        small[0],
        small[1],
        small[8],
        small[9],
        large[:4].reshape(-1),
        large[4:].reshape(-1),
    )


def solution(mesh):
    wide = mesh.shape["wide"]
    image = P("wide", None, None, "narrow")
    vector = P("narrow")
    return jax.shard_map(
        functools.partial(per_device, wide),
        mesh=mesh,
        in_specs=(
            image, image, P("wide"), P(None, "narrow"), P(None, None, "narrow", None), P("narrow", None),
            vector, vector, vector, vector, vector, vector, image, image,
        ),
        out_specs=(
            image, image, image, image, P(None, "narrow"), P(None, None, "narrow", None),
            P("narrow", None), vector, vector, vector, vector, vector, vector,
        ),
        check_vma=False,
    )
```

```python
import functools

import jax
import jax.numpy as jnp
from jax import lax
from jax.experimental import pallas as pl
from jax.experimental.pallas import tpu as pltpu
from jax.sharding import PartitionSpec as P

MESH = pl.DeviceIdType.MESH
EPS = 1e-05
ORDER = (
    ("e", "s0", "s2", "e"),
    ("s2", "s1"),
    ("s3", "s0", "e", "s2"),
    ("r0", "r1", "s3", "s1", "s0", "s2", "e", "s3", "r0", "r1", "s2", "s0", "s1", "s3", "e", "s3", "r0", "s1", "s2", "r1", "s3", "r0", "r1"),
)
WAYS = {"e": "d", "s0": "q", "s1": "q", "s2": "z", "s3": "z", "r0": "q", "r1": "q"}
NARROW = 4
CHUNKS = 4
ROW_TILE = 16
GROUP = 8
VIEWS_EACH = 2
CROPS_EACH = 4
TAPS = [(i, j) for i in range(3) for j in range(3)]
XOR = (0, 2, 1, 3)
POS = (0, 2, 1, 3)
F32 = jnp.float32
BF16 = jnp.bfloat16


def dot(a, b):
    return jnp.dot(a, b, preferred_element_type=F32)


def dot_right(a, b):
    return lax.dot_general(a, b, (((1,), (1,)), ((), ())), preferred_element_type=F32)


def dot_left(a, b):
    return lax.dot_general(a, b, (((0,), (0,)), ((), ())), preferred_element_type=F32)


def logistic(v):
    return 0.5 + 0.5 * jnp.tanh(0.5 * v)


def flip(index, bit):
    return index + bit - 2 * bit * ((index // bit) % 2)


def wider(tile, lanes):
    return jnp.concatenate([tile] * (lanes // 128), axis=1) if lanes > 128 else tile


def fold(v):
    return jnp.sum(v.reshape(v.shape[0] // 8, 8, v.shape[1]), axis=0)


def total(v):
    return jnp.sum(v, axis=0, keepdims=True)


def flat(v):
    return jnp.concatenate([v[k : k + 1] for k in range(v.shape[0])], axis=1)


class Done:
    def wait_recv(self):
        pass


class Links:
    def __init__(self, send_sems, recv_sems):
        self.send_sems, self.recv_sems, self.used, self.sent = send_sems, recv_sems, 0, []

    def send(self, source, target, peer, background=""):
        copy = pltpu.make_async_remote_copy(
            source,
            target,
            self.send_sems.at[self.used],
            self.recv_sems.at[self.used],
            device_id=peer,
            device_id_type=MESH,
        )
        self.used += 1
        copy.start()
        self.sent.append(copy)
        return copy


class Group:
    def __init__(self, links, copies, total, kind):
        self.live = True
        send_sem, recv_sem = links.send_sems.at[links.used], links.recv_sems.at[links.used]
        links.used += 1
        for source, target, peer in copies:
            copy = pltpu.make_async_remote_copy(
                source, target, send_sem, recv_sem, device_id=peer, device_id_type=MESH
            )
            copy.start()
        self.arrival = pltpu.make_async_copy(total, total, recv_sem)
        self.departure = pltpu.make_async_copy(total, total, send_sem)
        links.sent.append(self)

    def wait_recv(self):
        if self.live:
            self.arrival.wait()

    def wait_send(self):
        self.departure.wait()


def kernel(wide, dims, *refs):
    views_side, views_block, crops_side, crops_block, rows, padded = dims
    (
        image_count, views, crops, view_cot, crop_cot, w_reduce, w_spatial, w_expand,
        gain1, shift1, gain2, shift2, gain3, shift3,
        view_out, crop_out, view_grad, crop_grad, reduce_out, spatial_out, expand_out, small_out, large_out,
        count_ref, inner_vectors, outer_vectors, small, large,
        x, xs, cot, wr, ws, we, mask, stat, stat_all, keep, near_out, near_in, far_out, far_in,
        red, mix, back, view_pad, crop_pad, taps, mall, ht, b3, ge, gall, gm, tp, gr, res, dx,
        out_e, out_s, out_r, stage_e, part_e, came_e,
        part_s, came_s, part_r, came_r,
        send_sems, recv_sems, stat_send, stat_recv, local_sems,
    ) = refs
    w = lax.axis_index("wide")
    q = lax.axis_index("narrow")
    near, far = (w, flip(q, 1)), (w, flip(q, 2))
    inner = w_reduce.shape[1]
    own = x.shape[1]
    full = NARROW * inner
    chunk = padded // CHUNKS
    half = 2 * inner
    nview = views.shape[0]
    group = min(wide, GROUP)
    ex = tp.at[:, pl.ds(0, own)]
    links = Links(send_sems, recv_sems)
    slot = [0]

    def local(source, target):
        copy = pltpu.make_async_copy(source, target, local_sems.at[slot[0]])
        slot[0] += 1
        copy.start()
        return copy

    def part(r):
        return pl.ds(r * chunk, chunk)

    def lanes(p, width=inner):
        return pl.ds(p * width, width)

    def dyn_lanes(p, width=inner):
        return pl.ds(pl.multiple_of(p * width, width), width)

    def narrow_peer(p):
        i = q
        if XOR[p] & 1:
            i = flip(i, 1)
        if XOR[p] & 2:
            i = flip(i, 2)
        return i

    def loop(body, init):
        return lax.fori_loop(
            0, CHUNKS, lambda i, c: body(pl.ds(pl.multiple_of(i * chunk, chunk), chunk), c), init
        )

    def own_rows(p):
        return pl.ds(pl.multiple_of(narrow_peer(p) * own, own), own)

    load_count = local(image_count, count_ref)
    load_vectors = [local(ref, inner_vectors.at[k]) for k, ref in enumerate((gain1, shift1, gain2, shift2))]
    load_vectors += [local(ref, outer_vectors.at[k]) for k, ref in enumerate((gain3, shift3))]
    load_reduce = [local(w_reduce.at[own_rows(2 * k), :], wr.at[k, :, lanes(0)]) for k in range(2)]
    load_x = [local(views, x.at[pl.ds(0, nview)]), local(crops, x.at[pl.ds(nview, rows - nview)])]
    load_spatial = [
        local(w_spatial.at[:, dyn_lanes(narrow_peer(p))], ws.at[:, lanes(p)]) for p in range(NARROW)
    ]
    own_expand = local(w_expand.at[:, dyn_lanes(q, own)], we.at[lanes(0), :])
    load_cot = [
        local(view_cot, cot.at[pl.ds(0, nview)]), local(crop_cot, cot.at[pl.ds(nview, rows - nview)])
    ]
    barrier = pltpu.get_barrier_semaphore()

    def greet(k, c):
        pl.semaphore_signal(
            barrier,
            inc=1,
            device_id=(lax.rem(w + k % wide, wide), lax.rem(q + k // wide, NARROW)),
            device_id_type=MESH,
        )
        return c

    everyone = NARROW * wide - 1
    lax.fori_loop(1, everyone + 1, greet, 0, unroll=wide <= 16)

    load_count.wait()
    real = count_ref[0]
    row = lax.broadcasted_iota(jnp.int32, (chunk, 128), 0)
    for r in range(CHUNKS):
        at = row + r * chunk
        image = jnp.where(
            at < nview,
            (at % views_block) // VIEWS_EACH,
            ((at - nview) % crops_block) // CROPS_EACH,
        )
        alive = jnp.where((image < real) & (at < rows), 1.0, 0.0)
        mask[part(r)] = alive.astype(F32)
    tail = pl.ds(rows, padded - rows)
    x[tail] = jnp.zeros((padded - rows, own), BF16)
    xs[1, tail] = jnp.zeros((padded - rows, own), BF16)
    cot[tail] = jnp.zeros((padded - rows, own), BF16)
    taps[tail] = jnp.zeros((padded - rows, len(TAPS) * inner), BF16)
    view_pad[...] = jnp.zeros(view_pad.shape, BF16)
    crop_pad[...] = jnp.zeros(crop_pad.shape, BF16)
    my_count = real.astype(F32) * float(
        VIEWS_EACH * views_side**2 + CROPS_EACH * crops_side**2
    )

    pl.semaphore_wait(barrier, everyone)

    far_reduce = [
        links.send(w_reduce.at[own_rows(1 + 2 * k), :], wr.at[k, :, lanes(1)], far) for k in range(2)
    ]
    near_x = [
        links.send(views, xs.at[1, pl.ds(0, nview)], near),
        links.send(crops, xs.at[1, pl.ds(nview, rows - nview)], near),
    ]
    near_reduce = [links.send(w_reduce.at[own_rows(2), :], wr.at[0, :, lanes(2)], near)]

    def exchange(k, tile, everywhere=False):
        board, me, n = (stat_all, q * wide + w, everyone) if everywhere else (stat, w, wide - 1)
        sem = k + 4 if everywhere else k
        board[k, me] = tile

        def put(step, c):
            pltpu.make_async_remote_copy(
                board.at[k, me],
                board.at[k, me],
                stat_send.at[sem],
                stat_recv.at[sem],
                device_id=(lax.rem(w + step % wide, wide), lax.rem(q + step // wide, NARROW)),
                device_id_type=MESH,
            ).start()
            return c

        lax.fori_loop(1, n + 1, put, 0, unroll=wide <= 16)
        several = board.at[k, pl.ds(0, n)]
        pending.append(pltpu.make_async_copy(several, several, stat_send.at[sem]))
        return pltpu.make_async_copy(several, several, stat_recv.at[sem])

    pending = []

    def moments(ref, after_center=lambda center: None):
        size = ref.shape[1]
        zero = jnp.zeros((8, size), F32)
        sums = total(loop(lambda at, c: c + fold(ref[at, :] * wider(mask[at, :], size)), zero))
        center = sums / my_count
        after_center(center)
        squares = total(
            loop(
                lambda at, c: c + fold(jnp.square(ref[at, :] - center) * wider(mask[at, :], size)),
                zero,
            )
        )
        return sums, squares

    def rows_of(k, lo, n):
        return stat[k, :, pl.ds(lo, n), :]

    def combine(sums, squares, counts, pixels):
        center = jnp.sum(sums, axis=0) / pixels
        spread = (
            jnp.sum(squares + counts * jnp.square(sums / counts - center[None]), axis=0) / pixels
        )
        return center, lax.rsqrt(spread + EPS)

    def reduce_scatter(k, give, hold, target, before_hold=lambda: None, meanwhile=lambda: None):
        first, second = [], []
        for copy in in_use.pop(k, ()):
            copy.wait_send()
            links.sent = [other for other in links.sent if other is not copy]
        for r in range(CHUNKS):
            near_out[k, part(r)] = give(r).astype(BF16)
            first.append(links.send(near_out.at[k, part(r)], near_in.at[k, part(r)], near))
        before_hold()
        for r in range(CHUNKS):
            keep[part(r)] = hold(r)
            first[r].wait_recv()
            far_out[k, part(r)] = (
                keep[part(r), lanes(1)] + near_in[k, part(r), lanes(1)].astype(F32)
            ).astype(BF16)
            second.append(links.send(far_out.at[k, part(r)], far_in.at[k, part(r)], far))
            target[part(r)] = keep[part(r), lanes(0)] + near_in[k, part(r), lanes(0)].astype(F32)
        meanwhile()
        for r in range(CHUNKS):
            second[r].wait_recv()
            target[part(r)] = target[part(r)] + far_in[k, part(r)].astype(F32)
        in_use[k] = first + second

    in_use = {}

    def gather_start(ref):
        across = [
            links.send(ref.at[part(r), lanes(0)], ref.at[part(r), lanes(1)], far) for r in range(CHUNKS)
        ]
        straight = links.send(ref.at[:, lanes(0)], ref.at[:, lanes(2)], near)
        return across, straight, []

    def gather_pass(ref, copies, some):
        across, straight, onward = copies
        for r in some:
            across[r].wait_recv()
            onward.append(links.send(ref.at[part(r), lanes(1)], ref.at[part(r), lanes(3)], near))

    def gather_end(ref, copies, use=lambda r: None):
        across, straight, onward = copies
        for r in range(CHUNKS + 1):
            if len(onward) < CHUNKS:
                gather_pass(ref, copies, [len(onward)])
            if r == 1:
                straight.wait_recv()
            if r > 0:
                onward[r - 1].wait_recv()
                use(r - 1)

    pieces, low = [], 0
    for r in range(2 * CHUNKS):
        size = chunk // 2 // ROW_TILE * ROW_TILE
        size = size if r % 2 else chunk - size
        pieces.append(pl.ds(low, size))
        low += size
    across_x, onward_x = [], []

    def share_x(count):
        for _ in range(count):
            at = pieces[len(across_x)]
            across_x.append(links.send(x.at[at], xs.at[0, at], far, "x"))

    def share_end():
        while len(onward_x) < len(across_x):
            at = pieces[len(onward_x)]
            across_x[len(onward_x)].wait_recv()
            onward_x.append(links.send(xs.at[0, at], xs.at[2, at], near, "x"))

    group_start = w - lax.rem(w, group)

    def block_of(bits, index):
        return sum((index // bit) % 2 * (group // 2 >> k) for k, bit in enumerate(bits))

    def beyond(value, spare):
        bit, at = group, group
        while bit < wide:
            spare[at] = value.astype(BF16)
            copy = links.send(spare.at[at], spare.at[at + 1], (flip(w, bit), q))
            copy.wait_recv()
            value = spare[at].astype(F32) + spare[at + 1].astype(F32)
            bit, at = bit * 2, at + 2
        return value

    def add_block(parts, at, came):
        parts[at] = (parts[at].astype(F32) + came.astype(F32)).astype(BF16)

    def halved(kind, bits, parts, came, finish):
        low, size = 0, group
        for bit in bits:
            size //= 2
            side = (w // bit) % 2
            box = pl.ds(group - 2 * size, size)
            copy = links.send(
                parts.at[pl.ds(low + (1 - side) * size, size)], came.at[box], (flip(w, bit), q), kind
            )
            yield
            copy.wait_recv()
            low = low + side * size
            if size > 1:
                for k in range(size):
                    add_block(parts, low + k, came[group - 2 * size + k])
        value = parts[low].astype(F32) + came[group - 2].astype(F32)
        yield from finish(beyond(value, came))

    def doubled(kind, bits, out):
        low, size = block_of(bits, w), 1
        for bit in reversed(bits):
            box = pl.ds(low, size)
            copy = links.send(out.at[box], out.at[box], (flip(w, bit), q), kind)
            yield
            copy.wait_recv()
            low = low - (w // bit) % 2 * size
            size *= 2

    def group_peers(among):
        for k in range(1, len(among)):
            place = (lax.rem(w, group) + k * (among[1] - among[0])) % group
            yield (group_start + place, q), place

    def halved_then_direct(kind, bits, parts, came, finish):
        quads = group // 2
        side = (w // bits[0]) % 2
        copy = links.send(
            parts.at[pl.ds((1 - side) * quads, quads)], came.at[pl.ds(0, quads)], (flip(w, bits[0]), q), kind
        )
        yield
        copy.wait_recv()
        for k in range(quads):
            add_block(parts, side * quads + k, came[k])
        mine = block_of(bits, w)
        copy = Group(
            links,
            [
                (parts.at[block_of(bits, place)], came.at[quads + mine % quads], peer)
                for peer, place in group_peers(range(0, group, 2))
            ],
            came.at[pl.ds(quads, quads - 1)],
            kind,
        )
        came[quads + mine % quads] = parts[mine]
        yield
        copy.wait_recv()
        value = jnp.sum(came[pl.ds(quads, quads)].astype(F32), axis=0)
        yield from finish(beyond(value, came))

    def direct_then_doubled(kind, bits, out):
        mine = block_of(bits, w)
        copy = Group(
            links,
            [(out.at[mine], out.at[mine], peer) for peer, _ in group_peers(range(0, group, 2))],
            out.at[pl.ds(0, group // 2 - 1)],
            kind,
        )
        yield
        copy.wait_recv()
        box = pl.ds((w // bits[0]) % 2 * (group // 2), group // 2)
        copy = links.send(out.at[box], out.at[box], (flip(w, bits[0]), q), kind)
        yield
        copy.wait_recv()

    def direct(kind, bits, parts, came, finish):
        mine = block_of(bits, w)
        copy = Group(
            links,
            [
                (parts.at[block_of(bits, place)], came.at[mine], peer)
                for peer, place in group_peers(range(group))
            ],
            came.at[pl.ds(0, group - 1)],
            kind,
        )
        came[mine] = parts[mine]
        yield
        copy.wait_recv()
        value = jnp.sum(came[pl.ds(0, group)].astype(F32), axis=0)
        yield from finish(beyond(value, came))

    ways = {
        "h": ((1, 2, 4), halved, doubled),
        "z": ((2, 1, 4), halved, doubled),
        "q": ((1, 2, 4), halved_then_direct, direct_then_doubled),
        "d": ((1, 2, 4), direct, doubled),
    }

    def all_reduced(kind, way, parts, came, out, keep_sum, between=lambda: iter(())):
        bits, there, back = ways[way]

        def finish(value):
            keep_sum(block_of(bits, w), value)
            yield from between()
            yield from back(kind, bits, out)

        return there(kind, bits, parts, came, finish)

    tasks = {}

    def begin(name, task):
        tasks[name] = task
        next(task)

    def advance(*names):
        for name in names:
            if name in tasks and next(tasks[name], "end") == "end":
                del tasks[name]

    for copy in load_reduce + load_x:
        copy.wait()
    for copy in near_x:
        copy.wait_recv()

    def reduce_part(r, p):
        return dot(x[part(r)], wr[0, :, lanes(p)]) + dot(xs[1, part(r)], wr[1, :, lanes(p)])

    for r in range(CHUNKS):
        red[part(r)] = reduce_part(r, 0)
    for copy in far_reduce:
        copy.wait_recv()
    came = []
    for r in range(CHUNKS):
        far_out[0, part(r)] = reduce_part(r, 1).astype(BF16)
        came.append(links.send(far_out.at[0, part(r)], far_in.at[0, part(r)], far))
    near_reduce.append(links.send(wr.at[1, :, lanes(1)], wr.at[0, :, lanes(3)], near))
    for r in range(CHUNKS):
        came[r].wait_recv()
        red[part(r)] = red[part(r)] + far_in[0, part(r)].astype(F32)
    in_use[0] = came
    sent_expand = {
        p: links.send(
            w_expand.at[:, dyn_lanes(narrow_peer(p), own)], we.at[lanes(p), :], (w, narrow_peer(p))
        )
        for p in (3, 1, 2)
    }
    share_x(1)
    sums, squares = moments(red)
    arrived = exchange(
        0,
        jnp.concatenate(
            [sums, squares, jnp.full((1, inner), my_count, F32), jnp.zeros((5, inner), F32)], axis=0
        ),
    )
    for copy in load_spatial:
        copy.wait()
    arrived.wait()
    counts = rows_of(0, 2, 1)
    pixels = jnp.sum(counts, axis=0)
    center1, inverse1 = combine(rows_of(0, 0, 1), rows_of(0, 1, 1), counts, pixels)

    def normed(v, center, inverse, gain, shift):
        standard = (v - center) * inverse
        return standard, gain * standard + shift

    for copy in load_vectors:
        copy.wait()
    g1, s1, g2, s2 = (inner_vectors[k] for k in range(4))
    g3, s3 = (outer_vectors[k] for k in range(2))
    grids = (
        (views_side, views_block, 0, view_pad),
        (crops_side, crops_block, nview, crop_pad),
    )
    for side, block, lead, pad in grids:
        line = side * block
        for h in range(side):
            _, v = normed(red[pl.ds(lead + h * line, line)], center1, inverse1, g1, s1)
            pad[pl.ds(((h + 1) * (side + 2) + 1) * block, line)] = (v * logistic(v)).astype(BF16)
    for side, block, lead, pad in grids:
        line = side * block
        for t, (i, j) in enumerate(TAPS):
            for h in range(side):
                taps[pl.ds(lead + h * line, line), lanes(t)] = pad[
                    pl.ds(((h + i) * (side + 2) + j) * block, line)
                ]

    reduce_scatter(
        1,
        lambda r: dot(taps[part(r)], ws[:, pl.ds(half, half)]),
        lambda r: dot(taps[part(r)], ws[:, pl.ds(0, half)]),
        mix,
    )

    copies = []

    def centered(center):
        def body(at, c):
            mall[at, lanes(0)] = (mix[at] - center).astype(BF16)
            return c

        loop(body, 0)
        copies.append(gather_start(mall))

    sums, squares = moments(mix, centered)
    arrived = exchange(
        0, jnp.concatenate([sums, squares, g2, s2, jnp.zeros((4, inner), F32)], axis=0), True
    )
    own_expand.wait()
    for p in (2, 3, 1):
        sent_expand[p].wait_recv()
    gather_pass(mall, copies[0], range(2))
    arrived.wait()

    def board_rows(k, p, lo, n):
        return stat_all[k, pl.ds(narrow_peer(p) * wide, wide), pl.ds(lo, n), :]

    def board_row(k, p, lo):
        return stat_all[k, narrow_peer(p) * wide + w, pl.ds(lo, 1), :]

    blocks = [
        combine(board_rows(0, p, 0, 1), board_rows(0, p, 1, 1), counts, pixels) for p in range(NARROW)
    ]
    center2, inverse2 = blocks[0]
    inverse_all = jnp.concatenate([b[1] for b in blocks], axis=1)
    offset_all = jnp.concatenate(
        [board_row(0, p, 0) / my_count - blocks[p][0] for p in range(NARROW)], axis=1
    )
    gain_all = jnp.concatenate([board_row(0, p, 2) for p in range(NARROW)], axis=1)
    shift_all = jnp.concatenate([board_row(0, p, 3) for p in range(NARROW)], axis=1)
    scale_all = gain_all * inverse_all
    constant_all = scale_all * offset_all + shift_all

    def expand(r):
        v = mall[part(r), :].astype(F32) * scale_all + constant_all
        ht[part(r), :] = (v * logistic(v)).astype(BF16)
        ex[part(r), :] = dot(ht[part(r)], we[...])

    gather_end(mall, copies[0], expand)
    share_end()
    share_x(4)
    sums, squares = moments(ex)
    groups = own // 128

    def tiles(*values):
        return jnp.concatenate(
            [v[:, 128 * k : 128 * k + 128] for v in values for k in range(groups)], axis=0
        )

    arrived = exchange(1, tiles(sums, squares))
    for copy in load_cot:
        copy.wait()
    arrived.wait()
    center3, inverse3 = combine(
        rows_of(1, 0, groups), rows_of(1, groups, groups), counts, pixels
    )
    center3, inverse3 = flat(center3), flat(inverse3)

    def third(at, c):
        standard, v = normed(ex[at, :], center3, inverse3, g3, s3)
        v = v + x[at].astype(F32)
        s = logistic(v)
        alive = wider(mask[at], own)
        res[at] = (alive * (v * s)).astype(BF16)
        g = cot[at].astype(F32) * alive * (s * (1.0 + v * (1.0 - s)))
        b3[at] = g
        return c[0] + fold(g), c[1] + fold(g * standard)

    zero = jnp.zeros((8, own), F32)
    shift_sum, gain_sum = loop(third, (zero, zero))
    arrived = exchange(2, tiles(total(gain_sum), total(shift_sum)))
    results = [
        local(res.at[pl.ds(0, nview)], view_out), local(res.at[pl.ds(nview, rows - nview)], crop_out)
    ]
    arrived.wait()
    both = jnp.sum(stat[2], axis=0)
    large[...] = both
    results.append(local(large, large_out))

    def back_terms(gain_grad, shift_grad, offset, inverse, gain, n):
        scale = gain * inverse
        slope = scale * inverse * (gain_grad / n)
        return scale, scale * (shift_grad / n) + slope * offset, slope

    scale3, base3, slope3 = back_terms(
        flat(both[:groups]), flat(both[groups:]), -center3, inverse3, g3, wider(pixels, own)
    )

    def third_back(at, c):
        ge[at] = (
            scale3 * b3[at] - wider(mask[at], own) * (base3 + slope3 * ex[at, :])
        ).astype(BF16)
        return c

    loop(third_back, 0)

    size_e = inner // group

    def keep_e(mine, value):
        stage_e[...] = value.astype(BF16)
        out_e[mine, :, dyn_lanes(q, own)] = stage_e[0]

    def hand_on_e():
        mine = block_of(ways[WAYS["e"]][0], w)
        got = [
            links.send(
                stage_e.at[p], out_e.at[mine, :, dyn_lanes(q, own)], (w, narrow_peer(p)), "e"
            )
            for p in range(1, NARROW)
        ]
        yield
        for copy in got:
            copy.wait_recv()

    def expand_gradient():
        value = dot_left(ht[...], ge[...]).astype(BF16)
        for p in range(NARROW):
            part_e[:, p] = value[inner * p : inner * (p + 1)].reshape(group, size_e, own)
        begin("e", all_reduced("e", WAYS["e"], part_e, came_e, out_e, keep_e, hand_on_e))
        share_end()

    reduce_scatter(
        0,
        lambda r: dot_right(ge[part(r)], we[pl.ds(half, half), :]),
        lambda r: dot_right(ge[part(r)], we[pl.ds(0, half), :]),
        back,
        meanwhile=expand_gradient,
    )

    def slope_of(v):
        s = logistic(v)
        return s * (1.0 + v * (1.0 - s))

    def second_back(at, c):
        standard, v = normed(mix[at], center2, inverse2, g2, s2)
        g = back[at] * slope_of(v)
        gall[at, lanes(0)] = g.astype(BF16)
        return c[0] + fold(g), c[1] + fold(g * standard)

    zero = jnp.zeros((8, inner), F32)
    shift_sum, gain_sum = loop(second_back, (zero, zero))
    copies = gather_start(gall)
    arrived = exchange(
        1,
        jnp.concatenate([total(gain_sum), total(shift_sum), jnp.zeros((6, inner), F32)], axis=0),
        True,
    )
    gather_pass(gall, copies, range(2))
    arrived.wait()
    sums = [jnp.sum(board_rows(1, p, 0, 2), axis=0) for p in range(NARROW)]
    small[pl.ds(8, 8)] = jnp.concatenate([sums[0], jnp.zeros((6, inner), F32)], axis=0)
    scale2, base2, slope2 = back_terms(
        jnp.concatenate([v[0:1] for v in sums], axis=1),
        jnp.concatenate([v[1:2] for v in sums], axis=1),
        offset_all,
        inverse_all,
        gain_all,
        wider(pixels, full),
    )

    def columns(v, p, n=1):
        return v[:, inner * p : inner * (p + n)]

    def grad_mixed(at, some):
        for p in some:
            gm[at, lanes(p)] = (
                columns(scale2, p) * gall[at, lanes(p)].astype(F32)
                - mask[at] * (columns(base2, p) + columns(slope2, p) * mall[at, lanes(p)].astype(F32))
            ).astype(BF16)
        return 0

    def spatial_gradient(*some):
        value = dot_left(taps[...], jnp.concatenate([gm[:, lanes(p)] for p in some], axis=1))
        for k, p in enumerate(some):
            part_s[p] = columns(value, k).astype(BF16).reshape(part_s.shape[1:])

            def keep_s(mine, value, p=p):
                out_s[p, mine] = value.astype(BF16)

            name = "s%d" % p
            begin(
                name, all_reduced("s", WAYS[name], part_s.at[p], came_s.at[p], out_s.at[p], keep_s)
            )

    copies[1].wait_recv()
    loop(lambda at, c: grad_mixed(at, (0, 2)), 0)
    spatial_gradient(0, 2)
    advance("e")

    def spatial_back(r):
        grad_mixed(part(r), (1, 3))
        tp[part(r)] = dot_right(gm[part(r)], ws[...])

    gather_end(gall, (copies[0], Done(), copies[2]), spatial_back)
    share_x(3)
    shift_sum = gain_sum = zero
    for side, block, lead, pad in grids:
        line = side * block
        for h in range(side):
            g = None
            for t, (i, j) in enumerate(TAPS):
                source = h - (i - 1)
                if not 0 <= source < side:
                    continue
                first = lead + source * line
                if j == 1:
                    term = tp[pl.ds(first, line), lanes(t)]
                elif j == 0:
                    term = jnp.concatenate(
                        [tp[pl.ds(first + block, line - block), lanes(t)], jnp.zeros((block, inner), F32)]
                    )
                else:
                    term = jnp.concatenate(
                        [jnp.zeros((block, inner), F32), tp[pl.ds(first, line - block), lanes(t)]]
                    )
                g = term if g is None else g + term
            at = pl.ds(lead + h * line, line)
            standard, v = normed(red[at], center1, inverse1, g1, s1)
            g = g * slope_of(v)
            back[at] = g
            shift_sum = shift_sum + fold(g)
            gain_sum = gain_sum + fold(g * standard)
    back[tail] = jnp.zeros((padded - rows, inner), F32)
    arrived = exchange(
        3, jnp.concatenate([total(gain_sum), total(shift_sum), jnp.zeros((6, inner), F32)], axis=0)
    )

    spatial_gradient(1, 3)
    advance(*ORDER[0])
    arrived.wait()
    both = jnp.sum(stat[3], axis=0)
    small[pl.ds(0, 8)] = both
    results.append(local(small, small_out))
    scale1, base1, slope1 = back_terms(both[0:1], both[1:2], -center1, inverse1, g1, pixels)

    def first_grad(at, c):
        gr[at, lanes(0)] = (scale1 * back[at] - mask[at] * (base1 + slope1 * red[at])).astype(BF16)
        return c

    loop(first_grad, 0)
    copies = gather_start(gr)

    per = own // 4

    def reduce_gradient(k):
        for p in (k, 2 + k):
            source = x[...] if p == 0 else xs[p - 1]
            value = dot_left(gr[:, lanes(0)], source).astype(BF16)
            for m in range(4):
                part_r[k, narrow_peer(p) % 2 * 4 + m] = value[:, per * m : per * m + per]

        def keep_r(mine, value):
            out_r[k, mine] = value.T.astype(BF16)

        name = "r%d" % k
        begin(name, all_reduced("r", WAYS[name], part_r.at[k], came_r.at[k], out_r.at[k], keep_r))

    reduce_gradient(0)
    advance(*ORDER[1])
    share_end()
    for copy in onward_x:
        copy.wait_recv()
    reduce_gradient(1)
    advance(*ORDER[2])

    def input_gradient(r):
        dx[part(r)] = (dot_right(gr[part(r)], wr[0]) + b3[part(r)]).astype(BF16)

    for copy in near_reduce:
        copy.wait_recv()
    gather_end(gr, copies, input_gradient)
    results += [
        local(dx.at[pl.ds(0, nview)], view_grad), local(dx.at[pl.ds(nview, rows - nview)], crop_grad)
    ]
    advance(*ORDER[3])
    results.append(local(out_e, expand_out))
    while tasks:
        advance(*list(tasks))
    results += [
        local(out_s.at[p], spatial_out.at[:, :, dyn_lanes(narrow_peer(p))]) for p in range(NARROW)
    ]
    chip = q // 2
    results += [local(out_r.at[0], reduce_out.at[chip]), local(out_r.at[1], reduce_out.at[1 - chip])]
    for copy in links.sent:
        copy.wait_send()
    for copy in pending:
        copy.wait()
    for copy in results:
        copy.wait()


def rows_first(a):
    return a.transpose(1, 2, 0, 3).reshape(-1, a.shape[3])


def images_first(a, like):
    n, h, w, c = like.shape
    return a.reshape(h, w, n, c).transpose(2, 0, 1, 3)


def per_device(wide, *args):
    (
        views, crops, image_count, w_reduce, w_spatial, w_expand,
        gain_one, shift_one, gain_two, shift_two, gain_three, shift_three, view_cot, crop_cot,
    ) = args
    own = views.shape[3]
    inner = w_reduce.shape[1]
    full = NARROW * inner
    nview = views.shape[0] * views.shape[1] * views.shape[2]
    ncrop = crops.shape[0] * crops.shape[1] * crops.shape[2]
    rows = nview + ncrop
    quantum = CHUNKS * ROW_TILE
    padded = -(-rows // quantum) * quantum
    dims = (views.shape[1], views.shape[0], crops.shape[1], crops.shape[0], rows, padded)
    ntaps = len(TAPS) * inner
    group = min(wide, GROUP)
    slots = group + 2 * ((wide // group).bit_length() - 1)
    vm = pltpu.VMEM
    hbm = pl.BlockSpec(memory_space=pltpu.HBM)
    outs = pl.pallas_call(
        functools.partial(kernel, wide, dims),
        name="block",
        out_shape=(
            jax.ShapeDtypeStruct((nview, own), BF16),
            jax.ShapeDtypeStruct((ncrop, own), BF16),
            jax.ShapeDtypeStruct((nview, own), BF16),
            jax.ShapeDtypeStruct((ncrop, own), BF16),
            jax.ShapeDtypeStruct((2, group, own // 4, inner), BF16),
            jax.ShapeDtypeStruct((group, ntaps // group, full), BF16),
            jax.ShapeDtypeStruct((group, inner // group, NARROW * own), BF16),
            jax.ShapeDtypeStruct((16, inner), F32),
            jax.ShapeDtypeStruct((8, 128), F32),
        ),
        in_specs=[hbm] * 14,
        out_specs=[hbm] * 9,
        scratch_shapes=[
            pltpu.SMEM((1,), jnp.int32),
            vm((4, 1, inner), F32),
            vm((2, 1, own), F32),
            vm((16, inner), F32),
            vm((8, 128), F32),
            vm((padded, own), BF16),
            vm((NARROW - 1, padded, own), BF16),
            vm((padded, own), BF16),
            vm((2, own, full), BF16),
            vm((ntaps, full), BF16),
            vm((full, own), BF16),
            vm((padded, 128), F32),
            vm((4, wide, 8, 128), F32),
            vm((2, NARROW * wide, 8, 128), F32),
            vm((padded, 2 * inner), F32),
            vm((2, padded, 2 * inner), BF16),
            vm((2, padded, 2 * inner), BF16),
            vm((2, padded, inner), BF16),
            vm((2, padded, inner), BF16),
            vm((padded, inner), F32),
            vm((padded, inner), F32),
            vm((padded, inner), F32),
            vm(((dims[0] + 2) ** 2 * dims[1], inner), BF16),
            vm(((dims[2] + 2) ** 2 * dims[3], inner), BF16),
            vm((padded, ntaps), BF16),
            vm((padded, full), BF16),
            vm((padded, full), BF16),
            vm((padded, own), F32),
            vm((padded, own), BF16),
            vm((padded, full), BF16),
            vm((padded, full), BF16),
            vm((padded, ntaps), F32),
            vm((padded, full), BF16),
            vm((padded, own), BF16),
            vm((padded, own), BF16),
            vm((group, inner // group, NARROW * own), BF16),
            vm((NARROW, group, ntaps // group, inner), BF16),
            vm((2, group, own // 4, inner), BF16),
            vm((NARROW, inner // group, own), BF16),
            vm((group, NARROW, inner // group, own), BF16),
            vm((slots, NARROW, inner // group, own), BF16),
            vm((NARROW, group, ntaps // group, inner), BF16),
            vm((NARROW, slots, ntaps // group, inner), BF16),
            vm((2, group, inner, own // 4), BF16),
            vm((2, slots, inner, own // 4), BF16),
            pltpu.SemaphoreType.DMA((112,)),
            pltpu.SemaphoreType.DMA((112,)),
            pltpu.SemaphoreType.DMA((6,)),
            pltpu.SemaphoreType.DMA((6,)),
            pltpu.SemaphoreType.DMA((34,)),
        ],
        compiler_params=pltpu.CompilerParams(
            collective_id=0, has_side_effects=True, vmem_limit_bytes=62 * 2**20
        ),
    )(
        image_count,
        rows_first(views),
        rows_first(crops),
        rows_first(view_cot),
        rows_first(crop_cot),
        w_reduce,
        w_spatial.reshape(ntaps, full),
        w_expand,
        *(a.reshape(1, -1) for a in (gain_one, shift_one, gain_two, shift_two, gain_three, shift_three)),
    )
    shapes = [(outs[k].shape, BF16) for k in range(4)]
    shapes += [((NARROW * own, inner), F32), ((ntaps, full), F32), ((inner, NARROW * own), F32)]
    shapes += [((inner,), F32)] * 4 + [((own,), F32)] * 2
    outs = pl.pallas_call(
        release,
        name="release",
        out_shape=tuple(jax.ShapeDtypeStruct(*shape) for shape in shapes),
        in_specs=[hbm] * len(outs),
        out_specs=[hbm] * len(shapes),
        scratch_shapes=[
            vm(outs[4].shape, BF16),
            vm(outs[5].shape, BF16),
            vm(outs[6].shape, BF16),
            vm(shapes[4][0], F32),
            vm(shapes[5][0], F32),
            vm(shapes[6][0], F32),
            *[vm(outs[k].shape, BF16) for k in range(4)],
            vm(outs[7].shape, F32),
            vm(outs[8].shape, F32),
            pltpu.SemaphoreType.DMA((34,)),
        ],
        compiler_params=pltpu.CompilerParams(vmem_limit_bytes=62 * 2**20),
    )(*outs)
    images = (views, crops, views, crops)
    return (
        *(images_first(a, like) for a, like in zip(outs[:4], images)),
        outs[4],
        outs[5].reshape(w_spatial.shape),
        *outs[6:],
    )


def release(*refs):
    images, (reduce_in, spatial_in, expand_in, small, large) = refs[:4], refs[4:9]
    outs, (reduce_v, spatial_v, expand_v, reduce_f, spatial_f, expand_f, *staged, small_v, large_v, sems) = (
        refs[9:22],
        refs[22:],
    )
    used = [0]

    def copy(source, target):
        started = pltpu.make_async_copy(source, target, sems.at[used[0]])
        used[0] += 1
        started.start()
        return started

    loads = [copy(spatial_in, spatial_v), copy(expand_in, expand_v), copy(reduce_in, reduce_v)]
    arrivals = [copy(a, b) for a, b in zip(images, staged)]
    small_in, large_in = copy(small, small_v), copy(large, large_v)
    waits = []
    for started, a, b in zip(arrivals, staged, outs[:4]):
        started.wait()
        waits.append(copy(a, b))
    small_in.wait()
    large_in.wait()
    for k, row in enumerate((0, 1, 8, 9)):
        waits.append(copy(small_v.at[row], outs[7 + k]))
    groups = large.shape[0] // 2
    for k in range(2):
        for g in range(groups):
            waits.append(copy(large_v.at[k * groups + g], outs[11 + k].at[pl.ds(128 * g, 128)]))
    loads[0].wait()
    spatial_f[...] = spatial_v[...].astype(F32).reshape(spatial_f.shape)
    waits.append(copy(spatial_f, outs[5]))
    loads[1].wait()
    expand_f[...] = expand_v[...].astype(F32).reshape(expand_f.shape)
    waits.append(copy(expand_f, outs[6]))
    loads[2].wait()
    blocks, rows = reduce_v.shape[1:3]
    for k in range(2):
        for c in range(blocks):
            reduce_f[pl.ds((k * blocks + c) * rows, rows)] = reduce_v[k, c].astype(F32)
    waits.append(copy(reduce_f, outs[4]))
    for started in waits:
        started.wait()


def solution(mesh):
    wide = mesh.shape["wide"]
    image = P("wide", None, None, "narrow")
    vector = P("narrow")
    return jax.shard_map(
        functools.partial(per_device, wide),
        mesh=mesh,
        in_specs=(
            image, image, P("wide"), P(None, "narrow"), P(None, None, "narrow", None), P("narrow", None),
            vector, vector, vector, vector, vector, vector, image, image,
        ),
        out_specs=(
            image, image, image, image, P(None, "narrow"), P(None, None, "narrow", None),
            P("narrow", None), vector, vector, vector, vector, vector, vector,
        ),
        check_vma=False,
    )
```

```python
import functools

import jax
import jax.numpy as jnp
from jax import lax
from jax.experimental import pallas as pl
from jax.experimental.pallas import tpu as pltpu
from jax.sharding import PartitionSpec as P

MESH = pl.DeviceIdType.MESH
EPS = 1e-05
ORDER = (
    ('e', 's0', 's2', 'e'),
    ('s2', 's1'),
    ('s3', 's2', 's0', 'e'),
    ('r0', 'r1', 's3', 's1', 's0', 's2', 's3', 'e', 'r0', 'r1', 's2', 's0', 's1', 's3', 'e', 's3', 'r0', 's1', 's2', 'r1', 's3', 'r0', 'r1'),
)
WAYS = {"e": "d", "s0": "q", "s1": "q", "s2": "z", "s3": "z", "r0": "q", "r1": "q"}
NARROW = 4
CHUNKS = 2
COPIES = 75
ROW_TILE = 16
GROUP = 8
VIEWS_EACH = 2
CROPS_EACH = 4
TAPS = [(i, j) for i in range(3) for j in range(3)]
XOR = (0, 2, 1, 3)
POS = (0, 2, 1, 3)
F32 = jnp.float32
BF16 = jnp.bfloat16


def dot(a, b):
    return jnp.dot(a, b, preferred_element_type=F32)


def dot_right(a, b):
    return lax.dot_general(a, b, (((1,), (1,)), ((), ())), preferred_element_type=F32)


def dot_left(a, b):
    return lax.dot_general(a, b, (((0,), (0,)), ((), ())), preferred_element_type=F32)


def logistic(v):
    return 0.5 + 0.5 * jnp.tanh(0.5 * v)


def flip(index, bit):
    return index + bit - 2 * bit * ((index // bit) % 2)


def wider(tile, lanes):
    return jnp.concatenate([tile] * (lanes // 128), axis=1) if lanes > 128 else tile


def fold(v):
    return jnp.sum(v.reshape(v.shape[0] // 8, 8, v.shape[1]), axis=0)


def total(v):
    return jnp.sum(v, axis=0, keepdims=True)


def flat(v):
    return jnp.concatenate([v[k : k + 1] for k in range(v.shape[0])], axis=1)


class Links:
    def __init__(self, send_sems, recv_sems):
        self.send_sems, self.recv_sems, self.used, self.sent = send_sems, recv_sems, 0, []

    def send(self, source, target, peer, background=""):
        copy = pltpu.make_async_remote_copy(
            source,
            target,
            self.send_sems.at[self.used],
            self.recv_sems.at[self.used],
            device_id=peer,
            device_id_type=MESH,
        )
        self.used += 1
        copy.start()
        self.sent.append(copy)
        return copy

    def settle(self, copy):
        if any(other is copy for other in self.sent):
            copy.wait_send()
            self.sent = [other for other in self.sent if other is not copy]


class Group:
    def __init__(self, links, copies, total, kind):
        self.live = True
        send_sem, recv_sem = links.send_sems.at[links.used], links.recv_sems.at[links.used]
        links.used += 1
        for source, target, peer in copies:
            copy = pltpu.make_async_remote_copy(
                source, target, send_sem, recv_sem, device_id=peer, device_id_type=MESH
            )
            copy.start()
        self.arrival = pltpu.make_async_copy(total, total, recv_sem)
        self.departure = pltpu.make_async_copy(total, total, send_sem)
        links.sent.append(self)

    def wait_recv(self):
        if self.live:
            self.arrival.wait()

    def wait_send(self):
        self.departure.wait()


def kernel(wide, dims, *refs):
    views_side, views_block, crops_side, crops_block, rows, padded = dims
    (
        image_count, views, crops, view_cot, crop_cot, w_reduce, w_spatial, w_expand,
        gain1, shift1, gain2, shift2, gain3, shift3,
        view_out, crop_out, view_grad, crop_grad, reduce_out, spatial_out, expand_out, small_out, large_out,
        count_ref, inner_vectors, outer_vectors, small, large,
        x, xs, cot, wr, ws, we, mask, stat, stat_all, keep, near_out, near_in, far_out, far_in,
        red, mix, back, view_pad, crop_pad, taps, mall, ht, b3, ge, gall, gm, tp, gr, res, dx,
        out_e, out_s, out_r, stage_e, part_e, came_e,
        part_s, came_s, part_r, came_r,
        send_sems, recv_sems, stat_send, stat_recv, local_sems,
    ) = refs
    w = lax.axis_index("wide")
    q = lax.axis_index("narrow")
    near, far = (w, flip(q, 1)), (w, flip(q, 2))
    inner = w_reduce.shape[1]
    own = x.shape[1]
    full = NARROW * inner
    chunk = padded // CHUNKS
    half = 2 * inner
    nview = views.shape[0]
    group = min(wide, GROUP)
    ex = tp.at[:, pl.ds(0, own)]
    links = Links(send_sems, recv_sems)
    slot = [0]

    def local(source, target):
        copy = pltpu.make_async_copy(source, target, local_sems.at[slot[0]])
        slot[0] += 1
        copy.start()
        return copy

    def part(r):
        return pl.ds(r * chunk, chunk)

    def lanes(p, width=inner):
        return pl.ds(p * width, width)

    def dyn_lanes(p, width=inner):
        return pl.ds(pl.multiple_of(p * width, width), width)

    def narrow_peer(p):
        i = q
        if XOR[p] & 1:
            i = flip(i, 1)
        if XOR[p] & 2:
            i = flip(i, 2)
        return i

    def loop(body, init):
        return lax.fori_loop(
            0, CHUNKS, lambda i, c: body(pl.ds(pl.multiple_of(i * chunk, chunk), chunk), c), init
        )

    def own_rows(p):
        return pl.ds(pl.multiple_of(narrow_peer(p) * own, own), own)

    load_count = local(image_count, count_ref)
    load_vectors = [local(ref, inner_vectors.at[k]) for k, ref in enumerate((gain1, shift1, gain2, shift2))]
    load_vectors += [local(ref, outer_vectors.at[k]) for k, ref in enumerate((gain3, shift3))]
    load_reduce = [local(w_reduce.at[own_rows(2 * k), :], wr.at[k, :, lanes(0)]) for k in range(2)]
    load_x = [local(views, x.at[pl.ds(0, nview)]), local(crops, x.at[pl.ds(nview, rows - nview)])]
    load_spatial = [
        local(w_spatial.at[:, dyn_lanes(narrow_peer(p))], ws.at[:, lanes(p)]) for p in range(NARROW)
    ]
    own_expand = local(w_expand.at[:, dyn_lanes(q, own)], we.at[lanes(0), :])
    load_cot = [
        local(view_cot, cot.at[pl.ds(0, nview)]), local(crop_cot, cot.at[pl.ds(nview, rows - nview)])
    ]
    barrier = pltpu.get_barrier_semaphore()

    def greet(k, c):
        pl.semaphore_signal(
            barrier,
            inc=1,
            device_id=(lax.rem(w + k % wide, wide), lax.rem(q + k // wide, NARROW)),
            device_id_type=MESH,
        )
        return c

    everyone = NARROW * wide - 1
    lax.fori_loop(1, everyone + 1, greet, 0, unroll=wide <= 16)

    load_count.wait()
    real = count_ref[0]
    row = lax.broadcasted_iota(jnp.int32, (chunk, 128), 0)
    for r in range(CHUNKS):
        at = row + r * chunk
        image = jnp.where(
            at < nview,
            (at % views_block) // VIEWS_EACH,
            ((at - nview) % crops_block) // CROPS_EACH,
        )
        alive = jnp.where((image < real) & (at < rows), 1.0, 0.0)
        mask[part(r)] = alive.astype(F32)
    tail = pl.ds(rows, padded - rows)
    x[tail] = jnp.zeros((padded - rows, own), BF16)
    xs[1, tail] = jnp.zeros((padded - rows, own), BF16)
    cot[tail] = jnp.zeros((padded - rows, own), BF16)
    taps[tail] = jnp.zeros((padded - rows, len(TAPS) * inner), BF16)
    view_pad[...] = jnp.zeros(view_pad.shape, BF16)
    crop_pad[...] = jnp.zeros(crop_pad.shape, BF16)
    my_count = real.astype(F32) * float(
        VIEWS_EACH * views_side**2 + CROPS_EACH * crops_side**2
    )

    pl.semaphore_wait(barrier, everyone)

    far_reduce = [
        links.send(w_reduce.at[own_rows(1 + 2 * k), :], wr.at[k, :, lanes(1)], far) for k in range(2)
    ]
    near_x = [
        links.send(views, xs.at[1, pl.ds(0, nview)], near),
        links.send(crops, xs.at[1, pl.ds(nview, rows - nview)], near),
    ]
    near_reduce = [links.send(w_reduce.at[own_rows(2), :], wr.at[0, :, lanes(2)], near)]

    def exchange(k, tile, everywhere=False):
        board, me, n = (stat_all, q * wide + w, everyone) if everywhere else (stat, w, wide - 1)
        sem = k + 4 if everywhere else k
        board[k, me] = tile

        def put(step, c):
            pltpu.make_async_remote_copy(
                board.at[k, me],
                board.at[k, me],
                stat_send.at[sem],
                stat_recv.at[sem],
                device_id=(lax.rem(w + step % wide, wide), lax.rem(q + step // wide, NARROW)),
                device_id_type=MESH,
            ).start()
            return c

        lax.fori_loop(1, n + 1, put, 0, unroll=wide <= 16)
        several = board.at[k, pl.ds(0, n)]
        pending.append(pltpu.make_async_copy(several, several, stat_send.at[sem]))
        return pltpu.make_async_copy(several, several, stat_recv.at[sem])

    pending = []

    def moments(ref):
        size = ref.shape[1]
        zero = jnp.zeros((8, size), F32)
        sums = total(loop(lambda at, c: c + fold(ref[at, :] * wider(mask[at, :], size)), zero))
        center = sums / my_count
        squares = total(
            loop(
                lambda at, c: c + fold(jnp.square(ref[at, :] - center) * wider(mask[at, :], size)),
                zero,
            )
        )
        return sums, squares

    def rows_of(k, lo, n):
        return stat[k, :, pl.ds(lo, n), :]

    def combine(sums, squares, counts, pixels):
        center = jnp.sum(sums, axis=0) / pixels
        spread = (
            jnp.sum(squares + counts * jnp.square(sums / counts - center[None]), axis=0) / pixels
        )
        return center, lax.rsqrt(spread + EPS)

    def reduce_scatter(k, give, hold, target, after, meanwhile=lambda: None):
        first, second = [], []
        for copy in in_use.pop(k, ()):
            links.settle(copy)
        for r in range(CHUNKS):
            near_out[k, part(r)] = give(r).astype(BF16)
            first.append(links.send(near_out.at[k, part(r)], near_in.at[k, part(r)], near))
        for r in range(CHUNKS):
            keep[part(r)] = hold(r)
            first[r].wait_recv()
            far_out[k, part(r)] = (
                keep[part(r), lanes(1)] + near_in[k, part(r), lanes(1)].astype(F32)
            ).astype(BF16)
            second.append(links.send(far_out.at[k, part(r)], far_in.at[k, part(r)], far))
            target[part(r)] = keep[part(r), lanes(0)] + near_in[k, part(r), lanes(0)].astype(F32)
        meanwhile()
        for r in range(CHUNKS):
            second[r].wait_recv()
            target[part(r)] = target[part(r)] + far_in[k, part(r)].astype(F32)
            after(r)
        in_use[k] = first + second

    in_use = {}

    class Gather:
        def __init__(self, ref):
            self.ref, self.across, self.onward = ref, [], []

        def send(self, r):
            ref = self.ref
            self.across.append(links.send(ref.at[part(r), lanes(0)], ref.at[part(r), lanes(1)], far))
            if r == CHUNKS - 1:
                self.straight = links.send(ref.at[:, lanes(0)], ref.at[:, lanes(2)], near)

        def hand_on(self, count):
            for r in range(len(self.onward), min(len(self.onward) + count, CHUNKS)):
                self.across[r].wait_recv()
                self.onward.append(
                    links.send(self.ref.at[part(r), lanes(1)], self.ref.at[part(r), lanes(3)], near)
                )

        def near_end(self):
            if self.straight is not None:
                self.straight.wait_recv()
                self.straight = None

        def end(self, use):
            for r in range(CHUNKS + 1):
                self.hand_on(1)
                if r > 0:
                    self.near_end()
                    self.onward[r - 1].wait_recv()
                    use(r - 1)

    across_x, onward_x, shared = [], [], [0]

    def share_x(eighths):
        low = shared[0]
        shared[0] = low + eighths
        first, last = (padded // ROW_TILE * k // 8 * ROW_TILE for k in (low, shared[0]))
        at = pl.ds(first, last - first)
        across_x.append((at, links.send(x.at[at], xs.at[0, at], far, "x")))

    def share_end():
        while len(onward_x) < len(across_x):
            at, copy = across_x[len(onward_x)]
            copy.wait_recv()
            onward_x.append(links.send(xs.at[0, at], xs.at[2, at], near, "x"))

    group_start = w - lax.rem(w, group)

    def block_of(bits, index):
        return sum((index // bit) % 2 * (group // 2 >> k) for k, bit in enumerate(bits))

    def beyond(value, spare):
        bit, at = group, group
        while bit < wide:
            spare[at] = value.astype(BF16)
            copy = links.send(spare.at[at], spare.at[at + 1], (flip(w, bit), q))
            copy.wait_recv()
            value = spare[at].astype(F32) + spare[at + 1].astype(F32)
            bit, at = bit * 2, at + 2
        return value

    def add_block(parts, at, came):
        parts[at] = (parts[at].astype(F32) + came.astype(F32)).astype(BF16)

    def halved(kind, bits, parts, came, finish):
        low, size = 0, group
        for bit in bits:
            size //= 2
            side = (w // bit) % 2
            box = pl.ds(group - 2 * size, size)
            copy = links.send(
                parts.at[pl.ds(low + (1 - side) * size, size)], came.at[box], (flip(w, bit), q), kind
            )
            yield
            copy.wait_recv()
            low = low + side * size
            if size > 1:
                for k in range(size):
                    add_block(parts, low + k, came[group - 2 * size + k])
        value = parts[low].astype(F32) + came[group - 2].astype(F32)
        yield from finish(beyond(value, came))

    def doubled(kind, bits, out):
        low, size = block_of(bits, w), 1
        for bit in reversed(bits):
            box = pl.ds(low, size)
            copy = links.send(out.at[box], out.at[box], (flip(w, bit), q), kind)
            yield
            copy.wait_recv()
            low = low - (w // bit) % 2 * size
            size *= 2

    def group_peers(among):
        for k in range(1, len(among)):
            place = (lax.rem(w, group) + k * (among[1] - among[0])) % group
            yield (group_start + place, q), place

    def halved_then_direct(kind, bits, parts, came, finish):
        quads = group // 2
        side = (w // bits[0]) % 2
        copy = links.send(
            parts.at[pl.ds((1 - side) * quads, quads)], came.at[pl.ds(0, quads)], (flip(w, bits[0]), q), kind
        )
        yield
        copy.wait_recv()
        for k in range(quads):
            add_block(parts, side * quads + k, came[k])
        mine = block_of(bits, w)
        copy = Group(
            links,
            [
                (parts.at[block_of(bits, place)], came.at[quads + mine % quads], peer)
                for peer, place in group_peers(range(0, group, 2))
            ],
            came.at[pl.ds(quads, quads - 1)],
            kind,
        )
        came[quads + mine % quads] = parts[mine]
        yield
        copy.wait_recv()
        value = jnp.sum(came[pl.ds(quads, quads)].astype(F32), axis=0)
        yield from finish(beyond(value, came))

    def direct_then_doubled(kind, bits, out):
        mine = block_of(bits, w)
        copy = Group(
            links,
            [(out.at[mine], out.at[mine], peer) for peer, _ in group_peers(range(0, group, 2))],
            out.at[pl.ds(0, group // 2 - 1)],
            kind,
        )
        yield
        copy.wait_recv()
        box = pl.ds((w // bits[0]) % 2 * (group // 2), group // 2)
        copy = links.send(out.at[box], out.at[box], (flip(w, bits[0]), q), kind)
        yield
        copy.wait_recv()

    def direct(kind, bits, parts, came, finish):
        mine = block_of(bits, w)
        copy = Group(
            links,
            [
                (parts.at[block_of(bits, place)], came.at[mine], peer)
                for peer, place in group_peers(range(group))
            ],
            came.at[pl.ds(0, group - 1)],
            kind,
        )
        came[mine] = parts[mine]
        yield
        copy.wait_recv()
        value = jnp.sum(came[pl.ds(0, group)].astype(F32), axis=0)
        yield from finish(beyond(value, came))

    ways = {
        "h": ((1, 2, 4), halved, doubled),
        "z": ((2, 1, 4), halved, doubled),
        "q": ((1, 2, 4), halved_then_direct, direct_then_doubled),
        "d": ((1, 2, 4), direct, doubled),
    }

    def all_reduced(kind, way, parts, came, out, keep_sum, between=lambda: iter(())):
        bits, there, back = ways[way]

        def finish(value):
            keep_sum(block_of(bits, w), value)
            yield from between()
            yield from back(kind, bits, out)

        return there(kind, bits, parts, came, finish)

    tasks = {}

    def begin(name, task):
        tasks[name] = task
        next(task)

    def advance(*names):
        for name in names:
            if name in tasks and next(tasks[name], "end") == "end":
                del tasks[name]

    for copy in load_reduce + load_x:
        copy.wait()
    for copy in near_x:
        copy.wait_recv()

    def reduce_part(r, p):
        return dot(x[part(r)], wr[0, :, lanes(p)]) + dot(xs[1, part(r)], wr[1, :, lanes(p)])

    for r in range(CHUNKS):
        red[part(r)] = reduce_part(r, 0)
    for copy in far_reduce:
        copy.wait_recv()
    came = []
    for r in range(CHUNKS):
        far_out[0, part(r)] = reduce_part(r, 1).astype(BF16)
        came.append(links.send(far_out.at[0, part(r)], far_in.at[0, part(r)], far))
    near_reduce.append(links.send(wr.at[1, :, lanes(1)], wr.at[0, :, lanes(3)], near))
    for r in range(CHUNKS):
        came[r].wait_recv()
        red[part(r)] = red[part(r)] + far_in[0, part(r)].astype(F32)
    in_use[0] = came
    sent_expand = {
        p: links.send(
            w_expand.at[:, dyn_lanes(narrow_peer(p), own)], we.at[lanes(p), :], (w, narrow_peer(p))
        )
        for p in (3, 1, 2)
    }
    share_x(1)
    sums, squares = moments(red)
    arrived = exchange(
        0,
        jnp.concatenate(
            [sums, squares, jnp.full((1, inner), my_count, F32), jnp.zeros((5, inner), F32)], axis=0
        ),
    )
    for copy in load_spatial:
        copy.wait()
    arrived.wait()
    counts = rows_of(0, 2, 1)
    pixels = jnp.sum(counts, axis=0)
    center1, inverse1 = combine(rows_of(0, 0, 1), rows_of(0, 1, 1), counts, pixels)

    def normed(v, center, inverse, gain, shift):
        standard = (v - center) * inverse
        return standard, gain * standard + shift

    for copy in load_vectors:
        copy.wait()
    g1, s1, g2, s2 = (inner_vectors[k] for k in range(4))
    g3, s3 = (outer_vectors[k] for k in range(2))
    grids = (
        (views_side, views_block, 0, view_pad),
        (crops_side, crops_block, nview, crop_pad),
    )
    for side, block, lead, pad in grids:
        line = side * block
        for h in range(side):
            _, v = normed(red[pl.ds(lead + h * line, line)], center1, inverse1, g1, s1)
            pad[pl.ds(((h + 1) * (side + 2) + 1) * block, line)] = (v * logistic(v)).astype(BF16)
    for side, block, lead, pad in grids:
        line = side * block
        for t, (i, j) in enumerate(TAPS):
            for h in range(side):
                taps[pl.ds(lead + h * line, line), lanes(t)] = pad[
                    pl.ds(((h + i) * (side + 2) + j) * block, line)
                ]

    mixes = Gather(mall)
    reference = []

    def send_mix(r):
        if r == 0:
            alive = mask[part(0)]
            reference.append(total(fold(mix[part(0)] * alive)) / total(fold(alive)))
        mall[part(r), lanes(0)] = (mix[part(r)] - reference[0]).astype(BF16)
        mixes.send(r)

    reduce_scatter(
        1,
        lambda r: dot(taps[part(r)], ws[:, pl.ds(half, half)]),
        lambda r: dot(taps[part(r)], ws[:, pl.ds(0, half)]),
        mix,
        send_mix,
    )
    sums, squares = moments(mix)
    arrived = exchange(
        0,
        jnp.concatenate([sums, squares, g2, s2, reference[0], jnp.zeros((3, inner), F32)], axis=0),
        True,
    )
    own_expand.wait()
    for p in (2, 3, 1):
        sent_expand[p].wait_recv()
    mixes.hand_on(CHUNKS)
    arrived.wait()

    def board_rows(k, p, lo, n):
        return stat_all[k, pl.ds(narrow_peer(p) * wide, wide), pl.ds(lo, n), :]

    def board_row(k, p, lo):
        return stat_all[k, narrow_peer(p) * wide + w, pl.ds(lo, 1), :]

    blocks = [
        combine(board_rows(0, p, 0, 1), board_rows(0, p, 1, 1), counts, pixels) for p in range(NARROW)
    ]
    center2, inverse2 = blocks[0]
    inverse_all = jnp.concatenate([b[1] for b in blocks], axis=1)
    offset_all = jnp.concatenate(
        [board_row(0, p, 4) - blocks[p][0] for p in range(NARROW)], axis=1
    )
    gain_all = jnp.concatenate([board_row(0, p, 2) for p in range(NARROW)], axis=1)
    shift_all = jnp.concatenate([board_row(0, p, 3) for p in range(NARROW)], axis=1)
    scale_all = gain_all * inverse_all
    constant_all = scale_all * offset_all + shift_all

    def expand(r):
        v = mall[part(r), :].astype(F32) * scale_all + constant_all
        ht[part(r), :] = (v * logistic(v)).astype(BF16)
        ex[part(r), :] = dot(ht[part(r)], we[...])

    mixes.end(expand)
    share_end()
    share_x(5)
    sums, squares = moments(ex)
    groups = own // 128

    def tiles(*values):
        return jnp.concatenate(
            [v[:, 128 * k : 128 * k + 128] for v in values for k in range(groups)], axis=0
        )

    arrived = exchange(1, tiles(sums, squares))
    for copy in load_cot:
        copy.wait()
    arrived.wait()
    center3, inverse3 = combine(
        rows_of(1, 0, groups), rows_of(1, groups, groups), counts, pixels
    )
    center3, inverse3 = flat(center3), flat(inverse3)

    def third(at, c):
        standard, v = normed(ex[at, :], center3, inverse3, g3, s3)
        v = v + x[at].astype(F32)
        s = logistic(v)
        alive = wider(mask[at], own)
        res[at] = (alive * (v * s)).astype(BF16)
        g = cot[at].astype(F32) * alive * (s * (1.0 + v * (1.0 - s)))
        b3[at] = g
        return c[0] + fold(g), c[1] + fold(g * standard)

    zero = jnp.zeros((8, own), F32)
    shift_sum, gain_sum = loop(third, (zero, zero))
    arrived = exchange(2, tiles(total(gain_sum), total(shift_sum)))
    results = [
        local(res.at[pl.ds(0, nview)], view_out), local(res.at[pl.ds(nview, rows - nview)], crop_out)
    ]
    arrived.wait()
    both = jnp.sum(stat[2], axis=0)
    large[...] = both
    results.append(local(large, large_out))

    def back_terms(gain_grad, shift_grad, offset, inverse, gain, n):
        scale = gain * inverse
        slope = scale * inverse * (gain_grad / n)
        return scale, scale * (shift_grad / n) + slope * offset, slope

    scale3, base3, slope3 = back_terms(
        flat(both[:groups]), flat(both[groups:]), -center3, inverse3, g3, wider(pixels, own)
    )

    def third_back(at, c):
        ge[at] = (
            scale3 * b3[at] - wider(mask[at], own) * (base3 + slope3 * ex[at, :])
        ).astype(BF16)
        return c

    loop(third_back, 0)

    size_e = inner // group

    def keep_e(mine, value):
        stage_e[...] = value.astype(BF16)
        out_e[mine, :, dyn_lanes(q, own)] = stage_e[0]

    def hand_on_e():
        mine = block_of(ways[WAYS["e"]][0], w)
        got = [
            links.send(
                stage_e.at[p], out_e.at[mine, :, dyn_lanes(q, own)], (w, narrow_peer(p)), "e"
            )
            for p in range(1, NARROW)
        ]
        yield
        for copy in got:
            copy.wait_recv()

    def expand_gradient():
        value = dot_left(ht[...], ge[...]).astype(BF16)
        for p in range(NARROW):
            part_e[:, p] = value[inner * p : inner * (p + 1)].reshape(group, size_e, own)
        begin("e", all_reduced("e", WAYS["e"], part_e, came_e, out_e, keep_e, hand_on_e))
        share_end()

    def slope_of(v):
        s = logistic(v)
        return s * (1.0 + v * (1.0 - s))

    grads = Gather(gall)
    back_sums = [jnp.zeros((8, inner), F32)] * 2

    def second_back(r):
        standard, v = normed(mix[part(r)], center2, inverse2, g2, s2)
        g = back[part(r)] * slope_of(v)
        gall[part(r), lanes(0)] = g.astype(BF16)
        grads.send(r)
        back_sums[0] = back_sums[0] + fold(g * standard)
        back_sums[1] = back_sums[1] + fold(g)

    reduce_scatter(
        0,
        lambda r: dot_right(ge[part(r)], we[pl.ds(half, half), :]),
        lambda r: dot_right(ge[part(r)], we[pl.ds(0, half), :]),
        back,
        second_back,
        expand_gradient,
    )
    arrived = exchange(
        1,
        jnp.concatenate([*map(total, back_sums), jnp.zeros((6, inner), F32)], axis=0),
        True,
    )
    grads.hand_on(CHUNKS)
    arrived.wait()
    sums = [jnp.sum(board_rows(1, p, 0, 2), axis=0) for p in range(NARROW)]
    small[pl.ds(8, 8)] = jnp.concatenate([sums[0], jnp.zeros((6, inner), F32)], axis=0)
    scale2, base2, slope2 = back_terms(
        jnp.concatenate([v[0:1] for v in sums], axis=1),
        jnp.concatenate([v[1:2] for v in sums], axis=1),
        offset_all,
        inverse_all,
        gain_all,
        wider(pixels, full),
    )

    def columns(v, p, n=1):
        return v[:, inner * p : inner * (p + n)]

    def grad_mixed(at, some):
        for p in some:
            gm[at, lanes(p)] = (
                columns(scale2, p) * gall[at, lanes(p)].astype(F32)
                - mask[at] * (columns(base2, p) + columns(slope2, p) * mall[at, lanes(p)].astype(F32))
            ).astype(BF16)
        return 0

    def spatial_gradient(*some):
        value = dot_left(taps[...], jnp.concatenate([gm[:, lanes(p)] for p in some], axis=1))
        for k, p in enumerate(some):
            part_s[p] = columns(value, k).astype(BF16).reshape(part_s.shape[1:])

            def keep_s(mine, value, p=p):
                out_s[p, mine] = value.astype(BF16)

            name = "s%d" % p
            begin(
                name, all_reduced("s", WAYS[name], part_s.at[p], came_s.at[p], out_s.at[p], keep_s)
            )

    grads.near_end()
    loop(lambda at, c: grad_mixed(at, (0, 2)), 0)
    spatial_gradient(0, 2)
    advance("e")

    def spatial_back(r):
        grad_mixed(part(r), (1, 3))
        tp[part(r)] = dot_right(gm[part(r)], ws[...])

    grads.end(spatial_back)
    spatial_gradient(1, 3)
    share_x(2)
    shift_sum = gain_sum = jnp.zeros((8, inner), F32)
    for side, block, lead, pad in grids:
        line = side * block
        for h in range(side):
            g = None
            for t, (i, j) in enumerate(TAPS):
                source = h - (i - 1)
                if not 0 <= source < side:
                    continue
                first = lead + source * line
                if j == 1:
                    term = tp[pl.ds(first, line), lanes(t)]
                elif j == 0:
                    term = jnp.concatenate(
                        [tp[pl.ds(first + block, line - block), lanes(t)], jnp.zeros((block, inner), F32)]
                    )
                else:
                    term = jnp.concatenate(
                        [jnp.zeros((block, inner), F32), tp[pl.ds(first, line - block), lanes(t)]]
                    )
                g = term if g is None else g + term
            at = pl.ds(lead + h * line, line)
            standard, v = normed(red[at], center1, inverse1, g1, s1)
            g = g * slope_of(v)
            back[at] = g
            shift_sum = shift_sum + fold(g)
            gain_sum = gain_sum + fold(g * standard)
    back[tail] = jnp.zeros((padded - rows, inner), F32)
    arrived = exchange(
        3, jnp.concatenate([total(gain_sum), total(shift_sum), jnp.zeros((6, inner), F32)], axis=0)
    )

    advance(*ORDER[0])
    arrived.wait()
    both = jnp.sum(stat[3], axis=0)
    small[pl.ds(0, 8)] = both
    results.append(local(small, small_out))
    scale1, base1, slope1 = back_terms(both[0:1], both[1:2], -center1, inverse1, g1, pixels)

    def first_grad(at, c):
        gr[at, lanes(0)] = (scale1 * back[at] - mask[at] * (base1 + slope1 * red[at])).astype(BF16)
        return c

    loop(first_grad, 0)
    ends = Gather(gr)
    for r in range(CHUNKS):
        ends.send(r)

    per = own // 4

    def reduce_gradient(k):
        for p in (k, 2 + k):
            source = x[...] if p == 0 else xs[p - 1]
            value = dot_left(gr[:, lanes(0)], source).astype(BF16)
            for m in range(4):
                part_r[k, narrow_peer(p) % 2 * 4 + m] = value[:, per * m : per * m + per]

        def keep_r(mine, value):
            out_r[k, mine] = value.T.astype(BF16)

        name = "r%d" % k
        begin(name, all_reduced("r", WAYS[name], part_r.at[k], came_r.at[k], out_r.at[k], keep_r))

    reduce_gradient(0)
    advance(*ORDER[1])
    share_end()
    for copy in onward_x:
        copy.wait_recv()
    reduce_gradient(1)
    advance(*ORDER[2])

    def input_gradient(r):
        dx[part(r)] = (dot_right(gr[part(r)], wr[0]) + b3[part(r)]).astype(BF16)

    for copy in near_reduce:
        copy.wait_recv()
    ends.end(input_gradient)
    results += [
        local(dx.at[pl.ds(0, nview)], view_grad), local(dx.at[pl.ds(nview, rows - nview)], crop_grad)
    ]
    advance(*ORDER[3])
    results.append(local(out_e, expand_out))
    while tasks:
        advance(*list(tasks))
    results += [
        local(out_s.at[p], spatial_out.at[:, :, dyn_lanes(narrow_peer(p))]) for p in range(NARROW)
    ]
    chip = q // 2
    results += [local(out_r.at[0], reduce_out.at[chip]), local(out_r.at[1], reduce_out.at[1 - chip])]
    for copy in links.sent:
        copy.wait_send()
    for copy in pending:
        copy.wait()
    for copy in results:
        copy.wait()


def rows_first(a):
    return a.transpose(1, 2, 0, 3).reshape(-1, a.shape[3])


def images_first(a, like):
    n, h, w, c = like.shape
    return a.reshape(h, w, n, c).transpose(2, 0, 1, 3)


def per_device(wide, *args):
    (
        views, crops, image_count, w_reduce, w_spatial, w_expand,
        gain_one, shift_one, gain_two, shift_two, gain_three, shift_three, view_cot, crop_cot,
    ) = args
    own = views.shape[3]
    inner = w_reduce.shape[1]
    full = NARROW * inner
    nview = views.shape[0] * views.shape[1] * views.shape[2]
    ncrop = crops.shape[0] * crops.shape[1] * crops.shape[2]
    rows = nview + ncrop
    quantum = CHUNKS * ROW_TILE
    padded = -(-rows // quantum) * quantum
    dims = (views.shape[1], views.shape[0], crops.shape[1], crops.shape[0], rows, padded)
    ntaps = len(TAPS) * inner
    group = min(wide, GROUP)
    levels = (wide // group).bit_length() - 1
    slots = group + 2 * levels
    copies = COPIES + len(WAYS) * levels
    vm = pltpu.VMEM
    hbm = pl.BlockSpec(memory_space=pltpu.HBM)
    outs = pl.pallas_call(
        functools.partial(kernel, wide, dims),
        name="block",
        out_shape=(
            jax.ShapeDtypeStruct((nview, own), BF16),
            jax.ShapeDtypeStruct((ncrop, own), BF16),
            jax.ShapeDtypeStruct((nview, own), BF16),
            jax.ShapeDtypeStruct((ncrop, own), BF16),
            jax.ShapeDtypeStruct((2, group, own // 4, inner), BF16),
            jax.ShapeDtypeStruct((group, ntaps // group, full), BF16),
            jax.ShapeDtypeStruct((group, inner // group, NARROW * own), BF16),
            jax.ShapeDtypeStruct((16, inner), F32),
            jax.ShapeDtypeStruct((8, 128), F32),
        ),
        in_specs=[hbm] * 14,
        out_specs=[hbm] * 9,
        scratch_shapes=[
            pltpu.SMEM((1,), jnp.int32),
            vm((4, 1, inner), F32),
            vm((2, 1, own), F32),
            vm((16, inner), F32),
            vm((8, 128), F32),
            vm((padded, own), BF16),
            vm((NARROW - 1, padded, own), BF16),
            vm((padded, own), BF16),
            vm((2, own, full), BF16),
            vm((ntaps, full), BF16),
            vm((full, own), BF16),
            vm((padded, 128), F32),
            vm((4, wide, 8, 128), F32),
            vm((2, NARROW * wide, 8, 128), F32),
            vm((padded, 2 * inner), F32),
            vm((2, padded, 2 * inner), BF16),
            vm((2, padded, 2 * inner), BF16),
            vm((2, padded, inner), BF16),
            vm((2, padded, inner), BF16),
            vm((padded, inner), F32),
            vm((padded, inner), F32),
            vm((padded, inner), F32),
            vm(((dims[0] + 2) ** 2 * dims[1], inner), BF16),
            vm(((dims[2] + 2) ** 2 * dims[3], inner), BF16),
            vm((padded, ntaps), BF16),
            vm((padded, full), BF16),
            vm((padded, full), BF16),
            vm((padded, own), F32),
            vm((padded, own), BF16),
            vm((padded, full), BF16),
            vm((padded, full), BF16),
            vm((padded, ntaps), F32),
            vm((padded, full), BF16),
            vm((padded, own), BF16),
            vm((padded, own), BF16),
            vm((group, inner // group, NARROW * own), BF16),
            vm((NARROW, group, ntaps // group, inner), BF16),
            vm((2, group, own // 4, inner), BF16),
            vm((NARROW, inner // group, own), BF16),
            vm((group, NARROW, inner // group, own), BF16),
            vm((slots, NARROW, inner // group, own), BF16),
            vm((NARROW, group, ntaps // group, inner), BF16),
            vm((NARROW, slots, ntaps // group, inner), BF16),
            vm((2, group, inner, own // 4), BF16),
            vm((2, slots, inner, own // 4), BF16),
            pltpu.SemaphoreType.DMA((copies,)),
            pltpu.SemaphoreType.DMA((copies,)),
            pltpu.SemaphoreType.DMA((6,)),
            pltpu.SemaphoreType.DMA((6,)),
            pltpu.SemaphoreType.DMA((31,)),
        ],
        compiler_params=pltpu.CompilerParams(
            collective_id=0, has_side_effects=True, vmem_limit_bytes=62 * 2**20
        ),
    )(
        image_count,
        rows_first(views),
        rows_first(crops),
        rows_first(view_cot),
        rows_first(crop_cot),
        w_reduce,
        w_spatial.reshape(ntaps, full),
        w_expand,
        *(a.reshape(1, -1) for a in (gain_one, shift_one, gain_two, shift_two, gain_three, shift_three)),
    )
    shapes = [(outs[k].shape, BF16) for k in range(4)]
    shapes += [((NARROW * own, inner), F32), ((ntaps, full), F32), ((inner, NARROW * own), F32)]
    shapes += [((inner,), F32)] * 4 + [((own,), F32)] * 2
    outs = pl.pallas_call(
        release,
        name="release",
        out_shape=tuple(jax.ShapeDtypeStruct(*shape) for shape in shapes),
        in_specs=[hbm] * len(outs),
        out_specs=[hbm] * len(shapes),
        scratch_shapes=[
            vm(outs[4].shape, BF16),
            vm(outs[5].shape, BF16),
            vm(outs[6].shape, BF16),
            vm(shapes[4][0], F32),
            vm(shapes[5][0], F32),
            vm(shapes[6][0], F32),
            *[vm(outs[k].shape, BF16) for k in range(4)],
            vm(outs[7].shape, F32),
            vm(outs[8].shape, F32),
            pltpu.SemaphoreType.DMA((34,)),
        ],
        compiler_params=pltpu.CompilerParams(vmem_limit_bytes=62 * 2**20),
    )(*outs)
    images = (views, crops, views, crops)
    return (
        *(images_first(a, like) for a, like in zip(outs[:4], images)),
        outs[4],
        outs[5].reshape(w_spatial.shape),
        *outs[6:],
    )


def release(*refs):
    images, (reduce_in, spatial_in, expand_in, small, large) = refs[:4], refs[4:9]
    outs, (reduce_v, spatial_v, expand_v, reduce_f, spatial_f, expand_f, *staged, small_v, large_v, sems) = (
        refs[9:22],
        refs[22:],
    )
    used = [0]

    def copy(source, target):
        started = pltpu.make_async_copy(source, target, sems.at[used[0]])
        used[0] += 1
        started.start()
        return started

    loads = [copy(spatial_in, spatial_v), copy(expand_in, expand_v), copy(reduce_in, reduce_v)]
    arrivals = [copy(a, b) for a, b in zip(images, staged)]
    small_in, large_in = copy(small, small_v), copy(large, large_v)
    waits = []
    for started, a, b in zip(arrivals, staged, outs[:4]):
        started.wait()
        waits.append(copy(a, b))
    small_in.wait()
    large_in.wait()
    for k, row in enumerate((0, 1, 8, 9)):
        waits.append(copy(small_v.at[row], outs[7 + k]))
    groups = large.shape[0] // 2
    for k in range(2):
        for g in range(groups):
            waits.append(copy(large_v.at[k * groups + g], outs[11 + k].at[pl.ds(128 * g, 128)]))
    loads[0].wait()
    spatial_f[...] = spatial_v[...].astype(F32).reshape(spatial_f.shape)
    waits.append(copy(spatial_f, outs[5]))
    loads[1].wait()
    expand_f[...] = expand_v[...].astype(F32).reshape(expand_f.shape)
    waits.append(copy(expand_f, outs[6]))
    loads[2].wait()
    blocks, rows = reduce_v.shape[1:3]
    for k in range(2):
        for c in range(blocks):
            reduce_f[pl.ds((k * blocks + c) * rows, rows)] = reduce_v[k, c].astype(F32)
    waits.append(copy(reduce_f, outs[4]))
    for started in waits:
        started.wait()


def solution(mesh):
    wide = mesh.shape["wide"]
    image = P("wide", None, None, "narrow")
    vector = P("narrow")
    return jax.shard_map(
        functools.partial(per_device, wide),
        mesh=mesh,
        in_specs=(
            image, image, P("wide"), P(None, "narrow"), P(None, None, "narrow", None), P("narrow", None),
            vector, vector, vector, vector, vector, vector, image, image,
        ),
        out_specs=(
            image, image, image, image, P(None, "narrow"), P(None, None, "narrow", None),
            P("narrow", None), vector, vector, vector, vector, vector, vector,
        ),
        check_vma=False,
    )
```

```python
import functools

import jax
import jax.numpy as jnp
from jax import lax
from jax.experimental import pallas as pl
from jax.experimental.pallas import tpu as pltpu
from jax.sharding import PartitionSpec as P

MESH = pl.DeviceIdType.MESH
EPS = 1e-05
ORDER = (
    ('e', 's0', 's2', 'e'),
    ('s2', 's1'),
    ('s3', 's2', 's0', 'e'),
    ('r0', 'r1', 's3', 's1', 's0', 's2', 's3', 'e', 'r0', 'r1', 's2', 's0', 's1', 's3', 'e', 's3', 'r0', 's1', 's2', 'r1', 's3', 'r0', 'r1'),
)
WAYS = {"e": "d", "s0": "q", "s1": "q", "s2": "z", "s3": "z", "r0": "q", "r1": "q"}
NARROW = 4
CHUNKS = 2
COPIES = 75
ROW_TILE = 16
GROUP = 8
VIEWS_EACH = 2
CROPS_EACH = 4
TAPS = [(i, j) for i in range(3) for j in range(3)]
XOR = (0, 2, 1, 3)
POS = (0, 2, 1, 3)
F32 = jnp.float32
BF16 = jnp.bfloat16


def dot(a, b):
    return jnp.dot(a, b, preferred_element_type=F32)


def dot_right(a, b):
    return lax.dot_general(a, b, (((1,), (1,)), ((), ())), preferred_element_type=F32)


def dot_left(a, b):
    return lax.dot_general(a, b, (((0,), (0,)), ((), ())), preferred_element_type=F32)


def logistic(v):
    return 0.5 + 0.5 * jnp.tanh(0.5 * v)


def flip(index, bit):
    return index + bit - 2 * bit * ((index // bit) % 2)


def wider(tile, lanes):
    return jnp.concatenate([tile] * (lanes // 128), axis=1) if lanes > 128 else tile


def fold(v):
    return jnp.sum(v.reshape(v.shape[0] // 8, 8, v.shape[1]), axis=0)


def total(v):
    return jnp.sum(v, axis=0, keepdims=True)


def flat(v):
    return jnp.concatenate([v[k : k + 1] for k in range(v.shape[0])], axis=1)


class Links:
    def __init__(self, send_sems, recv_sems):
        self.send_sems, self.recv_sems, self.used, self.sent = send_sems, recv_sems, 0, []

    def send(self, source, target, peer, background=""):
        copy = pltpu.make_async_remote_copy(
            source,
            target,
            self.send_sems.at[self.used],
            self.recv_sems.at[self.used],
            device_id=peer,
            device_id_type=MESH,
        )
        self.used += 1
        copy.start()
        self.sent.append(copy)
        return copy

    def settle(self, copy):
        if any(other is copy for other in self.sent):
            copy.wait_send()
            self.sent = [other for other in self.sent if other is not copy]


class Group:
    def __init__(self, links, copies, total, kind):
        self.live = True
        send_sem, recv_sem = links.send_sems.at[links.used], links.recv_sems.at[links.used]
        links.used += 1
        for source, target, peer in copies:
            copy = pltpu.make_async_remote_copy(
                source, target, send_sem, recv_sem, device_id=peer, device_id_type=MESH
            )
            copy.start()
        self.arrival = pltpu.make_async_copy(total, total, recv_sem)
        self.departure = pltpu.make_async_copy(total, total, send_sem)
        links.sent.append(self)

    def wait_recv(self):
        if self.live:
            self.arrival.wait()

    def wait_send(self):
        self.departure.wait()


def kernel(wide, dims, *refs):
    views_side, views_block, crops_side, crops_block, rows, padded = dims
    (
        image_count, views, crops, view_cot, crop_cot, w_reduce, w_spatial, w_expand,
        gain1, shift1, gain2, shift2, gain3, shift3,
        view_out, crop_out, view_grad, crop_grad, reduce_out, spatial_out, expand_out, small_out, large_out,
        count_ref, inner_vectors, outer_vectors, small, large,
        x, xs, cot, wr, ws, we, mask, stat, stat_all, keep, near_out, near_in, far_out, far_in,
        red, mix, back, view_pad, crop_pad, taps, mall, ht, b3, ge, gall, gm, tp, gr, res, dx,
        out_e, out_s, out_r, stage_e, part_e, came_e,
        part_s, came_s, part_r, came_r,
        send_sems, recv_sems, stat_send, stat_recv, local_sems,
    ) = refs
    w = lax.axis_index("wide")
    q = lax.axis_index("narrow")
    near, far = (w, flip(q, 1)), (w, flip(q, 2))
    inner = w_reduce.shape[1]
    own = x.shape[1]
    full = NARROW * inner
    chunk = padded // CHUNKS
    half = 2 * inner
    nview = views.shape[0]
    group = min(wide, GROUP)
    ex = tp.at[:, pl.ds(0, own)]
    links = Links(send_sems, recv_sems)
    slot = [0]

    def local(source, target):
        copy = pltpu.make_async_copy(source, target, local_sems.at[slot[0]])
        slot[0] += 1
        copy.start()
        return copy

    def part(r):
        return pl.ds(r * chunk, chunk)

    def lanes(p, width=inner):
        return pl.ds(p * width, width)

    def dyn_lanes(p, width=inner):
        return pl.ds(pl.multiple_of(p * width, width), width)

    def narrow_peer(p):
        i = q
        if XOR[p] & 1:
            i = flip(i, 1)
        if XOR[p] & 2:
            i = flip(i, 2)
        return i

    def loop(body, init):
        return lax.fori_loop(
            0, CHUNKS, lambda i, c: body(pl.ds(pl.multiple_of(i * chunk, chunk), chunk), c), init
        )

    def own_rows(p):
        return pl.ds(pl.multiple_of(narrow_peer(p) * own, own), own)

    load_count = local(image_count, count_ref)
    load_vectors = [local(ref, inner_vectors.at[k]) for k, ref in enumerate((gain1, shift1, gain2, shift2))]
    load_vectors += [local(ref, outer_vectors.at[k]) for k, ref in enumerate((gain3, shift3))]
    load_reduce = [local(w_reduce.at[own_rows(2 * k), :], wr.at[k, :, lanes(0)]) for k in range(2)]
    load_x = [local(views, x.at[pl.ds(0, nview)]), local(crops, x.at[pl.ds(nview, rows - nview)])]
    load_spatial = [
        local(w_spatial.at[:, dyn_lanes(narrow_peer(p))], ws.at[:, lanes(p)]) for p in range(NARROW)
    ]
    own_expand = local(w_expand.at[:, dyn_lanes(q, own)], we.at[lanes(0), :])
    load_cot = [
        local(view_cot, cot.at[pl.ds(0, nview)]), local(crop_cot, cot.at[pl.ds(nview, rows - nview)])
    ]
    barrier = pltpu.get_barrier_semaphore()

    def greet(k, c):
        pl.semaphore_signal(
            barrier,
            inc=1,
            device_id=(lax.rem(w + k % wide, wide), lax.rem(q + k // wide, NARROW)),
            device_id_type=MESH,
        )
        return c

    everyone = NARROW * wide - 1
    lax.fori_loop(1, everyone + 1, greet, 0, unroll=wide <= 16)

    load_count.wait()
    real = count_ref[0]
    row = lax.broadcasted_iota(jnp.int32, (chunk, 128), 0)
    for r in range(CHUNKS):
        at = row + r * chunk
        image = jnp.where(
            at < nview,
            (at % views_block) // VIEWS_EACH,
            ((at - nview) % crops_block) // CROPS_EACH,
        )
        alive = jnp.where((image < real) & (at < rows), 1.0, 0.0)
        mask[part(r)] = alive.astype(F32)
    tail = pl.ds(rows, padded - rows)
    x[tail] = jnp.zeros((padded - rows, own), BF16)
    xs[1, tail] = jnp.zeros((padded - rows, own), BF16)
    cot[tail] = jnp.zeros((padded - rows, own), BF16)
    taps[tail] = jnp.zeros((padded - rows, len(TAPS) * inner), BF16)
    view_pad[...] = jnp.zeros(view_pad.shape, BF16)
    crop_pad[...] = jnp.zeros(crop_pad.shape, BF16)
    my_count = real.astype(F32) * float(
        VIEWS_EACH * views_side**2 + CROPS_EACH * crops_side**2
    )

    pl.semaphore_wait(barrier, everyone)

    far_reduce = [
        links.send(w_reduce.at[own_rows(1 + 2 * k), :], wr.at[k, :, lanes(1)], far) for k in range(2)
    ]
    near_x = [
        links.send(views, xs.at[1, pl.ds(0, nview)], near),
        links.send(crops, xs.at[1, pl.ds(nview, rows - nview)], near),
    ]
    near_reduce = [links.send(w_reduce.at[own_rows(2), :], wr.at[0, :, lanes(2)], near)]

    def exchange(k, tile, everywhere=False):
        board, me, n = (stat_all, q * wide + w, everyone) if everywhere else (stat, w, wide - 1)
        sem = k + 4 if everywhere else k
        board[k, me] = tile

        def put(step, c):
            pltpu.make_async_remote_copy(
                board.at[k, me],
                board.at[k, me],
                stat_send.at[sem],
                stat_recv.at[sem],
                device_id=(lax.rem(w + step % wide, wide), lax.rem(q + step // wide, NARROW)),
                device_id_type=MESH,
            ).start()
            return c

        lax.fori_loop(1, n + 1, put, 0, unroll=wide <= 16)
        several = board.at[k, pl.ds(0, n)]
        pending.append(pltpu.make_async_copy(several, several, stat_send.at[sem]))
        return pltpu.make_async_copy(several, several, stat_recv.at[sem])

    pending = []

    def moments(ref):
        size = ref.shape[1]
        zero = jnp.zeros((8, size), F32)
        sums = total(loop(lambda at, c: c + fold(ref[at, :] * wider(mask[at, :], size)), zero))
        center = sums / my_count
        squares = total(
            loop(
                lambda at, c: c + fold(jnp.square(ref[at, :] - center) * wider(mask[at, :], size)),
                zero,
            )
        )
        return sums, squares

    def rows_of(k, lo, n):
        return stat[k, :, pl.ds(lo, n), :]

    def combine(sums, squares, counts, pixels):
        center = jnp.sum(sums, axis=0) / pixels
        spread = (
            jnp.sum(squares + counts * jnp.square(sums / counts - center[None]), axis=0) / pixels
        )
        return center, lax.rsqrt(spread + EPS)

    def reduce_scatter(k, give, hold, target, after, meanwhile=lambda: None):
        first, second = [], []
        for copy in in_use.pop(k, ()):
            links.settle(copy)
        for r in range(CHUNKS):
            near_out[k, part(r)] = give(r).astype(BF16)
            first.append(links.send(near_out.at[k, part(r)], near_in.at[k, part(r)], near))
        for r in range(CHUNKS):
            keep[part(r)] = hold(r)
            first[r].wait_recv()
            far_out[k, part(r)] = (
                keep[part(r), lanes(1)] + near_in[k, part(r), lanes(1)].astype(F32)
            ).astype(BF16)
            second.append(links.send(far_out.at[k, part(r)], far_in.at[k, part(r)], far))
            target[part(r)] = keep[part(r), lanes(0)] + near_in[k, part(r), lanes(0)].astype(F32)
        meanwhile()
        for r in range(CHUNKS):
            second[r].wait_recv()
            target[part(r)] = target[part(r)] + far_in[k, part(r)].astype(F32)
            after(r)
        in_use[k] = first + second

    in_use = {}

    class Gather:
        def __init__(self, ref):
            self.ref, self.across, self.onward = ref, [], []

        def send(self, r):
            ref = self.ref
            self.across.append(links.send(ref.at[part(r), lanes(0)], ref.at[part(r), lanes(1)], far))
            if r == CHUNKS - 1:
                self.straight = links.send(ref.at[:, lanes(0)], ref.at[:, lanes(2)], near)

        def hand_on(self, count):
            for r in range(len(self.onward), min(len(self.onward) + count, CHUNKS)):
                self.across[r].wait_recv()
                self.onward.append(
                    links.send(self.ref.at[part(r), lanes(1)], self.ref.at[part(r), lanes(3)], near)
                )

        def near_end(self):
            if self.straight is not None:
                self.straight.wait_recv()
                self.straight = None

        def end(self, use):
            for r in range(CHUNKS + 1):
                self.hand_on(1)
                if r > 0:
                    self.near_end()
                    self.onward[r - 1].wait_recv()
                    use(r - 1)

    across_x, onward_x, shared = [], [], [0]

    def share_x(eighths):
        low = shared[0]
        shared[0] = low + eighths
        first, last = (padded // ROW_TILE * k // 8 * ROW_TILE for k in (low, shared[0]))
        at = pl.ds(first, last - first)
        across_x.append((at, links.send(x.at[at], xs.at[0, at], far, "x")))

    def share_end():
        while len(onward_x) < len(across_x):
            at, copy = across_x[len(onward_x)]
            copy.wait_recv()
            onward_x.append(links.send(xs.at[0, at], xs.at[2, at], near, "x"))

    group_start = w - lax.rem(w, group)

    def block_of(bits, index):
        return sum((index // bit) % 2 * (group // 2 >> k) for k, bit in enumerate(bits))

    def beyond(value, spare):
        bit, at = group, group
        while bit < wide:
            spare[at] = value.astype(BF16)
            copy = links.send(spare.at[at], spare.at[at + 1], (flip(w, bit), q))
            copy.wait_recv()
            value = spare[at].astype(F32) + spare[at + 1].astype(F32)
            bit, at = bit * 2, at + 2
        return value

    def add_block(parts, at, came):
        parts[at] = (parts[at].astype(F32) + came.astype(F32)).astype(BF16)

    def halved(kind, bits, parts, came, finish):
        low, size = 0, group
        for bit in bits:
            size //= 2
            side = (w // bit) % 2
            box = pl.ds(group - 2 * size, size)
            copy = links.send(
                parts.at[pl.ds(low + (1 - side) * size, size)], came.at[box], (flip(w, bit), q), kind
            )
            yield
            copy.wait_recv()
            low = low + side * size
            if size > 1:
                for k in range(size):
                    add_block(parts, low + k, came[group - 2 * size + k])
        value = parts[low].astype(F32) + came[group - 2].astype(F32)
        yield from finish(beyond(value, came))

    def doubled(kind, bits, out):
        low, size = block_of(bits, w), 1
        for bit in reversed(bits):
            box = pl.ds(low, size)
            copy = links.send(out.at[box], out.at[box], (flip(w, bit), q), kind)
            yield
            copy.wait_recv()
            low = low - (w // bit) % 2 * size
            size *= 2

    def group_peers(among):
        for k in range(1, len(among)):
            place = (lax.rem(w, group) + k * (among[1] - among[0])) % group
            yield (group_start + place, q), place

    def halved_then_direct(kind, bits, parts, came, finish):
        quads = group // 2
        side = (w // bits[0]) % 2
        copy = links.send(
            parts.at[pl.ds((1 - side) * quads, quads)], came.at[pl.ds(0, quads)], (flip(w, bits[0]), q), kind
        )
        yield
        copy.wait_recv()
        for k in range(quads):
            add_block(parts, side * quads + k, came[k])
        mine = block_of(bits, w)
        copy = Group(
            links,
            [
                (parts.at[block_of(bits, place)], came.at[quads + mine % quads], peer)
                for peer, place in group_peers(range(0, group, 2))
            ],
            came.at[pl.ds(quads, quads - 1)],
            kind,
        )
        came[quads + mine % quads] = parts[mine]
        yield
        copy.wait_recv()
        value = jnp.sum(came[pl.ds(quads, quads)].astype(F32), axis=0)
        yield from finish(beyond(value, came))

    def direct_then_doubled(kind, bits, out):
        mine = block_of(bits, w)
        copy = Group(
            links,
            [(out.at[mine], out.at[mine], peer) for peer, _ in group_peers(range(0, group, 2))],
            out.at[pl.ds(0, group // 2 - 1)],
            kind,
        )
        yield
        copy.wait_recv()
        box = pl.ds((w // bits[0]) % 2 * (group // 2), group // 2)
        copy = links.send(out.at[box], out.at[box], (flip(w, bits[0]), q), kind)
        yield
        copy.wait_recv()

    def direct(kind, bits, parts, came, finish):
        mine = block_of(bits, w)
        copy = Group(
            links,
            [
                (parts.at[block_of(bits, place)], came.at[mine], peer)
                for peer, place in group_peers(range(group))
            ],
            came.at[pl.ds(0, group - 1)],
            kind,
        )
        came[mine] = parts[mine]
        yield
        copy.wait_recv()
        value = jnp.sum(came[pl.ds(0, group)].astype(F32), axis=0)
        yield from finish(beyond(value, came))

    ways = {
        "h": ((1, 2, 4), halved, doubled),
        "z": ((2, 1, 4), halved, doubled),
        "q": ((1, 2, 4), halved_then_direct, direct_then_doubled),
        "d": ((1, 2, 4), direct, doubled),
    }

    def all_reduced(kind, way, parts, came, out, keep_sum, between=lambda: iter(())):
        bits, there, back = ways[way]

        def finish(value):
            keep_sum(block_of(bits, w), value)
            yield from between()
            yield from back(kind, bits, out)

        return there(kind, bits, parts, came, finish)

    tasks = {}

    def begin(name, task):
        tasks[name] = task
        next(task)

    def advance(*names):
        for name in names:
            if name in tasks and next(tasks[name], "end") == "end":
                del tasks[name]

    for copy in load_reduce + load_x:
        copy.wait()
    for copy in near_x:
        copy.wait_recv()

    def reduce_part(r, p):
        return dot(x[part(r)], wr[0, :, lanes(p)]) + dot(xs[1, part(r)], wr[1, :, lanes(p)])

    for r in range(CHUNKS):
        red[part(r)] = reduce_part(r, 0)
    for copy in far_reduce:
        copy.wait_recv()
    came = []
    for r in range(CHUNKS):
        far_out[0, part(r)] = reduce_part(r, 1).astype(BF16)
        came.append(links.send(far_out.at[0, part(r)], far_in.at[0, part(r)], far))
    near_reduce.append(links.send(wr.at[1, :, lanes(1)], wr.at[0, :, lanes(3)], near))
    for r in range(CHUNKS):
        came[r].wait_recv()
        red[part(r)] = red[part(r)] + far_in[0, part(r)].astype(F32)
    in_use[0] = came
    sent_expand = {
        p: links.send(
            w_expand.at[:, dyn_lanes(narrow_peer(p), own)], we.at[lanes(p), :], (w, narrow_peer(p))
        )
        for p in (3, 1, 2)
    }
    share_x(1)
    sums, squares = moments(red)
    arrived = exchange(
        0,
        jnp.concatenate(
            [sums, squares, jnp.full((1, inner), my_count, F32), jnp.zeros((5, inner), F32)], axis=0
        ),
    )
    for copy in load_spatial:
        copy.wait()
    arrived.wait()
    counts = rows_of(0, 2, 1)
    pixels = jnp.sum(counts, axis=0)
    center1, inverse1 = combine(rows_of(0, 0, 1), rows_of(0, 1, 1), counts, pixels)

    def normed(v, center, inverse, gain, shift):
        standard = (v - center) * inverse
        return standard, gain * standard + shift

    for copy in load_vectors:
        copy.wait()
    g1, s1, g2, s2 = (inner_vectors[k] for k in range(4))
    g3, s3 = (outer_vectors[k] for k in range(2))
    grids = (
        (views_side, views_block, 0, view_pad),
        (crops_side, crops_block, nview, crop_pad),
    )
    for side, block, lead, pad in grids:
        line = side * block
        for h in range(side):
            _, v = normed(red[pl.ds(lead + h * line, line)], center1, inverse1, g1, s1)
            pad[pl.ds(((h + 1) * (side + 2) + 1) * block, line)] = (v * logistic(v)).astype(BF16)
    for side, block, lead, pad in grids:
        line = side * block
        for t, (i, j) in enumerate(TAPS):
            for h in range(side):
                taps[pl.ds(lead + h * line, line), lanes(t)] = pad[
                    pl.ds(((h + i) * (side + 2) + j) * block, line)
                ]

    mixes = Gather(mall)
    reference = []

    def send_mix(r):
        if r == 0:
            alive = mask[part(0)]
            reference.append(total(fold(mix[part(0)] * alive)) / total(fold(alive)))
        mall[part(r), lanes(0)] = (mix[part(r)] - reference[0]).astype(BF16)
        mixes.send(r)

    reduce_scatter(
        1,
        lambda r: dot(taps[part(r)], ws[:, pl.ds(half, half)]),
        lambda r: dot(taps[part(r)], ws[:, pl.ds(0, half)]),
        mix,
        send_mix,
    )
    sums, squares = moments(mix)
    arrived = exchange(
        0,
        jnp.concatenate([sums, squares, g2, s2, reference[0], jnp.zeros((3, inner), F32)], axis=0),
        True,
    )
    own_expand.wait()
    for p in (2, 3, 1):
        sent_expand[p].wait_recv()
    mixes.hand_on(CHUNKS)
    arrived.wait()

    def board_rows(k, p, lo, n):
        return stat_all[k, pl.ds(narrow_peer(p) * wide, wide), pl.ds(lo, n), :]

    def board_row(k, p, lo):
        return stat_all[k, narrow_peer(p) * wide + w, pl.ds(lo, 1), :]

    blocks = [
        combine(board_rows(0, p, 0, 1), board_rows(0, p, 1, 1), counts, pixels) for p in range(NARROW)
    ]
    center2, inverse2 = blocks[0]
    inverse_all = jnp.concatenate([b[1] for b in blocks], axis=1)
    offset_all = jnp.concatenate(
        [board_row(0, p, 4) - blocks[p][0] for p in range(NARROW)], axis=1
    )
    gain_all = jnp.concatenate([board_row(0, p, 2) for p in range(NARROW)], axis=1)
    shift_all = jnp.concatenate([board_row(0, p, 3) for p in range(NARROW)], axis=1)
    scale_all = gain_all * inverse_all
    constant_all = scale_all * offset_all + shift_all

    def expand(r):
        v = mall[part(r), :].astype(F32) * scale_all + constant_all
        ht[part(r), :] = (v * logistic(v)).astype(BF16)
        ex[part(r), :] = dot(ht[part(r)], we[...])

    mixes.end(expand)
    share_end()
    share_x(5)
    sums, squares = moments(ex)
    groups = own // 128

    def tiles(*values):
        return jnp.concatenate(
            [v[:, 128 * k : 128 * k + 128] for v in values for k in range(groups)], axis=0
        )

    arrived = exchange(1, tiles(sums, squares))
    for copy in load_cot:
        copy.wait()
    arrived.wait()
    center3, inverse3 = combine(
        rows_of(1, 0, groups), rows_of(1, groups, groups), counts, pixels
    )
    center3, inverse3 = flat(center3), flat(inverse3)

    def third(at, c):
        standard, v = normed(ex[at, :], center3, inverse3, g3, s3)
        v = v + x[at].astype(F32)
        s = logistic(v)
        alive = wider(mask[at], own)
        res[at] = (alive * (v * s)).astype(BF16)
        g = cot[at].astype(F32) * alive * (s * (1.0 + v * (1.0 - s)))
        b3[at] = g
        return c[0] + fold(g), c[1] + fold(g * standard)

    zero = jnp.zeros((8, own), F32)
    shift_sum, gain_sum = loop(third, (zero, zero))
    arrived = exchange(2, tiles(total(gain_sum), total(shift_sum)))
    results = [
        local(res.at[pl.ds(0, nview)], view_out), local(res.at[pl.ds(nview, rows - nview)], crop_out)
    ]
    arrived.wait()
    both = jnp.sum(stat[2], axis=0)
    large[...] = both
    results.append(local(large, large_out))

    def back_terms(gain_grad, shift_grad, offset, inverse, gain, n):
        scale = gain * inverse
        slope = scale * inverse * (gain_grad / n)
        return scale, scale * (shift_grad / n) + slope * offset, slope

    scale3, base3, slope3 = back_terms(
        flat(both[:groups]), flat(both[groups:]), -center3, inverse3, g3, wider(pixels, own)
    )

    def third_back(at, c):
        ge[at] = (
            scale3 * b3[at] - wider(mask[at], own) * (base3 + slope3 * ex[at, :])
        ).astype(BF16)
        return c

    loop(third_back, 0)

    size_e = inner // group

    def keep_e(mine, value):
        stage_e[...] = value.astype(BF16)
        out_e[mine, :, dyn_lanes(q, own)] = stage_e[0]

    def hand_on_e():
        mine = block_of(ways[WAYS["e"]][0], w)
        got = [
            links.send(
                stage_e.at[p], out_e.at[mine, :, dyn_lanes(q, own)], (w, narrow_peer(p)), "e"
            )
            for p in range(1, NARROW)
        ]
        yield
        for copy in got:
            copy.wait_recv()

    def expand_gradient():
        value = dot_left(ht[...], ge[...]).astype(BF16)
        for p in range(NARROW):
            part_e[:, p] = value[inner * p : inner * (p + 1)].reshape(group, size_e, own)
        begin("e", all_reduced("e", WAYS["e"], part_e, came_e, out_e, keep_e, hand_on_e))
        share_end()

    def slope_of(v):
        s = logistic(v)
        return s * (1.0 + v * (1.0 - s))

    grads = Gather(gall)
    back_sums = [jnp.zeros((8, inner), F32)] * 2

    def second_back(r):
        standard, v = normed(mix[part(r)], center2, inverse2, g2, s2)
        g = back[part(r)] * slope_of(v)
        gall[part(r), lanes(0)] = g.astype(BF16)
        grads.send(r)
        back_sums[0] = back_sums[0] + fold(g * standard)
        back_sums[1] = back_sums[1] + fold(g)

    reduce_scatter(
        0,
        lambda r: dot_right(ge[part(r)], we[pl.ds(half, half), :]),
        lambda r: dot_right(ge[part(r)], we[pl.ds(0, half), :]),
        back,
        second_back,
        expand_gradient,
    )
    arrived = exchange(
        1,
        jnp.concatenate([*map(total, back_sums), jnp.zeros((6, inner), F32)], axis=0),
        True,
    )
    grads.hand_on(CHUNKS)
    arrived.wait()
    sums = [jnp.sum(board_rows(1, p, 0, 2), axis=0) for p in range(NARROW)]
    small[pl.ds(8, 8)] = jnp.concatenate([sums[0], jnp.zeros((6, inner), F32)], axis=0)
    scale2, base2, slope2 = back_terms(
        jnp.concatenate([v[0:1] for v in sums], axis=1),
        jnp.concatenate([v[1:2] for v in sums], axis=1),
        offset_all,
        inverse_all,
        gain_all,
        wider(pixels, full),
    )

    def columns(v, p, n=1):
        return v[:, inner * p : inner * (p + n)]

    def grad_mixed(at, some):
        for p in some:
            gm[at, lanes(p)] = (
                columns(scale2, p) * gall[at, lanes(p)].astype(F32)
                - mask[at] * (columns(base2, p) + columns(slope2, p) * mall[at, lanes(p)].astype(F32))
            ).astype(BF16)
        return 0

    def spatial_gradient(*some):
        value = dot_left(taps[...], jnp.concatenate([gm[:, lanes(p)] for p in some], axis=1))
        for k, p in enumerate(some):
            part_s[p] = columns(value, k).astype(BF16).reshape(part_s.shape[1:])

            def keep_s(mine, value, p=p):
                out_s[p, mine] = value.astype(BF16)

            name = "s%d" % p
            begin(
                name, all_reduced("s", WAYS[name], part_s.at[p], came_s.at[p], out_s.at[p], keep_s)
            )

    grads.near_end()
    loop(lambda at, c: grad_mixed(at, (0, 2)), 0)
    spatial_gradient(0, 2)
    advance("e")

    def spatial_back(r):
        grad_mixed(part(r), (1, 3))
        tp[part(r)] = dot_right(gm[part(r)], ws[...])

    grads.end(spatial_back)
    spatial_gradient(1, 3)
    share_x(2)
    shift_sum = gain_sum = jnp.zeros((8, inner), F32)
    for side, block, lead, pad in grids:
        line = side * block
        for h in range(side):
            g = None
            for t, (i, j) in enumerate(TAPS):
                source = h - (i - 1)
                if not 0 <= source < side:
                    continue
                first = lead + source * line
                if j == 1:
                    term = tp[pl.ds(first, line), lanes(t)]
                elif j == 0:
                    term = jnp.concatenate(
                        [tp[pl.ds(first + block, line - block), lanes(t)], jnp.zeros((block, inner), F32)]
                    )
                else:
                    term = jnp.concatenate(
                        [jnp.zeros((block, inner), F32), tp[pl.ds(first, line - block), lanes(t)]]
                    )
                g = term if g is None else g + term
            at = pl.ds(lead + h * line, line)
            standard, v = normed(red[at], center1, inverse1, g1, s1)
            g = g * slope_of(v)
            back[at] = g
            shift_sum = shift_sum + fold(g)
            gain_sum = gain_sum + fold(g * standard)
    back[tail] = jnp.zeros((padded - rows, inner), F32)
    arrived = exchange(
        3, jnp.concatenate([total(gain_sum), total(shift_sum), jnp.zeros((6, inner), F32)], axis=0)
    )

    advance(*ORDER[0])
    arrived.wait()
    both = jnp.sum(stat[3], axis=0)
    small[pl.ds(0, 8)] = both
    results.append(local(small, small_out))
    scale1, base1, slope1 = back_terms(both[0:1], both[1:2], -center1, inverse1, g1, pixels)

    def first_grad(at, c):
        gr[at, lanes(0)] = (scale1 * back[at] - mask[at] * (base1 + slope1 * red[at])).astype(BF16)
        return c

    loop(first_grad, 0)
    ends = Gather(gr)
    for r in range(CHUNKS):
        ends.send(r)

    per = own // 4

    def reduce_gradient(k):
        for p in (k, 2 + k):
            source = x[...] if p == 0 else xs[p - 1]
            value = dot_left(gr[:, lanes(0)], source).astype(BF16)
            for m in range(4):
                part_r[k, narrow_peer(p) % 2 * 4 + m] = value[:, per * m : per * m + per]

        def keep_r(mine, value):
            out_r[k, mine] = value.T.astype(BF16)

        name = "r%d" % k
        begin(name, all_reduced("r", WAYS[name], part_r.at[k], came_r.at[k], out_r.at[k], keep_r))

    reduce_gradient(0)
    advance(*ORDER[1])
    share_end()
    for copy in onward_x:
        copy.wait_recv()
    reduce_gradient(1)
    advance(*ORDER[2])

    def input_gradient(r):
        dx[part(r)] = (dot_right(gr[part(r)], wr[0]) + b3[part(r)]).astype(BF16)

    for copy in near_reduce:
        copy.wait_recv()
    ends.end(input_gradient)
    results += [
        local(dx.at[pl.ds(0, nview)], view_grad), local(dx.at[pl.ds(nview, rows - nview)], crop_grad)
    ]
    advance(*ORDER[3])
    results.append(local(out_e, expand_out))
    while tasks:
        advance(*list(tasks))
    results += [
        local(out_s.at[p], spatial_out.at[:, :, dyn_lanes(narrow_peer(p))]) for p in range(NARROW)
    ]
    chip = q // 2
    results += [local(out_r.at[0], reduce_out.at[chip]), local(out_r.at[1], reduce_out.at[1 - chip])]
    for copy in links.sent:
        copy.wait_send()
    for copy in pending:
        copy.wait()
    for copy in results:
        copy.wait()


def rows_first(a):
    return a.transpose(1, 2, 0, 3).reshape(-1, a.shape[3])


def images_first(a, like):
    n, h, w, c = like.shape
    return a.reshape(h, w, n, c).transpose(2, 0, 1, 3)


def per_device(wide, *args):
    (
        views, crops, image_count, w_reduce, w_spatial, w_expand,
        gain_one, shift_one, gain_two, shift_two, gain_three, shift_three, view_cot, crop_cot,
    ) = args
    own = views.shape[3]
    inner = w_reduce.shape[1]
    full = NARROW * inner
    nview = views.shape[0] * views.shape[1] * views.shape[2]
    ncrop = crops.shape[0] * crops.shape[1] * crops.shape[2]
    rows = nview + ncrop
    quantum = CHUNKS * ROW_TILE
    padded = -(-rows // quantum) * quantum
    dims = (views.shape[1], views.shape[0], crops.shape[1], crops.shape[0], rows, padded)
    ntaps = len(TAPS) * inner
    group = min(wide, GROUP)
    levels = (wide // group).bit_length() - 1
    slots = group + 2 * levels
    copies = COPIES + len(WAYS) * levels
    vm = pltpu.VMEM
    hbm = pl.BlockSpec(memory_space=pltpu.HBM)
    outs = pl.pallas_call(
        functools.partial(kernel, wide, dims),
        name="block",
        out_shape=(
            jax.ShapeDtypeStruct((nview, own), BF16),
            jax.ShapeDtypeStruct((ncrop, own), BF16),
            jax.ShapeDtypeStruct((nview, own), BF16),
            jax.ShapeDtypeStruct((ncrop, own), BF16),
            jax.ShapeDtypeStruct((2, group, own // 4, inner), BF16),
            jax.ShapeDtypeStruct((group, ntaps // group, full), BF16),
            jax.ShapeDtypeStruct((group, inner // group, NARROW * own), BF16),
            jax.ShapeDtypeStruct((16, inner), F32),
            jax.ShapeDtypeStruct((8, 128), F32),
        ),
        in_specs=[hbm] * 14,
        out_specs=[hbm] * 9,
        scratch_shapes=[
            pltpu.SMEM((1,), jnp.int32),
            vm((4, 1, inner), F32),
            vm((2, 1, own), F32),
            vm((16, inner), F32),
            vm((8, 128), F32),
            vm((padded, own), BF16),
            vm((NARROW - 1, padded, own), BF16),
            vm((padded, own), BF16),
            vm((2, own, full), BF16),
            vm((ntaps, full), BF16),
            vm((full, own), BF16),
            vm((padded, 128), F32),
            vm((4, wide, 8, 128), F32),
            vm((2, NARROW * wide, 8, 128), F32),
            vm((padded, 2 * inner), F32),
            vm((2, padded, 2 * inner), BF16),
            vm((2, padded, 2 * inner), BF16),
            vm((2, padded, inner), BF16),
            vm((2, padded, inner), BF16),
            vm((padded, inner), F32),
            vm((padded, inner), F32),
            vm((padded, inner), F32),
            vm(((dims[0] + 2) ** 2 * dims[1], inner), BF16),
            vm(((dims[2] + 2) ** 2 * dims[3], inner), BF16),
            vm((padded, ntaps), BF16),
            vm((padded, full), BF16),
            vm((padded, full), BF16),
            vm((padded, own), F32),
            vm((padded, own), BF16),
            vm((padded, full), BF16),
            vm((padded, full), BF16),
            vm((padded, ntaps), F32),
            vm((padded, full), BF16),
            vm((padded, own), BF16),
            vm((padded, own), BF16),
            vm((group, inner // group, NARROW * own), BF16),
            vm((NARROW, group, ntaps // group, inner), BF16),
            vm((2, group, own // 4, inner), BF16),
            vm((NARROW, inner // group, own), BF16),
            vm((group, NARROW, inner // group, own), BF16),
            vm((slots, NARROW, inner // group, own), BF16),
            vm((NARROW, group, ntaps // group, inner), BF16),
            vm((NARROW, slots, ntaps // group, inner), BF16),
            vm((2, group, inner, own // 4), BF16),
            vm((2, slots, inner, own // 4), BF16),
            pltpu.SemaphoreType.DMA((copies,)),
            pltpu.SemaphoreType.DMA((copies,)),
            pltpu.SemaphoreType.DMA((6,)),
            pltpu.SemaphoreType.DMA((6,)),
            pltpu.SemaphoreType.DMA((31,)),
        ],
        compiler_params=pltpu.CompilerParams(
            collective_id=0, has_side_effects=True, vmem_limit_bytes=62 * 2**20
        ),
    )(
        image_count,
        rows_first(views),
        rows_first(crops),
        rows_first(view_cot),
        rows_first(crop_cot),
        w_reduce,
        w_spatial.reshape(ntaps, full),
        w_expand,
        *(a.reshape(1, -1) for a in (gain_one, shift_one, gain_two, shift_two, gain_three, shift_three)),
    )
    shapes = [(outs[k].shape, BF16) for k in range(4)]
    shapes += [((NARROW * own, inner), F32), ((ntaps, full), F32), ((inner, NARROW * own), F32)]
    shapes += [((inner,), F32)] * 4 + [((own,), F32)] * 2
    outs = pl.pallas_call(
        release,
        name="release",
        out_shape=tuple(jax.ShapeDtypeStruct(*shape) for shape in shapes),
        in_specs=[hbm] * len(outs),
        out_specs=[hbm] * len(shapes),
        scratch_shapes=[
            vm(outs[4].shape, BF16),
            vm(outs[5].shape, BF16),
            vm(outs[6].shape, BF16),
            vm(shapes[4][0], F32),
            vm(shapes[5][0], F32),
            vm(shapes[6][0], F32),
            *[vm(outs[k].shape, BF16) for k in range(4)],
            vm(outs[7].shape, F32),
            vm(outs[8].shape, F32),
            pltpu.SemaphoreType.DMA((34,)),
        ],
        compiler_params=pltpu.CompilerParams(vmem_limit_bytes=62 * 2**20),
    )(*outs)
    images = (views, crops, views, crops)
    return (
        *(images_first(a, like) for a, like in zip(outs[:4], images)),
        outs[4],
        outs[5].reshape(w_spatial.shape),
        *outs[6:],
    )


def release(*refs):
    images, (reduce_in, spatial_in, expand_in, small, large) = refs[:4], refs[4:9]
    outs, (reduce_v, spatial_v, expand_v, reduce_f, spatial_f, expand_f, *staged, small_v, large_v, sems) = (
        refs[9:22],
        refs[22:],
    )
    used = [0]

    def copy(source, target):
        started = pltpu.make_async_copy(source, target, sems.at[used[0]])
        used[0] += 1
        started.start()
        return started

    loads = [copy(spatial_in, spatial_v), copy(expand_in, expand_v), copy(reduce_in, reduce_v)]
    arrivals = [copy(a, b) for a, b in zip(images, staged)]
    small_in, large_in = copy(small, small_v), copy(large, large_v)
    waits = []
    loads[0].wait()
    each = spatial_v.shape[1]
    for c in range(spatial_v.shape[0]):
        at = pl.ds(c * each, each)
        spatial_f[at] = spatial_v[c].astype(F32)
        if c % 2:
            pair = pl.ds((c - 1) * each, 2 * each)
            waits.append(copy(spatial_f.at[pair], outs[5].at[pair]))
    loads[1].wait()
    expand_f[...] = expand_v[...].astype(F32).reshape(expand_f.shape)
    waits.append(copy(expand_f, outs[6]))
    loads[2].wait()
    blocks, rows = reduce_v.shape[1:3]
    for k in range(2):
        for c in range(blocks):
            reduce_f[pl.ds((k * blocks + c) * rows, rows)] = reduce_v[k, c].astype(F32)
    waits.append(copy(reduce_f, outs[4]))
    for started, a, b in zip(arrivals, staged, outs[:4]):
        started.wait()
        waits.append(copy(a, b))
    small_in.wait()
    large_in.wait()
    for k, row in enumerate((0, 1, 8, 9)):
        waits.append(copy(small_v.at[row], outs[7 + k]))
    groups = large.shape[0] // 2
    for k in range(2):
        for g in range(groups):
            waits.append(copy(large_v.at[k * groups + g], outs[11 + k].at[pl.ds(128 * g, 128)]))
    for started in waits:
        started.wait()


def solution(mesh):
    wide = mesh.shape["wide"]
    image = P("wide", None, None, "narrow")
    vector = P("narrow")
    return jax.shard_map(
        functools.partial(per_device, wide),
        mesh=mesh,
        in_specs=(
            image, image, P("wide"), P(None, "narrow"), P(None, None, "narrow", None), P("narrow", None),
            vector, vector, vector, vector, vector, vector, image, image,
        ),
        out_specs=(
            image, image, image, image, P(None, "narrow"), P(None, None, "narrow", None),
            P("narrow", None), vector, vector, vector, vector, vector, vector,
        ),
        check_vma=False,
    )
```

```python
import functools

import jax
import jax.numpy as jnp
from jax import lax
from jax.experimental import pallas as pl
from jax.experimental.pallas import tpu as pltpu
from jax.sharding import PartitionSpec as P

MESH = pl.DeviceIdType.MESH
EPS = 1e-05
ORDER = (
    ('e', 's0', 's2', 'e'),
    ('s2', 's1'),
    ('s3', 's2', 's0', 'e'),
    ('r0', 'r1', 's3', 's1', 's0', 's2', 's3', 'e', 'r0', 'r1', 's2', 's0', 's1', 's3', 'e', 's3', 'r0', 's1', 's2', 'r1', 's3', 'r0', 'r1'),
)
WAYS = {"e": "d", "s0": "q", "s1": "q", "s2": "z", "s3": "z", "r0": "q", "r1": "q"}
NARROW = 4
CHUNKS = 2
COPIES = 75
ROW_TILE = 16
GROUP = 8
VIEWS_EACH = 2
CROPS_EACH = 4
TAPS = [(i, j) for i in range(3) for j in range(3)]
XOR = (0, 2, 1, 3)
POS = (0, 2, 1, 3)
F32 = jnp.float32
BF16 = jnp.bfloat16


def dot(a, b):
    return jnp.dot(a, b, preferred_element_type=F32)


def dot_right(a, b):
    return lax.dot_general(a, b, (((1,), (1,)), ((), ())), preferred_element_type=F32)


def dot_left(a, b):
    return lax.dot_general(a, b, (((0,), (0,)), ((), ())), preferred_element_type=F32)


def logistic(v):
    return 0.5 + 0.5 * jnp.tanh(0.5 * v)


def flip(index, bit):
    return index + bit - 2 * bit * ((index // bit) % 2)


def wider(tile, lanes):
    return jnp.concatenate([tile] * (lanes // 128), axis=1) if lanes > 128 else tile


def fold(v):
    return jnp.sum(v.reshape(v.shape[0] // 8, 8, v.shape[1]), axis=0)


def total(v):
    return jnp.sum(v, axis=0, keepdims=True)


def flat(v):
    return jnp.concatenate([v[k : k + 1] for k in range(v.shape[0])], axis=1)


class Links:
    def __init__(self, send_sems, recv_sems):
        self.send_sems, self.recv_sems, self.used, self.sent = send_sems, recv_sems, 0, []

    def send(self, source, target, peer, background=""):
        copy = pltpu.make_async_remote_copy(
            source,
            target,
            self.send_sems.at[self.used],
            self.recv_sems.at[self.used],
            device_id=peer,
            device_id_type=MESH,
        )
        self.used += 1
        copy.start()
        self.sent.append(copy)
        return copy

    def settle(self, copy):
        if any(other is copy for other in self.sent):
            copy.wait_send()
            self.sent = [other for other in self.sent if other is not copy]


class Group:
    def __init__(self, links, copies, total, kind):
        self.live = True
        send_sem, recv_sem = links.send_sems.at[links.used], links.recv_sems.at[links.used]
        links.used += 1
        for source, target, peer in copies:
            copy = pltpu.make_async_remote_copy(
                source, target, send_sem, recv_sem, device_id=peer, device_id_type=MESH
            )
            copy.start()
        self.arrival = pltpu.make_async_copy(total, total, recv_sem)
        self.departure = pltpu.make_async_copy(total, total, send_sem)
        links.sent.append(self)

    def wait_recv(self):
        if self.live:
            self.arrival.wait()

    def wait_send(self):
        self.departure.wait()


def kernel(wide, dims, *refs):
    views_side, views_block, crops_side, crops_block, rows, padded = dims
    (
        image_count, views, crops, view_cot, crop_cot, w_reduce, w_spatial, w_expand,
        gain1, shift1, gain2, shift2, gain3, shift3,
        view_out, crop_out, view_grad, crop_grad, reduce_out, spatial_out, expand_out, small_out, large_out,
        count_ref, inner_vectors, outer_vectors, small, large,
        x, xs, cot, wr, ws, we, mask, stat, stat_all, keep, near_out, near_in, far_out, far_in,
        red, mix, back, view_pad, crop_pad, taps, mall, ht, b3, ge, gall, gm, tp, gr, res, dx,
        out_e, out_s, out_r, stage_e, part_e, came_e,
        part_s, came_s, part_r, came_r,
        send_sems, recv_sems, stat_send, stat_recv, local_sems,
    ) = refs
    w = lax.axis_index("wide")
    q = lax.axis_index("narrow")
    near, far = (w, flip(q, 1)), (w, flip(q, 2))
    inner = w_reduce.shape[1]
    own = x.shape[1]
    full = NARROW * inner
    chunk = padded // CHUNKS
    half = 2 * inner
    nview = views.shape[0]
    group = min(wide, GROUP)
    ex = tp.at[:, pl.ds(0, own)]
    links = Links(send_sems, recv_sems)
    slot = [0]

    def local(source, target):
        copy = pltpu.make_async_copy(source, target, local_sems.at[slot[0]])
        slot[0] += 1
        copy.start()
        return copy

    def part(r):
        return pl.ds(r * chunk, chunk)

    def lanes(p, width=inner):
        return pl.ds(p * width, width)

    def dyn_lanes(p, width=inner):
        return pl.ds(pl.multiple_of(p * width, width), width)

    def narrow_peer(p):
        i = q
        if XOR[p] & 1:
            i = flip(i, 1)
        if XOR[p] & 2:
            i = flip(i, 2)
        return i

    def loop(body, init):
        return lax.fori_loop(
            0, CHUNKS, lambda i, c: body(pl.ds(pl.multiple_of(i * chunk, chunk), chunk), c), init
        )

    def own_rows(p):
        return pl.ds(pl.multiple_of(narrow_peer(p) * own, own), own)

    load_count = local(image_count, count_ref)
    load_vectors = [local(ref, inner_vectors.at[k]) for k, ref in enumerate((gain1, shift1, gain2, shift2))]
    load_vectors += [local(ref, outer_vectors.at[k]) for k, ref in enumerate((gain3, shift3))]
    load_reduce = [local(w_reduce.at[own_rows(2 * k), :], wr.at[k, :, lanes(0)]) for k in range(2)]
    load_x = [local(views, x.at[pl.ds(0, nview)]), local(crops, x.at[pl.ds(nview, rows - nview)])]
    load_spatial = [
        local(w_spatial.at[:, dyn_lanes(narrow_peer(p))], ws.at[:, lanes(p)]) for p in range(NARROW)
    ]
    own_expand = local(w_expand.at[:, dyn_lanes(q, own)], we.at[lanes(0), :])
    load_cot = [
        local(view_cot, cot.at[pl.ds(0, nview)]), local(crop_cot, cot.at[pl.ds(nview, rows - nview)])
    ]
    barrier = pltpu.get_barrier_semaphore()

    def greet(k, c):
        pl.semaphore_signal(
            barrier,
            inc=1,
            device_id=(lax.rem(w + k % wide, wide), lax.rem(q + k // wide, NARROW)),
            device_id_type=MESH,
        )
        return c

    everyone = NARROW * wide - 1
    lax.fori_loop(1, everyone + 1, greet, 0, unroll=wide <= 16)

    load_count.wait()
    real = count_ref[0]
    row = lax.broadcasted_iota(jnp.int32, (chunk, 128), 0)
    for r in range(CHUNKS):
        at = row + r * chunk
        image = jnp.where(
            at < nview,
            (at % views_block) // VIEWS_EACH,
            ((at - nview) % crops_block) // CROPS_EACH,
        )
        alive = jnp.where((image < real) & (at < rows), 1.0, 0.0)
        mask[part(r)] = alive.astype(F32)
    tail = pl.ds(rows, padded - rows)
    x[tail] = jnp.zeros((padded - rows, own), BF16)
    xs[1, tail] = jnp.zeros((padded - rows, own), BF16)
    cot[tail] = jnp.zeros((padded - rows, own), BF16)
    taps[tail] = jnp.zeros((padded - rows, len(TAPS) * inner), BF16)
    view_pad[...] = jnp.zeros(view_pad.shape, BF16)
    crop_pad[...] = jnp.zeros(crop_pad.shape, BF16)
    my_count = real.astype(F32) * float(
        VIEWS_EACH * views_side**2 + CROPS_EACH * crops_side**2
    )

    pl.semaphore_wait(barrier, everyone)

    far_reduce = [
        links.send(w_reduce.at[own_rows(1 + 2 * k), :], wr.at[k, :, lanes(1)], far) for k in range(2)
    ]
    near_x = [
        links.send(views, xs.at[1, pl.ds(0, nview)], near),
        links.send(crops, xs.at[1, pl.ds(nview, rows - nview)], near),
    ]
    near_reduce = [links.send(w_reduce.at[own_rows(2), :], wr.at[0, :, lanes(2)], near)]

    def exchange(k, tile, everywhere=False):
        board, me, n = (stat_all, q * wide + w, everyone) if everywhere else (stat, w, wide - 1)
        sem = k + 4 if everywhere else k
        board[k, me] = tile

        def put(step, c):
            pltpu.make_async_remote_copy(
                board.at[k, me],
                board.at[k, me],
                stat_send.at[sem],
                stat_recv.at[sem],
                device_id=(lax.rem(w + step % wide, wide), lax.rem(q + step // wide, NARROW)),
                device_id_type=MESH,
            ).start()
            return c

        lax.fori_loop(1, n + 1, put, 0, unroll=wide <= 16)
        several = board.at[k, pl.ds(0, n)]
        pending.append(pltpu.make_async_copy(several, several, stat_send.at[sem]))
        return pltpu.make_async_copy(several, several, stat_recv.at[sem])

    pending = []

    def moments(ref):
        size = ref.shape[1]
        zero = jnp.zeros((8, size), F32)
        sums = total(loop(lambda at, c: c + fold(ref[at, :] * wider(mask[at, :], size)), zero))
        center = sums / my_count
        squares = total(
            loop(
                lambda at, c: c + fold(jnp.square(ref[at, :] - center) * wider(mask[at, :], size)),
                zero,
            )
        )
        return sums, squares

    def rows_of(k, lo, n):
        return stat[k, :, pl.ds(lo, n), :]

    def combine(sums, squares, counts, pixels):
        center = jnp.sum(sums, axis=0) / pixels
        spread = (
            jnp.sum(squares + counts * jnp.square(sums / counts - center[None]), axis=0) / pixels
        )
        return center, lax.rsqrt(spread + EPS)

    def reduce_scatter(k, give, hold, target, after, meanwhile=lambda: None):
        first, second = [], []
        for copy in in_use.pop(k, ()):
            links.settle(copy)
        for r in range(CHUNKS):
            near_out[k, part(r)] = give(r).astype(BF16)
            first.append(links.send(near_out.at[k, part(r)], near_in.at[k, part(r)], near))
        for r in range(CHUNKS):
            keep[part(r)] = hold(r)
            first[r].wait_recv()
            far_out[k, part(r)] = (
                keep[part(r), lanes(1)] + near_in[k, part(r), lanes(1)].astype(F32)
            ).astype(BF16)
            second.append(links.send(far_out.at[k, part(r)], far_in.at[k, part(r)], far))
            target[part(r)] = keep[part(r), lanes(0)] + near_in[k, part(r), lanes(0)].astype(F32)
        meanwhile()
        for r in range(CHUNKS):
            second[r].wait_recv()
            target[part(r)] = target[part(r)] + far_in[k, part(r)].astype(F32)
            after(r)
        in_use[k] = first + second

    in_use = {}

    class Gather:
        def __init__(self, ref):
            self.ref, self.across, self.onward = ref, [], []

        def send(self, r):
            ref = self.ref
            self.across.append(links.send(ref.at[part(r), lanes(0)], ref.at[part(r), lanes(1)], far))
            if r == CHUNKS - 1:
                self.straight = links.send(ref.at[:, lanes(0)], ref.at[:, lanes(2)], near)

        def hand_on(self, count):
            for r in range(len(self.onward), min(len(self.onward) + count, CHUNKS)):
                self.across[r].wait_recv()
                self.onward.append(
                    links.send(self.ref.at[part(r), lanes(1)], self.ref.at[part(r), lanes(3)], near)
                )

        def near_end(self):
            if self.straight is not None:
                self.straight.wait_recv()
                self.straight = None

        def end(self, use):
            for r in range(CHUNKS + 1):
                self.hand_on(1)
                if r > 0:
                    self.near_end()
                    self.onward[r - 1].wait_recv()
                    use(r - 1)

    across_x, onward_x, shared = [], [], [0]

    def share_x(eighths):
        low = shared[0]
        shared[0] = low + eighths
        first, last = (padded // ROW_TILE * k // 8 * ROW_TILE for k in (low, shared[0]))
        at = pl.ds(first, last - first)
        across_x.append((at, links.send(x.at[at], xs.at[0, at], far, "x")))

    def share_end():
        while len(onward_x) < len(across_x):
            at, copy = across_x[len(onward_x)]
            copy.wait_recv()
            onward_x.append(links.send(xs.at[0, at], xs.at[2, at], near, "x"))

    group_start = w - lax.rem(w, group)

    def block_of(bits, index):
        return sum((index // bit) % 2 * (group // 2 >> k) for k, bit in enumerate(bits))

    def beyond(value, spare):
        bit, at = group, group
        while bit < wide:
            spare[at] = value.astype(BF16)
            copy = links.send(spare.at[at], spare.at[at + 1], (flip(w, bit), q))
            copy.wait_recv()
            value = spare[at].astype(F32) + spare[at + 1].astype(F32)
            bit, at = bit * 2, at + 2
        return value

    def add_block(parts, at, came):
        parts[at] = (parts[at].astype(F32) + came.astype(F32)).astype(BF16)

    def halved(kind, bits, parts, came, finish):
        low, size = 0, group
        for bit in bits:
            size //= 2
            side = (w // bit) % 2
            box = pl.ds(group - 2 * size, size)
            copy = links.send(
                parts.at[pl.ds(low + (1 - side) * size, size)], came.at[box], (flip(w, bit), q), kind
            )
            yield
            copy.wait_recv()
            low = low + side * size
            if size > 1:
                for k in range(size):
                    add_block(parts, low + k, came[group - 2 * size + k])
        value = parts[low].astype(F32) + came[group - 2].astype(F32)
        yield from finish(beyond(value, came))

    def doubled(kind, bits, out):
        low, size = block_of(bits, w), 1
        for bit in reversed(bits):
            box = pl.ds(low, size)
            copy = links.send(out.at[box], out.at[box], (flip(w, bit), q), kind)
            yield
            copy.wait_recv()
            low = low - (w // bit) % 2 * size
            size *= 2

    def group_peers(among):
        for k in range(1, len(among)):
            place = (lax.rem(w, group) + k * (among[1] - among[0])) % group
            yield (group_start + place, q), place

    def halved_then_direct(kind, bits, parts, came, finish):
        quads = group // 2
        side = (w // bits[0]) % 2
        copy = links.send(
            parts.at[pl.ds((1 - side) * quads, quads)], came.at[pl.ds(0, quads)], (flip(w, bits[0]), q), kind
        )
        yield
        copy.wait_recv()
        for k in range(quads):
            add_block(parts, side * quads + k, came[k])
        mine = block_of(bits, w)
        copy = Group(
            links,
            [
                (parts.at[block_of(bits, place)], came.at[quads + mine % quads], peer)
                for peer, place in group_peers(range(0, group, 2))
            ],
            came.at[pl.ds(quads, quads - 1)],
            kind,
        )
        came[quads + mine % quads] = parts[mine]
        yield
        copy.wait_recv()
        value = jnp.sum(came[pl.ds(quads, quads)].astype(F32), axis=0)
        yield from finish(beyond(value, came))

    def direct_then_doubled(kind, bits, out):
        mine = block_of(bits, w)
        copy = Group(
            links,
            [(out.at[mine], out.at[mine], peer) for peer, _ in group_peers(range(0, group, 2))],
            out.at[pl.ds(0, group // 2 - 1)],
            kind,
        )
        yield
        copy.wait_recv()
        box = pl.ds((w // bits[0]) % 2 * (group // 2), group // 2)
        copy = links.send(out.at[box], out.at[box], (flip(w, bits[0]), q), kind)
        yield
        copy.wait_recv()

    def direct(kind, bits, parts, came, finish):
        mine = block_of(bits, w)
        copy = Group(
            links,
            [
                (parts.at[block_of(bits, place)], came.at[mine], peer)
                for peer, place in group_peers(range(group))
            ],
            came.at[pl.ds(0, group - 1)],
            kind,
        )
        came[mine] = parts[mine]
        yield
        copy.wait_recv()
        value = jnp.sum(came[pl.ds(0, group)].astype(F32), axis=0)
        yield from finish(beyond(value, came))

    ways = {
        "h": ((1, 2, 4), halved, doubled),
        "z": ((2, 1, 4), halved, doubled),
        "q": ((1, 2, 4), halved_then_direct, direct_then_doubled),
        "d": ((1, 2, 4), direct, doubled),
    }

    def all_reduced(kind, way, parts, came, out, keep_sum, between=lambda: iter(())):
        bits, there, back = ways[way]

        def finish(value):
            keep_sum(block_of(bits, w), value)
            yield from between()
            yield from back(kind, bits, out)

        return there(kind, bits, parts, came, finish)

    tasks = {}

    def begin(name, task):
        tasks[name] = task
        next(task)

    def advance(*names):
        for name in names:
            if name in tasks and next(tasks[name], "end") == "end":
                del tasks[name]
                write_out(name)

    def write_out(name):
        if name == "e":
            results.append(local(out_e, expand_out))
            return
        k = int(name[1])
        if name[0] == "s":
            target = spatial_out.at[:, :, dyn_lanes(narrow_peer(k))]
            results.append(local(out_s.at[k], target))
        else:
            target = reduce_out.at[q // 2 if k == 0 else 1 - q // 2]
            results.append(local(out_r.at[k], target))

    for copy in load_reduce + load_x:
        copy.wait()
    for copy in near_x:
        copy.wait_recv()

    def reduce_part(r, p):
        return dot(x[part(r)], wr[0, :, lanes(p)]) + dot(xs[1, part(r)], wr[1, :, lanes(p)])

    for r in range(CHUNKS):
        red[part(r)] = reduce_part(r, 0)
    for copy in far_reduce:
        copy.wait_recv()
    came = []
    for r in range(CHUNKS):
        far_out[0, part(r)] = reduce_part(r, 1).astype(BF16)
        came.append(links.send(far_out.at[0, part(r)], far_in.at[0, part(r)], far))
    near_reduce.append(links.send(wr.at[1, :, lanes(1)], wr.at[0, :, lanes(3)], near))
    for r in range(CHUNKS):
        came[r].wait_recv()
        red[part(r)] = red[part(r)] + far_in[0, part(r)].astype(F32)
    in_use[0] = came
    sent_expand = {
        p: links.send(
            w_expand.at[:, dyn_lanes(narrow_peer(p), own)], we.at[lanes(p), :], (w, narrow_peer(p))
        )
        for p in (3, 1, 2)
    }
    share_x(1)
    sums, squares = moments(red)
    arrived = exchange(
        0,
        jnp.concatenate(
            [sums, squares, jnp.full((1, inner), my_count, F32), jnp.zeros((5, inner), F32)], axis=0
        ),
    )
    for copy in load_spatial:
        copy.wait()
    arrived.wait()
    counts = rows_of(0, 2, 1)
    pixels = jnp.sum(counts, axis=0)
    center1, inverse1 = combine(rows_of(0, 0, 1), rows_of(0, 1, 1), counts, pixels)

    def normed(v, center, inverse, gain, shift):
        standard = (v - center) * inverse
        return standard, gain * standard + shift

    for copy in load_vectors:
        copy.wait()
    g1, s1, g2, s2 = (inner_vectors[k] for k in range(4))
    g3, s3 = (outer_vectors[k] for k in range(2))
    grids = (
        (views_side, views_block, 0, view_pad),
        (crops_side, crops_block, nview, crop_pad),
    )
    for side, block, lead, pad in grids:
        line = side * block
        for h in range(side):
            _, v = normed(red[pl.ds(lead + h * line, line)], center1, inverse1, g1, s1)
            pad[pl.ds(((h + 1) * (side + 2) + 1) * block, line)] = (v * logistic(v)).astype(BF16)
    for side, block, lead, pad in grids:
        line = side * block
        for t, (i, j) in enumerate(TAPS):
            for h in range(side):
                taps[pl.ds(lead + h * line, line), lanes(t)] = pad[
                    pl.ds(((h + i) * (side + 2) + j) * block, line)
                ]

    mixes = Gather(mall)
    reference = []

    def send_mix(r):
        if r == 0:
            alive = mask[part(0)]
            reference.append(total(fold(mix[part(0)] * alive)) / total(fold(alive)))
        mall[part(r), lanes(0)] = (mix[part(r)] - reference[0]).astype(BF16)
        mixes.send(r)

    reduce_scatter(
        1,
        lambda r: dot(taps[part(r)], ws[:, pl.ds(half, half)]),
        lambda r: dot(taps[part(r)], ws[:, pl.ds(0, half)]),
        mix,
        send_mix,
    )
    sums, squares = moments(mix)
    arrived = exchange(
        0,
        jnp.concatenate([sums, squares, g2, s2, reference[0], jnp.zeros((3, inner), F32)], axis=0),
        True,
    )
    own_expand.wait()
    for p in (2, 3, 1):
        sent_expand[p].wait_recv()
    mixes.hand_on(CHUNKS)
    arrived.wait()

    def board_rows(k, p, lo, n):
        return stat_all[k, pl.ds(narrow_peer(p) * wide, wide), pl.ds(lo, n), :]

    def board_row(k, p, lo):
        return stat_all[k, narrow_peer(p) * wide + w, pl.ds(lo, 1), :]

    blocks = [
        combine(board_rows(0, p, 0, 1), board_rows(0, p, 1, 1), counts, pixels) for p in range(NARROW)
    ]
    center2, inverse2 = blocks[0]
    inverse_all = jnp.concatenate([b[1] for b in blocks], axis=1)
    offset_all = jnp.concatenate(
        [board_row(0, p, 4) - blocks[p][0] for p in range(NARROW)], axis=1
    )
    gain_all = jnp.concatenate([board_row(0, p, 2) for p in range(NARROW)], axis=1)
    shift_all = jnp.concatenate([board_row(0, p, 3) for p in range(NARROW)], axis=1)
    scale_all = gain_all * inverse_all
    constant_all = scale_all * offset_all + shift_all

    def expand(r):
        v = mall[part(r), :].astype(F32) * scale_all + constant_all
        ht[part(r), :] = (v * logistic(v)).astype(BF16)
        ex[part(r), :] = dot(ht[part(r)], we[...])

    mixes.end(expand)
    share_end()
    share_x(5)
    sums, squares = moments(ex)
    groups = own // 128

    def tiles(*values):
        return jnp.concatenate(
            [v[:, 128 * k : 128 * k + 128] for v in values for k in range(groups)], axis=0
        )

    arrived = exchange(1, tiles(sums, squares))
    for copy in load_cot:
        copy.wait()
    arrived.wait()
    center3, inverse3 = combine(
        rows_of(1, 0, groups), rows_of(1, groups, groups), counts, pixels
    )
    center3, inverse3 = flat(center3), flat(inverse3)

    def third(at, c):
        standard, v = normed(ex[at, :], center3, inverse3, g3, s3)
        v = v + x[at].astype(F32)
        s = logistic(v)
        alive = wider(mask[at], own)
        res[at] = (alive * (v * s)).astype(BF16)
        g = cot[at].astype(F32) * alive * (s * (1.0 + v * (1.0 - s)))
        b3[at] = g
        return c[0] + fold(g), c[1] + fold(g * standard)

    zero = jnp.zeros((8, own), F32)
    shift_sum, gain_sum = loop(third, (zero, zero))
    arrived = exchange(2, tiles(total(gain_sum), total(shift_sum)))
    results = [
        local(res.at[pl.ds(0, nview)], view_out), local(res.at[pl.ds(nview, rows - nview)], crop_out)
    ]
    arrived.wait()
    both = jnp.sum(stat[2], axis=0)
    large[...] = both
    results.append(local(large, large_out))

    def back_terms(gain_grad, shift_grad, offset, inverse, gain, n):
        scale = gain * inverse
        slope = scale * inverse * (gain_grad / n)
        return scale, scale * (shift_grad / n) + slope * offset, slope

    scale3, base3, slope3 = back_terms(
        flat(both[:groups]), flat(both[groups:]), -center3, inverse3, g3, wider(pixels, own)
    )

    def third_back(at, c):
        ge[at] = (
            scale3 * b3[at] - wider(mask[at], own) * (base3 + slope3 * ex[at, :])
        ).astype(BF16)
        return c

    loop(third_back, 0)

    size_e = inner // group

    def keep_e(mine, value):
        stage_e[...] = value.astype(BF16)
        out_e[mine, :, dyn_lanes(q, own)] = stage_e[0]

    def hand_on_e():
        mine = block_of(ways[WAYS["e"]][0], w)
        got = [
            links.send(
                stage_e.at[p], out_e.at[mine, :, dyn_lanes(q, own)], (w, narrow_peer(p)), "e"
            )
            for p in range(1, NARROW)
        ]
        yield
        for copy in got:
            copy.wait_recv()

    def expand_gradient():
        value = dot_left(ht[...], ge[...]).astype(BF16)
        for p in range(NARROW):
            part_e[:, p] = value[inner * p : inner * (p + 1)].reshape(group, size_e, own)
        begin("e", all_reduced("e", WAYS["e"], part_e, came_e, out_e, keep_e, hand_on_e))
        share_end()

    def slope_of(v):
        s = logistic(v)
        return s * (1.0 + v * (1.0 - s))

    grads = Gather(gall)
    back_sums = [jnp.zeros((8, inner), F32)] * 2

    def second_back(r):
        standard, v = normed(mix[part(r)], center2, inverse2, g2, s2)
        g = back[part(r)] * slope_of(v)
        gall[part(r), lanes(0)] = g.astype(BF16)
        grads.send(r)
        back_sums[0] = back_sums[0] + fold(g * standard)
        back_sums[1] = back_sums[1] + fold(g)

    reduce_scatter(
        0,
        lambda r: dot_right(ge[part(r)], we[pl.ds(half, half), :]),
        lambda r: dot_right(ge[part(r)], we[pl.ds(0, half), :]),
        back,
        second_back,
        expand_gradient,
    )
    arrived = exchange(
        1,
        jnp.concatenate([*map(total, back_sums), jnp.zeros((6, inner), F32)], axis=0),
        True,
    )
    grads.hand_on(CHUNKS)
    arrived.wait()
    sums = [jnp.sum(board_rows(1, p, 0, 2), axis=0) for p in range(NARROW)]
    small[pl.ds(8, 8)] = jnp.concatenate([sums[0], jnp.zeros((6, inner), F32)], axis=0)
    scale2, base2, slope2 = back_terms(
        jnp.concatenate([v[0:1] for v in sums], axis=1),
        jnp.concatenate([v[1:2] for v in sums], axis=1),
        offset_all,
        inverse_all,
        gain_all,
        wider(pixels, full),
    )

    def columns(v, p, n=1):
        return v[:, inner * p : inner * (p + n)]

    def grad_mixed(at, some):
        for p in some:
            gm[at, lanes(p)] = (
                columns(scale2, p) * gall[at, lanes(p)].astype(F32)
                - mask[at] * (columns(base2, p) + columns(slope2, p) * mall[at, lanes(p)].astype(F32))
            ).astype(BF16)
        return 0

    def spatial_gradient(*some):
        value = dot_left(taps[...], jnp.concatenate([gm[:, lanes(p)] for p in some], axis=1))
        for k, p in enumerate(some):
            part_s[p] = columns(value, k).astype(BF16).reshape(part_s.shape[1:])

            def keep_s(mine, value, p=p):
                out_s[p, mine] = value.astype(BF16)

            name = "s%d" % p
            begin(
                name, all_reduced("s", WAYS[name], part_s.at[p], came_s.at[p], out_s.at[p], keep_s)
            )

    grads.near_end()
    loop(lambda at, c: grad_mixed(at, (0, 2)), 0)
    spatial_gradient(0, 2)
    advance("e")

    def spatial_back(r):
        grad_mixed(part(r), (1, 3))
        tp[part(r)] = dot_right(gm[part(r)], ws[...])

    grads.end(spatial_back)
    spatial_gradient(1, 3)
    share_x(2)
    shift_sum = gain_sum = jnp.zeros((8, inner), F32)
    for side, block, lead, pad in grids:
        line = side * block
        for h in range(side):
            g = None
            for t, (i, j) in enumerate(TAPS):
                source = h - (i - 1)
                if not 0 <= source < side:
                    continue
                first = lead + source * line
                if j == 1:
                    term = tp[pl.ds(first, line), lanes(t)]
                elif j == 0:
                    term = jnp.concatenate(
                        [tp[pl.ds(first + block, line - block), lanes(t)], jnp.zeros((block, inner), F32)]
                    )
                else:
                    term = jnp.concatenate(
                        [jnp.zeros((block, inner), F32), tp[pl.ds(first, line - block), lanes(t)]]
                    )
                g = term if g is None else g + term
            at = pl.ds(lead + h * line, line)
            standard, v = normed(red[at], center1, inverse1, g1, s1)
            g = g * slope_of(v)
            back[at] = g
            shift_sum = shift_sum + fold(g)
            gain_sum = gain_sum + fold(g * standard)
    back[tail] = jnp.zeros((padded - rows, inner), F32)
    arrived = exchange(
        3, jnp.concatenate([total(gain_sum), total(shift_sum), jnp.zeros((6, inner), F32)], axis=0)
    )

    advance(*ORDER[0])
    arrived.wait()
    both = jnp.sum(stat[3], axis=0)
    small[pl.ds(0, 8)] = both
    results.append(local(small, small_out))
    scale1, base1, slope1 = back_terms(both[0:1], both[1:2], -center1, inverse1, g1, pixels)

    def first_grad(at, c):
        gr[at, lanes(0)] = (scale1 * back[at] - mask[at] * (base1 + slope1 * red[at])).astype(BF16)
        return c

    loop(first_grad, 0)
    ends = Gather(gr)
    for r in range(CHUNKS):
        ends.send(r)

    per = own // 4

    def reduce_gradient(k):
        for p in (k, 2 + k):
            source = x[...] if p == 0 else xs[p - 1]
            value = dot_left(gr[:, lanes(0)], source).astype(BF16)
            for m in range(4):
                part_r[k, narrow_peer(p) % 2 * 4 + m] = value[:, per * m : per * m + per]

        def keep_r(mine, value):
            out_r[k, mine] = value.T.astype(BF16)

        name = "r%d" % k
        begin(name, all_reduced("r", WAYS[name], part_r.at[k], came_r.at[k], out_r.at[k], keep_r))

    reduce_gradient(0)
    advance(*ORDER[1])
    share_end()
    for copy in onward_x:
        copy.wait_recv()
    reduce_gradient(1)
    advance(*ORDER[2])

    def input_gradient(r):
        dx[part(r)] = (dot_right(gr[part(r)], wr[0]) + b3[part(r)]).astype(BF16)

    for copy in near_reduce:
        copy.wait_recv()
    ends.end(input_gradient)
    results += [
        local(dx.at[pl.ds(0, nview)], view_grad), local(dx.at[pl.ds(nview, rows - nview)], crop_grad)
    ]
    advance(*ORDER[3])
    while tasks:
        advance(*list(tasks))
    for copy in links.sent:
        copy.wait_send()
    for copy in pending:
        copy.wait()
    for copy in results:
        copy.wait()


def rows_first(a):
    return a.transpose(1, 2, 0, 3).reshape(-1, a.shape[3])


def images_first(a, like):
    n, h, w, c = like.shape
    return a.reshape(h, w, n, c).transpose(2, 0, 1, 3)


def per_device(wide, *args):
    (
        views, crops, image_count, w_reduce, w_spatial, w_expand,
        gain_one, shift_one, gain_two, shift_two, gain_three, shift_three, view_cot, crop_cot,
    ) = args
    own = views.shape[3]
    inner = w_reduce.shape[1]
    full = NARROW * inner
    nview = views.shape[0] * views.shape[1] * views.shape[2]
    ncrop = crops.shape[0] * crops.shape[1] * crops.shape[2]
    rows = nview + ncrop
    quantum = CHUNKS * ROW_TILE
    padded = -(-rows // quantum) * quantum
    dims = (views.shape[1], views.shape[0], crops.shape[1], crops.shape[0], rows, padded)
    ntaps = len(TAPS) * inner
    group = min(wide, GROUP)
    levels = (wide // group).bit_length() - 1
    slots = group + 2 * levels
    copies = COPIES + len(WAYS) * levels
    vm = pltpu.VMEM
    hbm = pl.BlockSpec(memory_space=pltpu.HBM)
    outs = pl.pallas_call(
        functools.partial(kernel, wide, dims),
        name="block",
        out_shape=(
            jax.ShapeDtypeStruct((nview, own), BF16),
            jax.ShapeDtypeStruct((ncrop, own), BF16),
            jax.ShapeDtypeStruct((nview, own), BF16),
            jax.ShapeDtypeStruct((ncrop, own), BF16),
            jax.ShapeDtypeStruct((2, group, own // 4, inner), BF16),
            jax.ShapeDtypeStruct((group, ntaps // group, full), BF16),
            jax.ShapeDtypeStruct((group, inner // group, NARROW * own), BF16),
            jax.ShapeDtypeStruct((16, inner), F32),
            jax.ShapeDtypeStruct((8, 128), F32),
        ),
        in_specs=[hbm] * 14,
        out_specs=[hbm] * 9,
        scratch_shapes=[
            pltpu.SMEM((1,), jnp.int32),
            vm((4, 1, inner), F32),
            vm((2, 1, own), F32),
            vm((16, inner), F32),
            vm((8, 128), F32),
            vm((padded, own), BF16),
            vm((NARROW - 1, padded, own), BF16),
            vm((padded, own), BF16),
            vm((2, own, full), BF16),
            vm((ntaps, full), BF16),
            vm((full, own), BF16),
            vm((padded, 128), F32),
            vm((4, wide, 8, 128), F32),
            vm((2, NARROW * wide, 8, 128), F32),
            vm((padded, 2 * inner), F32),
            vm((2, padded, 2 * inner), BF16),
            vm((2, padded, 2 * inner), BF16),
            vm((2, padded, inner), BF16),
            vm((2, padded, inner), BF16),
            vm((padded, inner), F32),
            vm((padded, inner), F32),
            vm((padded, inner), F32),
            vm(((dims[0] + 2) ** 2 * dims[1], inner), BF16),
            vm(((dims[2] + 2) ** 2 * dims[3], inner), BF16),
            vm((padded, ntaps), BF16),
            vm((padded, full), BF16),
            vm((padded, full), BF16),
            vm((padded, own), F32),
            vm((padded, own), BF16),
            vm((padded, full), BF16),
            vm((padded, full), BF16),
            vm((padded, ntaps), F32),
            vm((padded, full), BF16),
            vm((padded, own), BF16),
            vm((padded, own), BF16),
            vm((group, inner // group, NARROW * own), BF16),
            vm((NARROW, group, ntaps // group, inner), BF16),
            vm((2, group, own // 4, inner), BF16),
            vm((NARROW, inner // group, own), BF16),
            vm((group, NARROW, inner // group, own), BF16),
            vm((slots, NARROW, inner // group, own), BF16),
            vm((NARROW, group, ntaps // group, inner), BF16),
            vm((NARROW, slots, ntaps // group, inner), BF16),
            vm((2, group, inner, own // 4), BF16),
            vm((2, slots, inner, own // 4), BF16),
            pltpu.SemaphoreType.DMA((copies,)),
            pltpu.SemaphoreType.DMA((copies,)),
            pltpu.SemaphoreType.DMA((6,)),
            pltpu.SemaphoreType.DMA((6,)),
            pltpu.SemaphoreType.DMA((31,)),
        ],
        compiler_params=pltpu.CompilerParams(
            collective_id=0, has_side_effects=True, vmem_limit_bytes=62 * 2**20
        ),
    )(
        image_count,
        rows_first(views),
        rows_first(crops),
        rows_first(view_cot),
        rows_first(crop_cot),
        w_reduce,
        w_spatial.reshape(ntaps, full),
        w_expand,
        *(a.reshape(1, -1) for a in (gain_one, shift_one, gain_two, shift_two, gain_three, shift_three)),
    )
    shapes = [(outs[k].shape, BF16) for k in range(4)]
    shapes += [((NARROW * own, inner), F32), ((ntaps, full), F32), ((inner, NARROW * own), F32)]
    shapes += [((inner,), F32)] * 4 + [((own,), F32)] * 2
    outs = pl.pallas_call(
        release,
        name="release",
        out_shape=tuple(jax.ShapeDtypeStruct(*shape) for shape in shapes),
        in_specs=[hbm] * len(outs),
        out_specs=[hbm] * len(shapes),
        scratch_shapes=[
            vm(outs[4].shape, BF16),
            vm(outs[5].shape, BF16),
            vm(outs[6].shape, BF16),
            vm(shapes[4][0], F32),
            vm(shapes[5][0], F32),
            vm(shapes[6][0], F32),
            *[vm(outs[k].shape, BF16) for k in range(4)],
            vm(outs[7].shape, F32),
            vm(outs[8].shape, F32),
            pltpu.SemaphoreType.DMA((34,)),
        ],
        compiler_params=pltpu.CompilerParams(vmem_limit_bytes=62 * 2**20),
    )(*outs)
    images = (views, crops, views, crops)
    return (
        *(images_first(a, like) for a, like in zip(outs[:4], images)),
        outs[4],
        outs[5].reshape(w_spatial.shape),
        *outs[6:],
    )


def release(*refs):
    images, (reduce_in, spatial_in, expand_in, small, large) = refs[:4], refs[4:9]
    outs, (reduce_v, spatial_v, expand_v, reduce_f, spatial_f, expand_f, *staged, small_v, large_v, sems) = (
        refs[9:22],
        refs[22:],
    )
    used = [0]

    def copy(source, target):
        started = pltpu.make_async_copy(source, target, sems.at[used[0]])
        used[0] += 1
        started.start()
        return started

    loads = [copy(spatial_in, spatial_v), copy(expand_in, expand_v), copy(reduce_in, reduce_v)]
    arrivals = [copy(a, b) for a, b in zip(images, staged)]
    small_in, large_in = copy(small, small_v), copy(large, large_v)
    waits = []
    loads[0].wait()
    each = spatial_v.shape[1]
    for c in range(spatial_v.shape[0]):
        at = pl.ds(c * each, each)
        spatial_f[at] = spatial_v[c].astype(F32)
        if c % 2:
            pair = pl.ds((c - 1) * each, 2 * each)
            waits.append(copy(spatial_f.at[pair], outs[5].at[pair]))
    loads[1].wait()
    expand_f[...] = expand_v[...].astype(F32).reshape(expand_f.shape)
    waits.append(copy(expand_f, outs[6]))
    loads[2].wait()
    blocks, rows = reduce_v.shape[1:3]
    for k in range(2):
        for c in range(blocks):
            reduce_f[pl.ds((k * blocks + c) * rows, rows)] = reduce_v[k, c].astype(F32)
    waits.append(copy(reduce_f, outs[4]))
    for started, a, b in zip(arrivals, staged, outs[:4]):
        started.wait()
        waits.append(copy(a, b))
    small_in.wait()
    large_in.wait()
    for k, row in enumerate((0, 1, 8, 9)):
        waits.append(copy(small_v.at[row], outs[7 + k]))
    groups = large.shape[0] // 2
    for k in range(2):
        for g in range(groups):
            waits.append(copy(large_v.at[k * groups + g], outs[11 + k].at[pl.ds(128 * g, 128)]))
    for started in waits:
        started.wait()


def solution(mesh):
    wide = mesh.shape["wide"]
    image = P("wide", None, None, "narrow")
    vector = P("narrow")
    return jax.shard_map(
        functools.partial(per_device, wide),
        mesh=mesh,
        in_specs=(
            image, image, P("wide"), P(None, "narrow"), P(None, None, "narrow", None), P("narrow", None),
            vector, vector, vector, vector, vector, vector, image, image,
        ),
        out_specs=(
            image, image, image, image, P(None, "narrow"), P(None, None, "narrow", None),
            P("narrow", None), vector, vector, vector, vector, vector, vector,
        ),
        check_vma=False,
    )
```
